512 devices in a mesh: gx: 16 (over z), gy: 8 (over y, core), gz: 4 (over x).
Axes of the slice: x: 4, y: 4, z: 16, core: 2. Of those that a mesh axis runs over, the one named last changes fastest.
Arguments:
- frac_positions: float32 [16, 16, 8, 3, 128], P('gx', 'gy', 'gz'), may hold values from 0 to 1
- shielding: float32 [16, 16, 8, 128], P('gx', 'gy', 'gz'), may hold values from 0.5 to 0.9
- hardness: float32 [16, 16, 8, 128], P('gx', 'gy', 'gz'), may hold values from 14 to 20
- electroneg: float32 [16, 16, 8, 128], P('gx', 'gy', 'gz'), may hold values from 3 to 9
- counts: int32 [16, 16, 8], P('gx', 'gy', 'gz'), may hold values from 64 to 128, as said below
- neighbor_list: int32 [16, 16, 8, 13], P('gx', 'gy', 'gz'), may hold values from -1 to 12, as said below
Outputs:
- charges: float32 [16, 16, 8, 128], P('gx', 'gy', 'gz')
- residual: float32 [2, 16, 16, 8, 128], P(None, 'gx', 'gy', 'gz')
The draws below stay inside these ranges and needn't reach their ends.
Inputs may be any that keep to these rules, and one draw needn't show every extreme that they name: `counts`: some cell holds exactly 64 atoms and some cell exactly 128. `neighbor_list`: each cell's row lists 9 to 13 distinct codes of 0 to 12 first, and -1 in the remaining entries; some row lists all 13 codes and some row only 9.
All inputs are finite; a program needn't handle non-finite values.
Results may differ from the reference program's by a relative error of at most 0.0003.
Values sent between devices are 32-bit elements; how exact they have to be, the bound alone decides.
No kernel may reach another device: no remote copies, remote signals or barrier semaphores. Data moves between devices by JAX's collectives and lax.ppermute only.
A program may use at most 64 MiB of HBM per device.

```python
import math
import jax
import jax.numpy as jnp
from jax import lax

SLOTS = 128
ITERS = 4
NX = 16
NY = 16
NZ = 8


def draw_counts(key, part):
    key = jax.random.fold_in(key, 1)
    first, second = jax.random.split(key)
    cells = NX * NY * NZ
    values = jax.random.randint(first, (cells,), 64, SLOTS + 1).astype(jnp.int32)
    spot = jax.random.randint(second, (), 0, cells).astype(jnp.int32)
    values = values.at[spot].set(64)
    values = values.at[(spot + 1) % cells].set(SLOTS)
    return values.reshape((NX, NY, NZ)).astype(jnp.int32)


def draw_neighbor_list(key, part):
    key = jax.random.fold_in(key, 2)
    first, second, third = jax.random.split(key, 3)
    cells = NX * NY * NZ
    row_keys = jax.random.split(first, cells)
    codes = jnp.arange(13, dtype=jnp.int32)
    rows = jax.vmap(lambda one_key: jax.random.permutation(one_key, codes))(row_keys)
    lengths = jax.random.randint(second, (cells,), 9, 14).astype(jnp.int32)
    spot = jax.random.randint(third, (), 0, cells).astype(jnp.int32)
    lengths = lengths.at[spot].set(13)
    lengths = lengths.at[(spot + 1) % cells].set(9)
    rows = jnp.where(codes[None, :] < lengths[:, None], rows, -1)
    return rows.reshape((NX, NY, NZ, 13)).astype(jnp.int32)


def levels(own_key, dims, cuts, smallest, largest):
    factor_of, own = 1.0, jax.random.fold_in(own_key, 6)
    for position, blocks in cuts:
        draws = jnp.exp(jax.random.uniform(jax.random.fold_in(own, position), (blocks,), jnp.float32, smallest / len(cuts), largest / len(cuts)))
        factor_of = factor_of * jnp.repeat(draws, dims[position] // blocks).reshape([-1 if axis == position else 1 for axis in range(len(dims))])
    return factor_of


def setup_inputs(seed: int = 0) -> dict:
    key_list = jax.random.split(jax.random.key(seed), 7)
    return {
        "frac_positions": jnp.clip(1.0 * jax.random.uniform(key_list[0], (NX, NY, NZ, 3, SLOTS), jnp.float32) ** levels(key_list[0], (NX, NY, NZ, 3, SLOTS), ((0, 16), (1, 8), (2, 4)), -0.2, 0.2), 0.0, 1.0),
        "shielding": jnp.clip(jnp.exp(math.log(0.9) - 0.5877866 * jax.random.uniform(key_list[1], (NX, NY, NZ, SLOTS), jnp.float32) ** levels(key_list[1], (NX, NY, NZ, SLOTS), ((0, 16), (1, 8), (2, 4)), -0.2, 0.2)), 0.5, 0.9),
        "hardness": jnp.clip(14.0 + 6.0 * jax.random.uniform(key_list[2], (NX, NY, NZ, SLOTS), jnp.float32) ** levels(key_list[2], (NX, NY, NZ, SLOTS), ((0, 16), (1, 8), (2, 4)), -0.2, 0.2), 14.0, 20.0),
        "electroneg": jnp.clip(3.0 + 6.0 * jax.random.uniform(key_list[3], (NX, NY, NZ, SLOTS), jnp.float32) ** levels(key_list[3], (NX, NY, NZ, SLOTS), ((0, 16), (1, 8), (2, 4)), -0.2, 0.2), 3.0, 9.0),
        "counts": draw_counts(jax.random.fold_in(key_list[6], 71), 0),
        "neighbor_list": draw_neighbor_list(jax.random.fold_in(key_list[6], 71), 0),
    }


CUTOFF = 10.0
COULOMB = 14.4
HALF_SHELL = [(0, 0, 1), (0, 1, -1), (0, 1, 0), (0, 1, 1), (1, -1, -1), (1, -1, 0), (1, -1, 1), (1, 0, -1), (1, 0, 0), (1, 0, 1), (1, 1, -1), (1, 1, 0), (1, 1, 1)]

def pair_tile(place_i, shield_i, mask_i, place_j, shield_j, mask_j, offset):
    square = jnp.zeros(place_i.shape[:-2] + (place_i.shape[-1], place_j.shape[-1]), jnp.float32)
    for component in range(3):
        apart = (offset[component] + place_j[..., component, None, :] - place_i[..., component, :, None]) * CUTOFF
        square = square + apart * apart
    radius = jnp.sqrt(square)
    ratio = radius / CUTOFF
    fourth = ratio * ratio * ratio * ratio
    taper = 1.0 + fourth * (-35.0 + ratio * (84.0 + ratio * (-70.0 + 20.0 * ratio)))
    screen = (shield_i[..., :, None] * shield_j[..., None, :]) ** (-1.5)
    coulomb = COULOMB * taper / jnp.cbrt(square * radius + screen)
    return jnp.where(ratio < 1.0, coulomb, 0.0) * mask_i[..., :, None] * mask_j[..., None, :]

def offset_terms(offset, flag_col, places, shields, masks, field, mirror, drop_diagonal):
    shift = (-offset[0], -offset[1], -offset[2])
    vector = jnp.array(offset, jnp.float32)
    identity = jnp.eye(places.shape[-1], dtype=jnp.float32)

    def rolled(array):
        return jnp.roll(array, shift, axis=(0, 1, 2))

    def slab(items):
        place_i, shield_i, mask_i, place_j, shield_j, mask_j, chosen, field_i, field_j = items
        tile = pair_tile(place_i, shield_i, mask_i, place_j, shield_j, mask_j, vector) * chosen[..., None, None]
        if drop_diagonal:
            tile = tile * (1.0 - identity)
        to_own = jnp.einsum('bcij,bcrj->bcri', tile, field_j, precision=lax.Precision.HIGHEST)
        to_other = jnp.einsum('bcij,bcri->bcrj', tile, field_i, precision=lax.Precision.HIGHEST)
        return (to_own, to_other)
    own, other = lax.map(slab, (places, shields, masks, rolled(places), rolled(shields), rolled(masks), flag_col, field, rolled(field)))
    if mirror:
        return own + jnp.roll(other, offset, axis=(0, 1, 2))
    return own

def operate(field, places, shields, masks, hardness, flags):
    result = (hardness * masks)[:, :, :, None, :] * field
    result = result + offset_terms((0, 0, 0), jnp.ones(masks.shape[:3], jnp.float32), places, shields, masks, field, False, True)
    for number, offset in enumerate(HALF_SHELL):
        result = result + offset_terms(offset, flags[..., number], places, shields, masks, field, True, False)
    return result

def reference(frac_positions, shielding, hardness, electroneg, counts, neighbor_list):
    slots = jnp.arange(hardness.shape[-1], dtype=jnp.int32)
    masks = (slots < counts[..., None]).astype(jnp.float32)
    codes = jnp.arange(13, dtype=jnp.int32)
    flags = jnp.any(neighbor_list[..., :, None] == codes, axis=-2).astype(jnp.float32)
    right = jnp.stack([-electroneg * masks, -masks], axis=3)

    def inner(first, second):
        return lax.optimization_barrier(jnp.sum(first * second, axis=(0, 1, 2, 4)))
    solution = jnp.zeros_like(right)
    residual = right
    direction = right
    norm_now = inner(residual, residual)
    for step in range(ITERS):
        image = operate(direction, frac_positions, shielding, masks, hardness, flags)
        alpha = norm_now / inner(direction, image)
        solution = solution + alpha[:, None] * direction
        residual = residual - alpha[:, None] * image
        norm_next = inner(residual, residual)
        direction = residual + (norm_next / norm_now)[:, None] * direction
        norm_now = norm_next
    totals = lax.optimization_barrier(jnp.sum(solution, axis=(0, 1, 2, 4)))
    charges = solution[:, :, :, 0, :] - totals[0] / totals[1] * solution[:, :, :, 1, :]
    return (charges, jnp.moveaxis(residual, 3, 0))
```

```python
import functools

import jax
import jax.numpy as jnp
from jax import lax
from jax.experimental import pallas as pl
from jax.experimental.pallas import tpu as pltpu
from jax.sharding import PartitionSpec as P

CODES = {
    (0, 0, 1): 0,
    (0, 1, -1): 1,
    (0, 1, 0): 2,
    (0, 1, 1): 3,
    (1, -1, -1): 4,
    (1, -1, 0): 5,
    (1, -1, 1): 6,
    (1, 0, -1): 7,
    (1, 0, 0): 8,
    (1, 0, 1): 9,
    (1, 1, -1): 10,
    (1, 1, 0): 11,
    (1, 1, 1): 12,
}
SHELL = [(x, y, z) for x in (-1, 0, 1) for y in (-1, 0, 1) for z in (-1, 0, 1)]

SHIFT = (220.0, 110.0, 145.0, 140.0)
SCALE = (60.0, 70.0, 70.0, 70.0)
BACK = (0.0, 0.7, 1.0, 1.0)
PAIRS = [(i, j) for i in range(4) for j in range(i, 5)]
VMEM = pl.BlockSpec(memory_space=pltpu.VMEM)
PARAMS = pltpu.CompilerParams(vmem_limit_bytes=24 * 1024 * 1024)


def cell_index(x, y, z):
    return (x * 4 + y) * 4 + z


OWN = [cell_index(1, 1 + y, 1 + z) for y in range(2) for z in range(2)]


def spread(row):
    return jnp.broadcast_to(row, (8, 128))


def reduce_rows(total_ref, image_ref):
    for field in range(8):
        block = total_ref[field * 16 : (field + 1) * 16].reshape(128, 128)
        image_ref[field : field + 1, :] = jnp.sum(block.T, axis=0, keepdims=True)


def next_basis(step, image, field, before, mask, hard):
    value = image * mask + hard * field
    value = (value - SHIFT[step] * field) * (1.0 / SCALE[step])
    if BACK[step]:
        value = value - BACK[step] * before
    return value


def tile_kernel(packed_ref, hard_ref, tiles_ref, field_ref, next_ref, aux_ref, rows, cols, amp, total, image):
    lane_row = lax.broadcasted_iota(jnp.int32, (1, 128), 1)
    for x in range(3):
        for y in range(4):
            for z in range(4):
                cell = cell_index(x, y, z)
                block = packed_ref[cell]
                for number, shift in enumerate((x - 1.0, y - 1.0, z - 1.0)):
                    rows[cell, number] = spread(block[number : number + 1] + shift)
                for number in range(3, 6):
                    rows[cell, number] = spread(block[number : number + 1])
    for own, cell in enumerate(OWN):
        y, z = 1 + own // 2, 1 + own % 2
        for number in range(4):
            column = jnp.broadcast_to(rows[cell, number, 0:1, :], (128, 128)).T
            cols[own, number] = column.reshape(16, 8, 128)
        for number, offset in enumerate(SHELL):
            if offset in CODES:
                source, code = cell, CODES[offset]
            elif offset == (0, 0, 0):
                source = None
            else:
                source = cell_index(1 + offset[0], y + offset[1], z + offset[2])
                code = CODES[tuple(-value for value in offset)]
            if source is None:
                amp[own * 27 + number] = jnp.full((8, 128), 1.44, jnp.float32)
            else:
                flag = packed_ref[source, 6:7, code : code + 1]
                amp[own * 27 + number] = jnp.broadcast_to(1.44 * flag, (8, 128))

    sub = lax.broadcasted_iota(jnp.int32, (8, 128), 0)
    lane = lax.broadcasted_iota(jnp.int32, (8, 128), 1)

    def body(index, carry):
        own = index // 16
        chunk = index - own * 16
        base = (own // 2) * 4 + own % 2
        xi, yi, zi, si = [cols[own, number, chunk] for number in range(4)]
        sums = [jnp.zeros((8, 128), jnp.float32) for _ in range(2)]
        for number, offset in enumerate(SHELL):
            cell = base + cell_index(1 + offset[0], 1 + offset[1], 1 + offset[2])
            dx = rows[cell, 0] - xi
            dy = rows[cell, 1] - yi
            dz = rows[cell, 2] - zi
            square = jnp.maximum(dx * dx + dy * dy + dz * dz, 1e-30)
            ratio = square * lax.rsqrt(square)
            fourth = square * square
            taper = 1.0 + fourth * (-35.0 + ratio * (84.0 + ratio * (-70.0 + 20.0 * ratio)))
            cube = square * ratio + rows[cell, 3] * si
            value = taper * jnp.exp2(jnp.log(cube) * (-1.0 / (3.0 * 0.6931471805599453)))
            value = value * amp[own * 27 + number]
            keep = square < 1.0
            if offset == (0, 0, 0):
                keep = keep & (sub + chunk * 8 != lane)
            value = jnp.where(keep, value, 0.0)
            tiles_ref[(own * 27 + number) * 16 + chunk] = value
            for system in range(2):
                sums[system] = sums[system] + value * rows[cell, 4 + system]
        for system in range(2):
            total[(system * 4 + own) * 16 + chunk] = sums[system]
        return carry

    lax.fori_loop(0, 64, body, 0)
    reduce_rows(total, image)
    for own, cell in enumerate(OWN):
        for system in range(2):
            row = system * 4 + own
            field_ref[row : row + 1] = packed_ref[cell, 4 + system : 5 + system]
            aux_ref[row : row + 1] = -packed_ref[cell, 5:6]
            aux_ref[8 + row : 9 + row] = hard_ref[own : own + 1] * -packed_ref[cell, 5:6]
    field = field_ref[...]
    next_ref[...] = next_basis(0, image[...], field, None, aux_ref[0:8], aux_ref[8:16])


def run_tiles(packed, hard):
    shape = functools.partial(jax.ShapeDtypeStruct, dtype=jnp.float32)
    return pl.pallas_call(
        tile_kernel,
        out_shape=(shape((108 * 16, 8, 128)), shape((8, 128)), shape((8, 128)), shape((16, 128))),
        in_specs=[VMEM, VMEM],
        out_specs=(VMEM, VMEM, VMEM, VMEM),
        scratch_shapes=[
            pltpu.VMEM((48, 6, 8, 128), jnp.float32),
            pltpu.VMEM((4, 4, 16, 8, 128), jnp.float32),
            pltpu.VMEM((108, 8, 128), jnp.float32),
            pltpu.VMEM((128, 8, 128), jnp.float32),
            pltpu.VMEM((8, 128), jnp.float32),
        ],
        compiler_params=PARAMS,
        name="tiles",
    )(packed, hard)


def gram_row(fields):
    entries = [fields[i] * fields[j] for i, j in PAIRS] + fields[:4]
    lane = lax.broadcasted_iota(jnp.int32, (1, 128), 1)
    row = jnp.zeros((1, 128), jnp.float32)
    for number, entry in enumerate(entries):
        for system in range(2):
            part = jnp.sum(entry[system * 4 : system * 4 + 4], axis=0, keepdims=True)
            part = jnp.sum(part, axis=1, keepdims=True)
            row = row + jnp.where(lane == 2 * number + system, part, 0.0)
    return row


def apply_kernel(step, last, tiles_ref, halo_ref, aux_ref, *refs):
    count = step + 1
    fields = [ref for ref in refs[:count]]
    next_ref = refs[count]
    rest = refs[count + 1 :]
    if last:
        gram_ref, rest = rest[0], rest[1:]
    rows, total, image = rest
    for system in range(2):
        for cell in range(48):
            rows[cell * 2 + system] = spread(halo_ref[system * 48 + cell : system * 48 + cell + 1])

    def body(index, carry):
        own = index // 4
        group = index - own * 4
        base = (own // 2) * 4 + own % 2
        sums = [[jnp.zeros((8, 128), jnp.float32) for _ in range(4)] for _ in range(2)]
        for number, offset in enumerate(SHELL):
            cell = base + cell_index(1 + offset[0], 1 + offset[1], 1 + offset[2])
            right = [rows[cell * 2 + system] for system in range(2)]
            for part in range(4):
                tile = tiles_ref[(own * 27 + number) * 16 + group * 4 + part]
                for system in range(2):
                    sums[system][part] = sums[system][part] + tile * right[system]
        for system in range(2):
            for part in range(4):
                total[(system * 4 + own) * 16 + group * 4 + part] = sums[system][part]
        return carry

    lax.fori_loop(0, 16, body, 0)
    reduce_rows(total, image)
    values = [field[...] for field in fields]
    new = next_basis(step, image[...], values[-1], values[-2], aux_ref[0:8], aux_ref[8:16])
    next_ref[...] = new
    if last:
        gram_ref[...] = gram_row(values + [new])


def run_apply(step, last, tiles, halo, aux, fields):
    shape = functools.partial(jax.ShapeDtypeStruct, dtype=jnp.float32)
    outs = (shape((8, 128)), shape((1, 128))) if last else (shape((8, 128)),)
    return pl.pallas_call(
        functools.partial(apply_kernel, step, last),
        out_shape=outs,
        in_specs=[VMEM] * (3 + len(fields)),
        out_specs=tuple(VMEM for _ in outs),
        scratch_shapes=[
            pltpu.VMEM((96, 8, 128), jnp.float32),
            pltpu.VMEM((128, 8, 128), jnp.float32),
            pltpu.VMEM((8, 128), jnp.float32),
        ],
        compiler_params=PARAMS,
        name=f"apply{step}",
    )(tiles, halo, aux, *fields)


def combine(coefs, fields):
    value = coefs[0] * fields[0]
    for coef, field in zip(coefs[1:], fields[1:]):
        value = value + coef * field
    return value


def finish_kernel(gram_ref, w0, w1, w2, w3, w4, charges_ref, residual_ref):
    fields = [ref[...] for ref in (w0, w1, w2, w3, w4)]
    summed = spread(jnp.sum(gram_ref[...], axis=0, keepdims=True))
    lane = lax.broadcasted_iota(jnp.int32, (8, 128), 1)
    system = lax.broadcasted_iota(jnp.int32, (8, 128), 0) // 4

    def entry(number):
        picked = jnp.where(lane == 2 * number + system, summed, 0.0)
        return jnp.broadcast_to(jnp.sum(picked, axis=1, keepdims=True), (8, 128))

    gram = {}
    for number, (i, j) in enumerate(PAIRS):
        gram[i, j] = gram[j, i] = entry(number)
    totals = [entry(len(PAIRS) + number) for number in range(4)]

    def dot(left, right):
        result = None
        for i, a in enumerate(left):
            part = None
            for j, b in enumerate(right):
                term = gram[i, j] * b
                part = term if part is None else part + term
            result = a * part if result is None else result + a * part
        return result

    def multiply(vector):
        size = len(vector)
        out = []
        for row in range(size + 1):
            value = None
            if row >= 1:
                value = SCALE[row - 1] * vector[row - 1]
            if row < size:
                term = SHIFT[row] * vector[row]
                value = term if value is None else value + term
            if row + 1 < size:
                value = value + SCALE[row + 1] * BACK[row + 1] * vector[row + 1]
            out.append(value)
        return out

    one = jnp.ones((8, 128), jnp.float32)
    residual = [one]
    direction = [one]
    answer = []
    norm_now = gram[0, 0]
    for step in range(4):
        image = multiply(direction)
        alpha = norm_now / dot(direction, image)
        answer = [
            alpha * d if k >= len(answer) else answer[k] + alpha * d for k, d in enumerate(direction)
        ]
        residual = [
            residual[k] - alpha * value if k < len(residual) else -alpha * value
            for k, value in enumerate(image)
        ]
        if step == 3:
            break
        norm_next = dot(residual, residual)
        ratio = norm_next / norm_now
        direction = [
            value + ratio * direction[k] if k < len(direction) else value
            for k, value in enumerate(residual)
        ]
        norm_now = norm_next
    residual_ref[...] = combine(residual, fields)
    solution = combine(answer, fields[:4])
    total = combine(answer, totals)
    charges_ref[...] = solution[0:4] - total[0:4] / total[4:8] * solution[4:8]


def run_finish(gathered, fields):
    shape = functools.partial(jax.ShapeDtypeStruct, dtype=jnp.float32)
    return pl.pallas_call(
        finish_kernel,
        out_shape=(shape((4, 128)), shape((8, 128))),
        in_specs=[VMEM] * 6,
        out_specs=(VMEM, VMEM),
        compiler_params=PARAMS,
        name="finish",
    )(gathered, *fields)


X = ("xa", "xb")


def swap(value):
    return lax.ppermute(value, "core", [(0, 1), (1, 0)])


def opposite(value, axes, count):
    pairs = []
    for place in range(count):
        pairs.append((place * 2, (place + 1) % count * 2))
        pairs.append((place * 2 + 1, (place - 1) % count * 2 + 1))
    return lax.ppermute(value, axes, pairs)


def opposite_last(value, axis, count):
    pairs = []
    for place in range(count):
        pairs.append((place, (place + 1) % count))
        pairs.append((count + place, count + (place - 1) % count))
    return lax.ppermute(value, ("core", axis), pairs)


def edge_swap(value, count):
    pairs = []
    for place in range(count):
        pairs.append((place * 2 + 1, (place + 1) % count * 2))
        pairs.append(((place + 1) % count * 2, place * 2 + 1))
    return lax.ppermute(value, ("yc", "core"), pairs)


def ordered(core, mine, other, axis):
    first = jnp.where(core == 0, mine, other)
    second = jnp.where(core == 0, other, mine)
    return first, second


def exchange(value, dim, core, sizes, form):
    count_x, count_y, count_z = sizes
    lead = (slice(None),) * dim
    sent = jnp.where(core == 0, value[lead + (slice(None), slice(0, 1))], value[lead + (slice(None), slice(1, 2))])
    edge = edge_swap(sent, count_y)
    low = jnp.concatenate([edge, value], axis=dim + 1)
    high = jnp.concatenate([value, edge], axis=dim + 1)
    three = jnp.where(core == 0, low, high)
    other = swap(three)
    first, second = ordered(core, three, other, dim + 1)
    six = jnp.concatenate([first, second], axis=dim + 1)
    arrived = opposite(six, X + ("core",), count_x)
    other = swap(arrived)
    first, second = ordered(core, arrived, other, dim)
    layers = jnp.concatenate([first, six, second], axis=dim)
    if form == "pair":
        sent = jnp.where(
            core == 0,
            layers[lead + (slice(None), slice(None), slice(1, 2))],
            layers[lead + (slice(None), slice(None), slice(0, 1))],
        )
        arrived = opposite_last(sent, "gz", count_z)
        other = swap(arrived)
        first, second = ordered(core, arrived, other, dim)
        block = jnp.concatenate([first, layers, second], axis=dim + 2)
        return jnp.where(
            core == 0,
            block[lead + (slice(None), slice(0, 4))],
            block[lead + (slice(None), slice(2, 6))],
        )
    own = jnp.where(
        core == 0,
        layers[lead + (slice(None), slice(0, 4))],
        layers[lead + (slice(None), slice(2, 6))],
    )
    every = spread_all(own, "gz", count_z)
    here = lax.axis_index("gz")
    below = lax.dynamic_index_in_dim(every, lax.rem(here + count_z - 1, count_z), 0, keepdims=False)
    above = lax.dynamic_index_in_dim(every, lax.rem(here + 1, count_z), 0, keepdims=False)
    return jnp.concatenate(
        [
            below[lead + (slice(None), slice(None), slice(1, 2))],
            own,
            above[lead + (slice(None), slice(None), slice(0, 1))],
        ],
        axis=dim + 2,
    )


def spread_all(value, axes, count):
    sent = jnp.broadcast_to(value[None], (count,) + value.shape)
    return lax.all_to_all(sent, axes, 0, 0)


def shards(frac_positions, shielding, hardness, electroneg, counts, neighbor_list):
    wide, narrow = lax.axis_size("xa"), lax.axis_size("xb")
    count_y, count_z = lax.axis_size("yc"), lax.axis_size("gz")
    sizes = (wide * narrow, count_y, count_z)
    core = lax.axis_index("core")
    masks = (lax.broadcasted_iota(jnp.int32, hardness.shape, 3) < counts[..., None]).astype(
        jnp.float32
    )
    codes = jnp.arange(13, dtype=jnp.int32)
    flags = jnp.any(neighbor_list[..., :, None] == codes, axis=-2).astype(jnp.float32)
    flag_row = jnp.pad(flags, ((0, 0), (0, 0), (0, 0), (0, 115)))
    screen = (shielding**-1.5) * (1000.0**-0.5)
    packed = jnp.concatenate(
        [
            frac_positions,
            screen[:, :, :, None],
            (-electroneg * masks)[:, :, :, None],
            -masks[:, :, :, None],
            flag_row[:, :, :, None],
            jnp.zeros_like(flag_row)[:, :, :, None],
        ],
        axis=3,
    )
    packed = exchange(packed, 0, core, sizes, "pair").reshape(48, 8, 128)
    tiles, w0, w1, aux = run_tiles(packed, hardness.reshape(4, 128))
    fields = [w0, w1]
    for step, form in ((1, "pair"), (2, "all"), (3, "all")):
        halo = exchange(fields[-1].reshape(2, 1, 2, 2, 128), 1, core, sizes, form)
        outs = run_apply(step, step == 3, tiles, halo.reshape(96, 128), aux, fields)
        fields.append(outs[0])
    gram = outs[1]
    gram = jnp.sum(spread_all(gram, ("yc", "core"), 2 * count_y), axis=0)
    gram = jnp.sum(spread_all(gram, "gz", count_z), axis=0)
    gram = jnp.sum(spread_all(gram, "xb", narrow), axis=0)
    gram = spread_all(gram, "xa", wide)
    charges, residual = run_finish(gram.reshape(wide, 128), fields)
    return charges.reshape(1, 2, 2, 128), residual.reshape(2, 1, 2, 2, 128)


def solution(mesh):
    count_x, count_y, count_z = mesh.devices.shape
    wide = 4 if count_x % 4 == 0 else 1
    mesh = jax.sharding.Mesh(
        mesh.devices.reshape(wide, count_x // wide, count_y // 2, 2, count_z),
        ("xa", "xb", "yc", "core", "gz"),
    )
    x, y = ("xa", "xb"), ("yc", "core")
    placed = (
        P(x, y, "gz", None, None),
        P(x, y, "gz", None),
        P(x, y, "gz", None),
        P(x, y, "gz", None),
        P(x, y, "gz"),
        P(x, y, "gz", None),
    )
    return jax.shard_map(
        shards,
        mesh=mesh,
        in_specs=placed,
        out_specs=(P(x, y, "gz", None), P(None, x, y, "gz", None)),
        check_vma=False,
    )
```

```python
import functools

import jax
import jax.numpy as jnp
from jax import lax
from jax.experimental import pallas as pl
from jax.experimental.pallas import tpu as pltpu
from jax.sharding import PartitionSpec as P

CODES = {
    (0, 0, 1): 0,
    (0, 1, -1): 1,
    (0, 1, 0): 2,
    (0, 1, 1): 3,
    (1, -1, -1): 4,
    (1, -1, 0): 5,
    (1, -1, 1): 6,
    (1, 0, -1): 7,
    (1, 0, 0): 8,
    (1, 0, 1): 9,
    (1, 1, -1): 10,
    (1, 1, 0): 11,
    (1, 1, 1): 12,
}
SHELL = [(x, y, z) for x in (-1, 0, 1) for y in (-1, 0, 1) for z in (-1, 0, 1)]

SHIFT = (220.0, 110.0, 145.0, 140.0)
SCALE = (60.0, 70.0, 70.0, 70.0)
BACK = (0.0, 0.7, 1.0, 1.0)
PAIRS = [(i, j) for i in range(4) for j in range(i, 5)]
VMEM = pl.BlockSpec(memory_space=pltpu.VMEM)
PARAMS = pltpu.CompilerParams(vmem_limit_bytes=24 * 1024 * 1024)


OWN = [(1 + y) * 4 + 1 + z for y in range(2) for z in range(2)]
SAME = [offset for offset in SHELL if offset[0] == 0]
SIDE = [offset for offset in SHELL if offset[0] != 0]


def spread(row):
    return jnp.broadcast_to(row, (8, 128))


def reduce_rows(total_ref, image_ref):
    for field in range(8):
        block = total_ref[field * 16 : (field + 1) * 16].reshape(128, 128)
        image_ref[field : field + 1, :] = jnp.sum(block.T, axis=0, keepdims=True)


def next_basis(step, image, field, before, mask, hard):
    value = image * mask + hard * field
    value = (value - SHIFT[step] * field) * (1.0 / SCALE[step])
    if BACK[step]:
        value = value - BACK[step] * before
    return value


def pack_kernel(*refs):
    sources, packed_ref, inputs, semaphores = refs[:6], refs[6], refs[7:13], refs[13]
    copies = [
        pltpu.make_async_copy(source, target, semaphores.at[number])
        for number, (source, target) in enumerate(zip(sources, inputs))
    ]
    for copy in copies:
        copy.start()
    for copy in copies:
        copy.wait()
    place_ref, shield_ref, hard_ref, electro_ref, count_ref, list_ref = inputs
    lane = lax.broadcasted_iota(jnp.int32, (1, 128), 1)
    for y in range(2):
        for z in range(2):
            cell = 2 * y + z
            count = jnp.broadcast_to(count_ref[0, y : y + 1, z : z + 1], (1, 128))
            mask = jnp.where(lane < count, 1.0, 0.0)
            flags = jnp.zeros((1, 128), jnp.float32)
            for number in range(13):
                code = jnp.broadcast_to(list_ref[0, y, z : z + 1, number : number + 1], (1, 128))
                flags = jnp.where(lane == code, 1.0, flags)
            for number in range(3):
                packed_ref[cell, number : number + 1] = place_ref[0, y, number, z : z + 1]
            shield = shield_ref[0, y, z : z + 1]
            packed_ref[cell, 3:4] = jnp.exp(-1.5 * jnp.log(shield)) * (1000.0**-0.5)
            packed_ref[cell, 4:5] = -electro_ref[0, y, z : z + 1] * mask
            packed_ref[cell, 5:6] = -mask
            packed_ref[cell, 6:7] = flags
            packed_ref[cell, 7:8] = hard_ref[0, y, z : z + 1]


def run_pack(*inputs):
    return pl.pallas_call(
        pack_kernel,
        out_shape=jax.ShapeDtypeStruct((4, 8, 128), jnp.float32),
        in_specs=[pl.BlockSpec(memory_space=pltpu.HBM)] * 6,
        out_specs=VMEM,
        scratch_shapes=[pltpu.VMEM(value.shape, value.dtype) for value in inputs]
        + [pltpu.SemaphoreType.DMA((6,))],
        compiler_params=pltpu.CompilerParams(vmem_limit_bytes=63 * 1024 * 1024),
        name="pack",
    )(*inputs)


def fill_rows(packed_ref, rows, first, layer):
    for y in range(4):
        for z in range(4):
            cell = y * 4 + z
            block = packed_ref[cell]
            for number, shift in enumerate((float(layer), y - 1.0, z - 1.0)):
                rows[first + cell, number] = spread(block[number : number + 1] + shift)
            for number in range(3, 6):
                rows[first + cell, number] = spread(block[number : number + 1])


def neighbor(offset):
    layer = 1 if offset[0] == 1 else 0
    return layer * 16 + (1 + offset[1]) * 4 + 1 + offset[2]


def fill_away(offsets, own_ref, lower_ref, rows, away):
    for own, cell in enumerate(OWN):
        y, z = own // 2, own % 2
        for number, offset in enumerate(offsets):
            row = rows[neighbor(offset) + y * 4 + z, 0]
            if offset in CODES:
                flag = own_ref[cell, 6:7, CODES[offset] : CODES[offset] + 1]
            elif offset == (0, 0, 0):
                flag = None
            else:
                code = CODES[tuple(-value for value in offset)]
                flag = lower_ref[cell + offset[1] * 4 + offset[2], 6:7, code : code + 1]
            if flag is not None:
                row = row + jnp.broadcast_to((1.0 - flag) * 100.0, (8, 128))
            away[own * len(offsets) + number] = row


def build_tiles(offsets, rows, cols, away, tiles_ref, before, total):
    sub = lax.broadcasted_iota(jnp.int32, (8, 128), 0)
    lane = lax.broadcasted_iota(jnp.int32, (8, 128), 1)
    size = len(offsets)

    def body(index, carry):
        own = index // 16
        chunk = index - own * 16
        base = (own // 2) * 4 + own % 2
        xi, yi, zi, si = [cols[(own * 4 + number) * 16 + chunk] for number in range(4)]
        if before is None:
            sums = [jnp.zeros((8, 128), jnp.float32) for _ in range(2)]
        else:
            sums = [before[(system * 4 + own) * 16 + chunk] for system in range(2)]
        for number, offset in enumerate(offsets):
            cell = base + neighbor(offset)
            dx = away[own * size + number] - xi
            dy = rows[cell, 1] - yi
            dz = rows[cell, 2] - zi
            square = jnp.maximum(dx * dx + dy * dy + dz * dz, 1e-30)
            ratio = square * lax.rsqrt(square)
            fourth = square * square
            taper = 1.44 + fourth * (-50.4 + ratio * (120.96 + ratio * (-100.8 + 28.8 * ratio)))
            cube = square * ratio + rows[cell, 3] * si
            value = taper * jnp.exp2(jnp.log(cube) * (-1.0 / (3.0 * 0.6931471805599453)))
            keep = square < 1.0
            if offset == (0, 0, 0):
                keep = keep & (sub + chunk * 8 != lane)
            value = jnp.where(keep, value, 0.0)
            tiles_ref[(own * size + number) * 16 + chunk] = value
            for system in range(2):
                sums[system] = sums[system] + value * rows[cell, 4 + system]
        for system in range(2):
            total[(system * 4 + own) * 16 + chunk] = sums[system]
        return carry

    lax.fori_loop(0, 64, body, 0)


def same_kernel(own_ref, tiles_ref, cols_ref, total_ref, field_ref, aux_ref, rows, away):
    fill_rows(own_ref, rows, 0, 0)
    for own, cell in enumerate(OWN):
        for number in range(4):
            column = jnp.broadcast_to(rows[cell, number, 0:1, :], (128, 128)).T
            start = (own * 4 + number) * 16
            cols_ref[start : start + 16] = column.reshape(16, 8, 128)
        for system in range(2):
            row = system * 4 + own
            mask = -own_ref[cell, 5:6]
            field_ref[row : row + 1] = own_ref[cell, 4 + system : 5 + system]
            aux_ref[row : row + 1] = mask
            aux_ref[8 + row : 9 + row] = own_ref[cell, 7:8] * mask
    fill_away(SAME, own_ref, own_ref, rows, away)
    build_tiles(SAME, rows, cols_ref, away, tiles_ref, None, total_ref)


def side_kernel(own_ref, lower_ref, upper_ref, cols_ref, before_ref, field_ref, aux_ref, tiles_ref, next_ref, rows, away, total, image):
    fill_rows(lower_ref, rows, 0, -1)
    fill_rows(upper_ref, rows, 16, 1)
    fill_away(SIDE, own_ref, lower_ref, rows, away)
    build_tiles(SIDE, rows, cols_ref, away, tiles_ref, before_ref, total)
    reduce_rows(total, image)
    next_ref[...] = next_basis(0, image[...], field_ref[...], None, aux_ref[0:8], aux_ref[8:16])


SHAPE = functools.partial(jax.ShapeDtypeStruct, dtype=jnp.float32)


def cost(flops):
    return pl.CostEstimate(flops=flops, bytes_accessed=4 * 1024 * 1024, transcendentals=0)


def run_same(own):
    return pl.pallas_call(
        same_kernel,
        out_shape=(
            SHAPE((36 * 16, 8, 128)),
            SHAPE((256, 8, 128)),
            SHAPE((128, 8, 128)),
            SHAPE((8, 128)),
            SHAPE((16, 128)),
        ),
        in_specs=[VMEM],
        out_specs=(VMEM,) * 5,
        scratch_shapes=[
            pltpu.VMEM((16, 6, 8, 128), jnp.float32),
            pltpu.VMEM((36, 8, 128), jnp.float32),
        ],
        compiler_params=PARAMS,
        cost_estimate=cost(40 * 36 * 16384),
        name="tiles_same",
    )(own)


def run_side(*inputs):
    return pl.pallas_call(
        side_kernel,
        out_shape=(SHAPE((72 * 16, 8, 128)), SHAPE((8, 128))),
        in_specs=[VMEM] * 7,
        out_specs=(VMEM,) * 2,
        scratch_shapes=[
            pltpu.VMEM((32, 6, 8, 128), jnp.float32),
            pltpu.VMEM((72, 8, 128), jnp.float32),
            pltpu.VMEM((128, 8, 128), jnp.float32),
            pltpu.VMEM((8, 128), jnp.float32),
        ],
        compiler_params=PARAMS,
        cost_estimate=cost(40 * 72 * 16384),
        name="tiles_side",
    )(*inputs)


def gram_row(fields):
    entries = [fields[i] * fields[j] for i, j in PAIRS] + fields[:4]
    lane = lax.broadcasted_iota(jnp.int32, (1, 128), 1)
    row = jnp.zeros((1, 128), jnp.float32)
    for number, entry in enumerate(entries):
        for system in range(2):
            part = jnp.sum(entry[system * 4 : system * 4 + 4], axis=0, keepdims=True)
            part = jnp.sum(part, axis=1, keepdims=True)
            row = row + jnp.where(lane == 2 * number + system, part, 0.0)
    return row


def fill_fields(halo_ref, rows, first):
    for system in range(2):
        for cell in range(16):
            row = system * 16 + cell
            rows[(first + cell) * 2 + system] = spread(halo_ref[row : row + 1])


def apply_tiles(offsets, tiles_ref, rows, before, total):
    size = len(offsets)

    def body(index, carry):
        own = index // 4
        group = index - own * 4
        base = (own // 2) * 4 + own % 2
        places = [[(system * 4 + own) * 16 + group * 4 + part for part in range(4)] for system in range(2)]
        if before is None:
            sums = [[jnp.zeros((8, 128), jnp.float32) for _ in range(4)] for _ in range(2)]
        else:
            sums = [[before[place] for place in line] for line in places]
        for number, offset in enumerate(offsets):
            cell = base + neighbor(offset)
            right = [rows[cell * 2 + system] for system in range(2)]
            for part in range(4):
                tile = tiles_ref[(own * size + number) * 16 + group * 4 + part]
                for system in range(2):
                    sums[system][part] = sums[system][part] + tile * right[system]
        for system in range(2):
            for part in range(4):
                total[places[system][part]] = sums[system][part]
        return carry

    lax.fori_loop(0, 16, body, 0)


def apply_same_kernel(tiles_ref, halo_ref, total_ref, rows):
    fill_fields(halo_ref, rows, 0)
    apply_tiles(SAME, tiles_ref, rows, None, total_ref)


def apply_side_kernel(step, last, tiles_ref, lower_ref, upper_ref, before_ref, aux_ref, *refs):
    count = step + 1
    fields, next_ref, rest = refs[:count], refs[count], refs[count + 1 :]
    if last:
        gram_ref, rest = rest[0], rest[1:]
    rows, total, image = rest
    fill_fields(lower_ref, rows, 0)
    fill_fields(upper_ref, rows, 16)
    apply_tiles(SIDE, tiles_ref, rows, before_ref, total)
    reduce_rows(total, image)
    values = [field[...] for field in fields]
    new = next_basis(step, image[...], values[-1], values[-2], aux_ref[0:8], aux_ref[8:16])
    next_ref[...] = new
    if last:
        gram_ref[...] = gram_row(values + [new])


def run_apply_same(tiles, halo):
    return pl.pallas_call(
        apply_same_kernel,
        out_shape=SHAPE((128, 8, 128)),
        in_specs=[VMEM] * 2,
        out_specs=VMEM,
        scratch_shapes=[pltpu.VMEM((32, 8, 128), jnp.float32)],
        compiler_params=PARAMS,
        cost_estimate=cost(4 * 36 * 16384),
        name="apply_same",
    )(tiles, halo)


def run_apply_side(step, last, tiles, lower, upper, before, aux, fields):
    outs = (SHAPE((8, 128)), SHAPE((1, 128))) if last else (SHAPE((8, 128)),)
    return pl.pallas_call(
        functools.partial(apply_side_kernel, step, last),
        out_shape=outs,
        in_specs=[VMEM] * (5 + len(fields)),
        out_specs=tuple(VMEM for _ in outs),
        scratch_shapes=[
            pltpu.VMEM((64, 8, 128), jnp.float32),
            pltpu.VMEM((128, 8, 128), jnp.float32),
            pltpu.VMEM((8, 128), jnp.float32),
        ],
        compiler_params=PARAMS,
        cost_estimate=cost(4 * 72 * 16384),
        name=f"apply_side{step}",
    )(tiles, lower, upper, before, aux, *fields)


def combine(coefs, fields):
    value = coefs[0] * fields[0]
    for coef, field in zip(coefs[1:], fields[1:]):
        value = value + coef * field
    return value


def finish_kernel(gram_ref, w0, w1, w2, w3, w4, charges_ref, residual_ref):
    fields = [ref[...] for ref in (w0, w1, w2, w3, w4)]
    summed = spread(jnp.sum(gram_ref[...], axis=0, keepdims=True))
    lane = lax.broadcasted_iota(jnp.int32, (8, 128), 1)
    system = lax.broadcasted_iota(jnp.int32, (8, 128), 0) // 4

    def entry(number):
        picked = jnp.where(lane == 2 * number + system, summed, 0.0)
        return jnp.broadcast_to(jnp.sum(picked, axis=1, keepdims=True), (8, 128))

    gram = {}
    for number, (i, j) in enumerate(PAIRS):
        gram[i, j] = gram[j, i] = entry(number)
    totals = [entry(len(PAIRS) + number) for number in range(4)]

    def dot(left, right):
        result = None
        for i, a in enumerate(left):
            part = None
            for j, b in enumerate(right):
                term = gram[i, j] * b
                part = term if part is None else part + term
            result = a * part if result is None else result + a * part
        return result

    def multiply(vector):
        size = len(vector)
        out = []
        for row in range(size + 1):
            value = None
            if row >= 1:
                value = SCALE[row - 1] * vector[row - 1]
            if row < size:
                term = SHIFT[row] * vector[row]
                value = term if value is None else value + term
            if row + 1 < size:
                value = value + SCALE[row + 1] * BACK[row + 1] * vector[row + 1]
            out.append(value)
        return out

    one = jnp.ones((8, 128), jnp.float32)
    residual = [one]
    direction = [one]
    answer = []
    norm_now = gram[0, 0]
    for step in range(4):
        image = multiply(direction)
        alpha = norm_now / dot(direction, image)
        answer = [
            alpha * d if k >= len(answer) else answer[k] + alpha * d for k, d in enumerate(direction)
        ]
        residual = [
            residual[k] - alpha * value if k < len(residual) else -alpha * value
            for k, value in enumerate(image)
        ]
        if step == 3:
            break
        norm_next = dot(residual, residual)
        ratio = norm_next / norm_now
        direction = [
            value + ratio * direction[k] if k < len(direction) else value
            for k, value in enumerate(residual)
        ]
        norm_now = norm_next
    value = combine(residual, fields)
    solution = combine(answer, fields[:4])
    total = combine(answer, totals)
    charges = solution[0:4] - total[0:4] / total[4:8] * solution[4:8]
    for y in range(2):
        charges_ref[0, y] = charges[2 * y : 2 * y + 2]
        for system in range(2):
            row = system * 4 + 2 * y
            residual_ref[system, 0, y] = value[row : row + 2]


def run_finish(gathered, fields):
    shape = functools.partial(jax.ShapeDtypeStruct, dtype=jnp.float32)
    return pl.pallas_call(
        finish_kernel,
        out_shape=(shape((1, 2, 2, 128)), shape((2, 1, 2, 2, 128))),
        in_specs=[VMEM] * 6,
        out_specs=(VMEM, VMEM),
        compiler_params=PARAMS,
        name="finish",
    )(gathered, *fields)


def shifted(value, axis, steps):
    count = lax.axis_size(axis)
    pairs = [(source, (source + steps) % count) for source in range(count)]
    return lax.ppermute(value, axis, pairs)


def spread_all(value, axes, count):
    sent = jnp.broadcast_to(value[None], (count,) + value.shape)
    return lax.all_to_all(sent, axes, 0, 0)


def around(every, axis, group, cells):
    count = lax.axis_size(axis)
    here = lax.axis_index(axis)

    def part(place):
        return lax.dynamic_index_in_dim(every, place, group, keepdims=False)

    cells = cells - 1
    below = lax.slice_in_dim(part(lax.rem(here + count - 1, count)), 1, 2, axis=cells)
    above = lax.slice_in_dim(part(lax.rem(here + 1, count)), 0, 1, axis=cells)
    return jnp.concatenate([below, part(here), above], axis=cells)


def exchange(value, dim):
    count_y, count_z = lax.axis_size("gy"), lax.axis_size("gz")
    every = spread_all(value, ("gy", "gz"), count_y * count_z)
    every = every.reshape((count_y, count_z) + value.shape)
    block = around(every, "gy", 0, 2 + dim)
    block = around(block, "gz", 0, 2 + dim)
    return block, shifted(block, "gx", 1), shifted(block, "gx", -1)


def shards(frac_positions, shielding, hardness, electroneg, counts, neighbor_list):
    count_x, count_y, count_z = [lax.axis_size(axis) for axis in ("gx", "gy", "gz")]
    places = frac_positions.transpose(0, 1, 3, 2, 4)
    packed = run_pack(places, shielding, hardness, electroneg, counts, neighbor_list)
    layers = exchange(packed.reshape(2, 2, 8, 128), 0)
    own, lower, upper = [layer.reshape(16, 8, 128) for layer in layers]
    tiles_same, cols, total, w0, aux = run_same(own)
    tiles_side, w1 = run_side(own, lower, upper, cols, total, w0, aux)
    fields = [w0, w1]
    for step in (1, 2, 3):
        layers = exchange(fields[-1].reshape(2, 2, 2, 128), 1)
        own, lower, upper = [layer.reshape(32, 128) for layer in layers]
        total = run_apply_same(tiles_same, own)
        outs = run_apply_side(step, step == 3, tiles_side, lower, upper, total, aux, fields)
        fields.append(outs[0])
    gram = outs[1]
    gram = jnp.sum(spread_all(gram, ("gy", "gz"), count_y * count_z), axis=0)
    gram = spread_all(gram, "gx", count_x)
    return run_finish(gram.reshape(count_x, 128), fields)


def solution(mesh):
    placed = (
        P("gx", "gy", "gz", None, None),
        P("gx", "gy", "gz", None),
        P("gx", "gy", "gz", None),
        P("gx", "gy", "gz", None),
        P("gx", "gy", "gz"),
        P("gx", "gy", "gz", None),
    )
    return jax.shard_map(
        shards,
        mesh=mesh,
        in_specs=placed,
        out_specs=(P("gx", "gy", "gz", None), P(None, "gx", "gy", "gz", None)),
        check_vma=False,
    )
```

```python
import functools

import jax
import jax.numpy as jnp
from jax import lax
from jax.experimental import pallas as pl
from jax.experimental.pallas import tpu as pltpu
from jax.sharding import PartitionSpec as P

CODES = {
    (0, 0, 1): 0,
    (0, 1, -1): 1,
    (0, 1, 0): 2,
    (0, 1, 1): 3,
    (1, -1, -1): 4,
    (1, -1, 0): 5,
    (1, -1, 1): 6,
    (1, 0, -1): 7,
    (1, 0, 0): 8,
    (1, 0, 1): 9,
    (1, 1, -1): 10,
    (1, 1, 0): 11,
    (1, 1, 1): 12,
}
SHELL = [(x, y, z) for x in (-1, 0, 1) for y in (-1, 0, 1) for z in (-1, 0, 1)]

SHIFT = (220.0, 110.0, 145.0, 140.0)
SCALE = (60.0, 70.0, 70.0, 70.0)
BACK = (0.0, 0.7, 1.0, 1.0)
PAIRS = [(i, j) for i in range(4) for j in range(i, 5)]
VMEM = pl.BlockSpec(memory_space=pltpu.VMEM)
SMEM = pl.BlockSpec(memory_space=pltpu.SMEM)
PARAMS = pltpu.CompilerParams(vmem_limit_bytes=24 * 1024 * 1024)


CHIP = [(1 + y) * 4 + 1 + z for y in range(4) for z in range(2)]
PLANE = [(y, z) for y in (-1, 0, 1) for z in (-1, 0, 1)]


def spread(row):
    return jnp.broadcast_to(row, (8, 128))


def reduce_rows(total_ref, image_ref):
    for field in range(image_ref.shape[0]):
        block = total_ref[field * 16 : (field + 1) * 16].reshape(128, 128)
        image_ref[field : field + 1, :] = jnp.sum(block.T, axis=0, keepdims=True)


def next_basis(step, image, field, before, mask, hard):
    value = image * mask + hard * field
    value = (value - SHIFT[step] * field) * (1.0 / SCALE[step])
    if BACK[step]:
        value = value - BACK[step] * before
    return value


def pack_kernel(*refs):
    sources, packed_ref, inputs, semaphores = refs[:6], refs[6], refs[7:13], refs[13]
    copies = [
        pltpu.make_async_copy(source, target, semaphores.at[number])
        for number, (source, target) in enumerate(zip(sources, inputs))
    ]
    for copy in copies:
        copy.start()
    for copy in copies:
        copy.wait()
    place_ref, shield_ref, hard_ref, electro_ref, count_ref, list_ref = inputs
    lane = lax.broadcasted_iota(jnp.int32, (1, 128), 1)
    for y in range(2):
        for z in range(2):
            cell = 2 * y + z
            count = jnp.broadcast_to(count_ref[0, y : y + 1, z : z + 1], (1, 128))
            mask = jnp.where(lane < count, 1.0, 0.0)
            flags = jnp.zeros((1, 128), jnp.float32)
            for number in range(13):
                code = jnp.broadcast_to(list_ref[0, y, z : z + 1, number : number + 1], (1, 128))
                flags = jnp.where(lane == code, 1.0, flags)
            rows = []
            for number in range(3):
                rows.append(place_ref[0, y, number, z : z + 1])
            shield = shield_ref[0, y, z : z + 1]
            rows.append(jnp.exp(-1.5 * jnp.log(shield)) * (1000.0**-0.5))
            rows.append(-electro_ref[0, y, z : z + 1] * mask)
            rows.append(-mask)
            rows.append(flags)
            rows.append(hard_ref[0, y, z : z + 1])
            block = jnp.concatenate(rows, axis=0)
            for copy in range(packed_ref.shape[0]):
                packed_ref[copy, cell] = block


def run_pack(count, *inputs):
    return pl.pallas_call(
        pack_kernel,
        out_shape=jax.ShapeDtypeStruct((count, 4, 8, 128), jnp.float32),
        in_specs=[pl.BlockSpec(memory_space=pltpu.HBM)] * 6,
        out_specs=VMEM,
        scratch_shapes=[pltpu.VMEM(value.shape, value.dtype) for value in inputs]
        + [pltpu.SemaphoreType.DMA((6,))],
        compiler_params=pltpu.CompilerParams(vmem_limit_bytes=63 * 1024 * 1024),
        name="pack",
    )(*inputs)


def fill_rows(packed_ref, rows, layer):
    for y in range(6):
        for z in range(4):
            cell = y * 4 + z
            block = packed_ref[cell]
            for number, shift in enumerate((layer, y - 1.0, z - 1.0)):
                rows[cell, number] = spread(block[number : number + 1] + shift)
            for number in range(3, 6):
                rows[cell, number] = spread(block[number : number + 1])


def move_away(flag):
    return jnp.broadcast_to((1.0 - flag) * 100.0, (8, 128))


def build_tiles(same, size, base_of, cols, away, rows, tiles_ref, start_of, total):
    sub = lax.broadcasted_iota(jnp.int32, (8, 128), 0)
    lane = lax.broadcasted_iota(jnp.int32, (8, 128), 1)

    def body(index, carry):
        cell = index // 16
        chunk = index - cell * 16
        chip, base = base_of(cell)
        xi, yi, zi, si = [cols[(chip * 4 + number) * 16 + chunk] for number in range(4)]
        sums = [start_of(system, cell, chunk) for system in range(2)]
        for number, (dy, dz) in enumerate(PLANE):
            other = base + dy * 4 + dz
            dx = away[cell * 9 + number] - xi
            dy = rows[other, 1] - yi
            dz = rows[other, 2] - zi
            square = jnp.maximum(dx * dx + dy * dy + dz * dz, 1e-30)
            ratio = square * lax.rsqrt(square)
            fourth = square * square
            taper = 1.44 + fourth * (-50.4 + ratio * (120.96 + ratio * (-100.8 + 28.8 * ratio)))
            cube = square * ratio + rows[other, 3] * si
            value = taper * jnp.exp2(jnp.log(cube) * (-1.0 / (3.0 * 0.6931471805599453)))
            keep = square < 1.0
            if same and number == 4:
                keep = keep & (sub + chunk * 8 != lane)
            value = jnp.where(keep, value, 0.0)
            tiles_ref[(cell * 9 + number) * 16 + chunk] = value
            for system in range(2):
                sums[system] = sums[system] + value * rows[other, 4 + system]
        for system in range(2):
            total[(system * size + cell) * 16 + chunk] = sums[system]
        return carry

    lax.fori_loop(0, size * 16, body, 0)


def own_base(core):
    def place(own):
        chip = core * 4 + own
        return chip, (1 + chip // 2) * 4 + 1 + chip % 2

    return place


def chip_base(cell):
    return cell, (1 + cell // 2) * 4 + 1 + cell % 2


def nothing(system, cell, chunk):
    return jnp.zeros((8, 128), jnp.float32)


def partly(before, core):
    def start(system, cell, chunk):
        mine = jnp.where(cell // 4 == core, 1.0, 0.0)
        return before[(system * 4 + cell % 4) * 16 + chunk] * mine

    return start


def same_kernel(place_ref, region_ref, tiles_ref, cols_ref, total_ref, field_ref, aux_ref, rows, away):
    core = place_ref[0]
    fill_rows(region_ref, rows, 0.0)
    for chip, cell in enumerate(CHIP):
        for number in range(4):
            column = jnp.broadcast_to(rows[cell, number, 0:1, :], (128, 128)).T
            start = (chip * 4 + number) * 16
            cols_ref[start : start + 16] = column.reshape(16, 8, 128)
    for cell in range(24):
        mask = -region_ref[cell, 5:6]
        for system in range(2):
            row = system * 24 + cell
            field_ref[row : row + 1] = region_ref[cell, 4 + system : 5 + system]
            aux_ref[row : row + 1] = mask
            aux_ref[48 + row : 49 + row] = region_ref[cell, 7:8] * mask
    for own in range(4):
        _, base = own_base(core)(own)
        for number, (dy, dz) in enumerate(PLANE):
            other = base + dy * 4 + dz
            row = rows[other, 0]
            if (0, dy, dz) in CODES:
                code = CODES[0, dy, dz]
                row = row + move_away(region_ref[base, 6:7, code : code + 1])
            elif (dy, dz) != (0, 0):
                code = CODES[0, -dy, -dz]
                row = row + move_away(region_ref[other, 6:7, code : code + 1])
            away[own * 9 + number] = row
    build_tiles(True, 4, own_base(core), cols_ref, away, rows, tiles_ref, nothing, total_ref)


def side_kernel(place_ref, region_ref, side_ref, cols_ref, before_ref, tiles_ref, image_ref, rows, away, total):
    core = place_ref[0]
    upper = jnp.where(core == 1, 1.0, 0.0)
    fill_rows(side_ref, rows, 2.0 * upper - 1.0)
    for chip, cell in enumerate(CHIP):
        for number, (dy, dz) in enumerate(PLANE):
            other = cell + dy * 4 + dz
            code, back = CODES[1, dy, dz], CODES[1, -dy, -dz]
            flag = upper * region_ref[cell, 6:7, code : code + 1]
            flag = flag + (1.0 - upper) * side_ref[other, 6:7, back : back + 1]
            away[chip * 9 + number] = rows[other, 0] + move_away(flag)
    start = partly(before_ref, core)
    build_tiles(False, 8, chip_base, cols_ref, away, rows, tiles_ref, start, total)
    reduce_rows(total, image_ref)


SHAPE = functools.partial(jax.ShapeDtypeStruct, dtype=jnp.float32)


def cost(flops):
    return pl.CostEstimate(flops=flops, bytes_accessed=4 * 1024 * 1024, transcendentals=0)


def run_same(place, region):
    return pl.pallas_call(
        same_kernel,
        out_shape=(
            SHAPE((36 * 16, 8, 128)),
            SHAPE((512, 8, 128)),
            SHAPE((128, 8, 128)),
            SHAPE((48, 128)),
            SHAPE((96, 128)),
        ),
        in_specs=[SMEM, VMEM],
        out_specs=(VMEM,) * 5,
        scratch_shapes=[
            pltpu.VMEM((24, 6, 8, 128), jnp.float32),
            pltpu.VMEM((36, 8, 128), jnp.float32),
        ],
        compiler_params=PARAMS,
        cost_estimate=cost(40 * 36 * 16384),
        name="tiles_same",
    )(place, region)


def run_side(*inputs):
    return pl.pallas_call(
        side_kernel,
        out_shape=(SHAPE((72 * 16, 8, 128)), SHAPE((16, 128))),
        in_specs=[SMEM] + [VMEM] * 4,
        out_specs=(VMEM,) * 2,
        scratch_shapes=[
            pltpu.VMEM((24, 6, 8, 128), jnp.float32),
            pltpu.VMEM((72, 8, 128), jnp.float32),
            pltpu.VMEM((256, 8, 128), jnp.float32),
        ],
        compiler_params=PARAMS,
        cost_estimate=cost(40 * 72 * 16384),
        name="tiles_side",
    )(*inputs)


def gram_row(fields, last):
    lane = lax.broadcasted_iota(jnp.int32, (1, 128), 1)
    row = jnp.zeros((1, 128), jnp.float32)
    for system in range(2):
        mine = [0.5 * field for field in fields[system]]
        entries = [
            fields[system][i] * last[system] if j == 4 else mine[i] * fields[system][j] for i, j in PAIRS
        ] + mine
        for number, entry in enumerate(entries):
            part = jnp.sum(jnp.sum(entry, axis=0, keepdims=True), axis=1, keepdims=True)
            row = row + jnp.where(lane == 2 * number + system, part, 0.0)
    return row


def fill_fields(field_ref, rows):
    for system in range(2):
        for cell in range(24):
            row = system * 24 + cell
            rows[cell * 2 + system] = spread(field_ref[row : row + 1])


def apply_tiles(size, base_of, tiles_ref, rows, start_of, total):
    def body(index, carry):
        cell = index // 4
        group = index - cell * 4
        _, base = base_of(cell)
        chunks = [group * 4 + part for part in range(4)]
        sums = [[start_of(system, cell, chunk) for chunk in chunks] for system in range(2)]
        for number, (dy, dz) in enumerate(PLANE):
            other = base + dy * 4 + dz
            right = [rows[other * 2 + system] for system in range(2)]
            for part, chunk in enumerate(chunks):
                tile = tiles_ref[(cell * 9 + number) * 16 + chunk]
                for system in range(2):
                    sums[system][part] = sums[system][part] + tile * right[system]
        for system in range(2):
            for part, chunk in enumerate(chunks):
                total[(system * size + cell) * 16 + chunk] = sums[system][part]
        return carry

    lax.fori_loop(0, size * 4, body, 0)


def update_kernel(step, place_ref, every_ref, aux_ref, *refs):
    fields, next_ref, image = refs[: step + 1], refs[step + 1], refs[step + 2]
    chips, line, chip_y, chip_z = place_ref[1], place_ref[2], place_ref[3], place_ref[4]
    ys = [(lax.rem(chip_y + chips - 1, chips), 3)]
    ys += [(chip_y, inner) for inner in range(4)] + [(lax.rem(chip_y + 1, chips), 0)]
    zs = [(lax.rem(chip_z + line - 1, line), 1), (chip_z, 0), (chip_z, 1), (lax.rem(chip_z + 1, line), 0)]
    for y, (place_y, inner_y) in enumerate(ys):
        for z, (place_z, inner_z) in enumerate(zs):
            device = 2 * place_y * line + place_z
            for system in range(2):
                source = system * 8 + inner_y * 2 + inner_z
                row = system * 24 + y * 4 + z
                both = every_ref[device, source : source + 1] + every_ref[device + line, source : source + 1]
                image[row : row + 1] = both
    before = fields[step - 1][...] if step else None
    next_ref[...] = next_basis(step, image[...], fields[step][...], before, aux_ref[0:48], aux_ref[48:96])


def run_update(step, place, every, aux, fields):
    return pl.pallas_call(
        functools.partial(update_kernel, step),
        out_shape=SHAPE((48, 128)),
        in_specs=[SMEM] + [VMEM] * (2 + len(fields)),
        out_specs=VMEM,
        scratch_shapes=[pltpu.VMEM((48, 128), jnp.float32)],
        compiler_params=PARAMS,
        name=f"update{step}",
    )(place, every, aux, *fields)


def apply_same_kernel(place_ref, tiles_ref, field_ref, total_ref, rows):
    fill_fields(field_ref, rows)
    apply_tiles(4, own_base(place_ref[0]), tiles_ref, rows, nothing, total_ref)


def apply_side_kernel(last, place_ref, tiles_ref, side_ref, before_ref, *refs):
    core = place_ref[0]
    if last:
        aux_ref, fields, image_ref, (rows, total) = refs[0], refs[1:5], refs[5], refs[6:]
        partial = image_ref.at[8:24]
    else:
        image_ref, rows, total = refs
        partial = image_ref
    fill_fields(side_ref, rows)
    apply_tiles(8, chip_base, tiles_ref, rows, partly(before_ref, core), total)
    reduce_rows(total, partial)
    if last:

        def chip(ref, system, first):
            parts = [ref[first + system * 24 + cell : first + system * 24 + cell + 2] for cell in (5, 9, 13, 17)]
            return jnp.concatenate(parts, axis=0)

        mine = [[chip(field, system, 0) for field in fields] for system in range(2)]
        images = []
        for system in range(2):
            diagonal = 0.5 * (chip(aux_ref, system, 48) - SHIFT[3])
            image = partial[system * 8 : system * 8 + 8] + diagonal * mine[system][3]
            images.append(image * (1.0 / SCALE[3]) - 0.5 * BACK[3] * mine[system][2])
        image_ref[0:8] = jnp.broadcast_to(gram_row(mine, images), (8, 128))


def run_apply_same(place, tiles, field):
    return pl.pallas_call(
        apply_same_kernel,
        out_shape=SHAPE((128, 8, 128)),
        in_specs=[SMEM] + [VMEM] * 2,
        out_specs=VMEM,
        scratch_shapes=[pltpu.VMEM((48, 8, 128), jnp.float32)],
        compiler_params=PARAMS,
        cost_estimate=cost(4 * 36 * 16384),
        name="apply_same",
    )(place, tiles, field)


def run_apply_side(last, place, tiles, side, before, *more):
    return pl.pallas_call(
        functools.partial(apply_side_kernel, last),
        out_shape=SHAPE((24 if last else 16, 128)),
        in_specs=[SMEM] + [VMEM] * (3 + len(more)),
        out_specs=VMEM,
        scratch_shapes=[
            pltpu.VMEM((48, 8, 128), jnp.float32),
            pltpu.VMEM((256, 8, 128), jnp.float32),
        ],
        compiler_params=PARAMS,
        cost_estimate=cost(4 * 72 * 16384),
        name="apply_last" if last else "apply_side",
    )(place, tiles, side, before, *more)


def combine(coefs, fields):
    value = coefs[0] * fields[0]
    for coef, field in zip(coefs[1:], fields[1:]):
        value = value + coef * field
    return value


def finish_kernel(place_ref, gram_ref, every_ref, aux_ref, *refs):
    regions, (charges_ref, residual_ref, own, image) = refs[:4], refs[4:]
    core, line, chip_y, chip_z = place_ref[0], place_ref[2], place_ref[3], place_ref[4]
    device = 2 * chip_y * line + chip_z
    for system in range(2):
        for cell in range(4):
            row = system * 4 + cell
            place = system * 24 + (1 + 2 * core + cell // 2) * 4 + 1 + cell % 2
            source = 8 + system * 8 + 4 * core + cell
            both = every_ref[device, pl.ds(source, 1)] + every_ref[device + line, pl.ds(source, 1)]
            image[row : row + 1] = both
            for number, region in enumerate(regions):
                own[number, row : row + 1] = region[pl.ds(place, 1)]
            own[4, row : row + 1] = aux_ref[pl.ds(place, 1)]
            own[5, row : row + 1] = aux_ref[pl.ds(48 + place, 1)]
    fields = [own[number] for number in range(4)]
    fields.append(next_basis(3, image[...], fields[3], fields[2], own[4], own[5]))
    summed = spread(jnp.sum(gram_ref[...], axis=0, keepdims=True))
    lane = lax.broadcasted_iota(jnp.int32, (8, 128), 1)
    system = lax.broadcasted_iota(jnp.int32, (8, 128), 0) // 4

    def entry(number):
        picked = jnp.where(lane == 2 * number + system, summed, 0.0)
        return jnp.broadcast_to(jnp.sum(picked, axis=1, keepdims=True), (8, 128))

    gram = {}
    for number, (i, j) in enumerate(PAIRS):
        gram[i, j] = gram[j, i] = entry(number)
    totals = [entry(len(PAIRS) + number) for number in range(4)]

    def dot(left, right):
        result = None
        for i, a in enumerate(left):
            part = None
            for j, b in enumerate(right):
                term = gram[i, j] * b
                part = term if part is None else part + term
            result = a * part if result is None else result + a * part
        return result

    def multiply(vector):
        size = len(vector)
        out = []
        for row in range(size + 1):
            value = None
            if row >= 1:
                value = SCALE[row - 1] * vector[row - 1]
            if row < size:
                term = SHIFT[row] * vector[row]
                value = term if value is None else value + term
            if row + 1 < size:
                value = value + SCALE[row + 1] * BACK[row + 1] * vector[row + 1]
            out.append(value)
        return out

    one = jnp.ones((8, 128), jnp.float32)
    residual = [one]
    direction = [one]
    answer = []
    norm_now = gram[0, 0]
    for step in range(4):
        image = multiply(direction)
        alpha = norm_now / dot(direction, image)
        answer = [
            alpha * d if k >= len(answer) else answer[k] + alpha * d for k, d in enumerate(direction)
        ]
        residual = [
            residual[k] - alpha * value if k < len(residual) else -alpha * value
            for k, value in enumerate(image)
        ]
        if step == 3:
            break
        norm_next = dot(residual, residual)
        ratio = norm_next / norm_now
        direction = [
            value + ratio * direction[k] if k < len(direction) else value
            for k, value in enumerate(residual)
        ]
        norm_now = norm_next
    value = combine(residual, fields)
    solution = combine(answer, fields[:4])
    total = combine(answer, totals)
    charges = solution[0:4] - total[0:4] / total[4:8] * solution[4:8]
    for y in range(2):
        charges_ref[0, y] = charges[2 * y : 2 * y + 2]
        for system in range(2):
            row = system * 4 + 2 * y
            residual_ref[system, 0, y] = value[row : row + 2]


def run_finish(place, gram, every, aux, fields):
    return pl.pallas_call(
        finish_kernel,
        out_shape=(SHAPE((1, 2, 2, 128)), SHAPE((2, 1, 2, 2, 128))),
        in_specs=[SMEM] + [VMEM] * 7,
        out_specs=(VMEM, VMEM),
        scratch_shapes=[pltpu.VMEM((6, 8, 128), jnp.float32), pltpu.VMEM((8, 128), jnp.float32)],
        compiler_params=PARAMS,
        name="finish",
    )(place, gram, every, aux, *fields)


def opposite(value):
    count_x, count_y = lax.axis_size("gx"), lax.axis_size("gy")
    pairs = []
    for x in range(count_x):
        for y in range(count_y):
            target = (x + 1) % count_x if y % 2 == 0 else (x - 1) % count_x
            pairs.append((x * count_y + y, target * count_y + y))
    return lax.ppermute(value, ("gx", "gy"), pairs)


def spread_all(value, axes, count):
    sent = jnp.broadcast_to(value[None], (count,) + value.shape)
    return lax.all_to_all(sent, axes, 0, 0)


def region_of(every, chips, line, chip_y, chip_z):
    def part(place, axis):
        return lax.dynamic_index_in_dim(every, place, axis, keepdims=False)

    every = every.reshape((chips, 2, line) + every.shape[2:])
    every = jnp.moveaxis(every, 2, 1).reshape((chips, line, 4) + every.shape[4:])
    below = part(lax.rem(chip_y + chips - 1, chips), 0)[:, 3:4]
    above = part(lax.rem(chip_y + 1, chips), 0)[:, 0:1]
    every = jnp.concatenate([below, part(chip_y, 0), above], axis=1)
    below = part(lax.rem(chip_z + line - 1, line), 0)[:, 1:2]
    above = part(lax.rem(chip_z + 1, line), 0)[:, 0:1]
    return jnp.concatenate([below, part(chip_z, 0), above], axis=1)


def shards(frac_positions, shielding, hardness, electroneg, counts, neighbor_list):
    count_x, count_y, count_z = [lax.axis_size(axis) for axis in ("gx", "gy", "gz")]
    chips, plane = count_y // 2, count_y * count_z
    chip_y, core = lax.axis_index("gy") // 2, lax.rem(lax.axis_index("gy"), 2)
    chip_z = lax.axis_index("gz")
    place = jnp.stack([core, jnp.int32(chips), jnp.int32(count_z), chip_y, chip_z])

    places = frac_positions.transpose(0, 1, 3, 2, 4)
    packed = run_pack(plane, places, shielding, hardness, electroneg, counts, neighbor_list)
    every = lax.all_to_all(packed, ("gy", "gz"), 0, 0)
    every = every.reshape(count_y, count_z, 2, 2, 8, 128)
    region = region_of(every, chips, count_z, chip_y, chip_z).reshape(24, 8, 128)
    side = opposite(region)
    tiles_same, cols, total, field, aux = run_same(place, region)
    tiles_side, image = run_side(place, region, side, cols, total)
    fields = [field]
    for step in range(3):
        every = spread_all(image, ("gy", "gz"), plane)
        fields.append(run_update(step, place, every, aux, fields))
        side = opposite(fields[-1])
        total = run_apply_same(place, tiles_same, fields[-1])
        more = [aux] + fields if step == 2 else []
        image = run_apply_side(step == 2, place, tiles_side, side, total, *more)
    every = spread_all(image, ("gy", "gz"), plane)
    gram = spread_all(jnp.sum(every[:, 0:1], axis=0), "gx", count_x)
    return run_finish(place, gram.reshape(count_x, 128), every, aux, fields)


def solution(mesh):
    placed = (
        P("gx", "gy", "gz", None, None),
        P("gx", "gy", "gz", None),
        P("gx", "gy", "gz", None),
        P("gx", "gy", "gz", None),
        P("gx", "gy", "gz"),
        P("gx", "gy", "gz", None),
    )
    return jax.shard_map(
        shards,
        mesh=mesh,
        in_specs=placed,
        out_specs=(P("gx", "gy", "gz", None), P(None, "gx", "gy", "gz", None)),
        check_vma=False,
    )
```

```python
import functools

import jax
import jax.numpy as jnp
from jax import lax
from jax.experimental import pallas as pl
from jax.experimental.pallas import tpu as pltpu
from jax.sharding import PartitionSpec as P

CODES = {
    (0, 0, 1): 0,
    (0, 1, -1): 1,
    (0, 1, 0): 2,
    (0, 1, 1): 3,
    (1, -1, -1): 4,
    (1, -1, 0): 5,
    (1, -1, 1): 6,
    (1, 0, -1): 7,
    (1, 0, 0): 8,
    (1, 0, 1): 9,
    (1, 1, -1): 10,
    (1, 1, 0): 11,
    (1, 1, 1): 12,
}
SHELL = [(x, y, z) for x in (-1, 0, 1) for y in (-1, 0, 1) for z in (-1, 0, 1)]

SHIFT = (220.0, 110.0, 145.0, 140.0)
SCALE = (60.0, 70.0, 70.0, 70.0)
BACK = (0.0, 0.7, 1.0, 1.0)
PAIRS = [(i, j) for i in range(4) for j in range(i, 5)]
VMEM = pl.BlockSpec(memory_space=pltpu.VMEM)
SMEM = pl.BlockSpec(memory_space=pltpu.SMEM)
PARAMS = pltpu.CompilerParams(vmem_limit_bytes=24 * 1024 * 1024)


OWN = [(1 + y) * 4 + 1 + z for y in range(2) for z in range(2)]
SAME = [offset for offset in SHELL if offset[0] == 0]
SIDE = [offset for offset in SHELL if offset[0] != 0]


def spread(row):
    return jnp.broadcast_to(row, (8, 128))


def reduce_rows(total_ref, image_ref):
    for field in range(8):
        block = total_ref[field * 16 : (field + 1) * 16].reshape(128, 128)
        image_ref[field : field + 1, :] = jnp.sum(block.T, axis=0, keepdims=True)


def next_basis(step, image, field, before, mask, hard):
    value = image * mask + hard * field
    value = (value - SHIFT[step] * field) * (1.0 / SCALE[step])
    if BACK[step]:
        value = value - BACK[step] * before
    return value


def pack_kernel(order_ref, *refs):
    sources, packed_ref, inputs, semaphores = refs[:6], refs[6], refs[7:13], refs[13]
    copies = [
        pltpu.make_async_copy(source, target, semaphores.at[number])
        for number, (source, target) in enumerate(zip(sources, inputs))
    ]
    for copy in copies:
        copy.start()
    for copy in copies:
        copy.wait()
    place_ref, shield_ref, hard_ref, electro_ref, count_ref, list_ref = inputs
    lane = lax.broadcasted_iota(jnp.int32, (1, 128), 1)
    for y in range(2):
        for z in range(2):
            cell = 2 * y + z
            count = jnp.broadcast_to(count_ref[0, y : y + 1, z : z + 1], (1, 128))
            mask = jnp.where(lane < count, 1.0, 0.0)
            flags = jnp.zeros((1, 128), jnp.float32)
            for number in range(13):
                code = jnp.broadcast_to(list_ref[0, y, z : z + 1, number : number + 1], (1, 128))
                flags = jnp.where(lane == code, 1.0, flags)
            rows = []
            for number in range(3):
                rows.append(place_ref[0, y, number, z : z + 1])
            shield = shield_ref[0, y, z : z + 1]
            rows.append(jnp.exp(-1.5 * jnp.log(shield)) * (1000.0**-0.5))
            rows.append(-electro_ref[0, y, z : z + 1] * mask)
            rows.append(-mask)
            rows.append(flags)
            rows.append(hard_ref[0, y, z : z + 1])
            block = jnp.concatenate(rows, axis=0)
            for copy in range(packed_ref.shape[0]):
                packed_ref[copy, cell] = block


def run_pack(count, order, *inputs):
    return pl.pallas_call(
        pack_kernel,
        out_shape=jax.ShapeDtypeStruct((count, 4, 8, 128), jnp.float32),
        in_specs=[SMEM] + [pl.BlockSpec(memory_space=pltpu.HBM)] * 6,
        out_specs=VMEM,
        scratch_shapes=[pltpu.VMEM(value.shape, value.dtype) for value in inputs]
        + [pltpu.SemaphoreType.DMA((6,))],
        compiler_params=pltpu.CompilerParams(vmem_limit_bytes=63 * 1024 * 1024),
        name="pack",
    )(order, *inputs)


def fill_rows(packed_ref, rows, first, layer):
    for y in range(4):
        for z in range(4):
            cell = y * 4 + z
            block = packed_ref[cell]
            for number, shift in enumerate((float(layer), y - 1.0, z - 1.0)):
                rows[first + cell, number] = spread(block[number : number + 1] + shift)
            for number in range(3, 6):
                rows[first + cell, number] = spread(block[number : number + 1])


def neighbor(offset):
    layer = 1 if offset[0] == 1 else 0
    return layer * 16 + (1 + offset[1]) * 4 + 1 + offset[2]


def fill_away(offsets, own_ref, lower_ref, rows, away):
    for own, cell in enumerate(OWN):
        y, z = own // 2, own % 2
        for number, offset in enumerate(offsets):
            row = rows[neighbor(offset) + y * 4 + z, 0]
            if offset in CODES:
                flag = own_ref[cell, 6:7, CODES[offset] : CODES[offset] + 1]
            elif offset == (0, 0, 0):
                flag = None
            else:
                code = CODES[tuple(-value for value in offset)]
                flag = lower_ref[cell + offset[1] * 4 + offset[2], 6:7, code : code + 1]
            if flag is not None:
                row = row + jnp.broadcast_to((1.0 - flag) * 100.0, (8, 128))
            away[own * len(offsets) + number] = row


def build_tiles(offsets, rows, cols, away, tiles_ref, before, total):
    sub = lax.broadcasted_iota(jnp.int32, (8, 128), 0)
    lane = lax.broadcasted_iota(jnp.int32, (8, 128), 1)
    size = len(offsets)

    def body(own, base, chunk):
        xi, yi, zi, si = [cols[(own * 4 + number) * 16 + chunk] for number in range(4)]
        if before is None:
            sums = [jnp.zeros((8, 128), jnp.float32) for _ in range(2)]
        else:
            sums = [before[(system * 4 + own) * 16 + chunk] for system in range(2)]
        for number, offset in enumerate(offsets):
            cell = base + neighbor(offset)
            dx = away[own * size + number] - xi
            dy = rows[cell, 1] - yi
            dz = rows[cell, 2] - zi
            square = jnp.maximum(dx * dx + dy * dy + dz * dz, 1e-30)
            ratio = square * lax.rsqrt(square)
            fourth = square * square
            taper = 1.44 + fourth * (-50.4 + ratio * (120.96 + ratio * (-100.8 + 28.8 * ratio)))
            cube = square * ratio + rows[cell, 3] * si
            value = taper * jnp.exp2(jnp.log(cube) * (-1.0 / (3.0 * 0.6931471805599453)))
            keep = square < 1.0
            if offset == (0, 0, 0):
                keep = keep & (sub + chunk * 8 != lane)
            value = jnp.where(keep, value, 0.0)
            tiles_ref[(own * size + number) * 16 + chunk] = value
            for system in range(2):
                sums[system] = sums[system] + value * rows[cell, 4 + system]
        for system in range(2):
            total[(system * 4 + own) * 16 + chunk] = sums[system]

    for own in range(4):
        base = (own // 2) * 4 + own % 2

        def step(index, carry, own=own, base=base):
            for part in range(2):
                body(own, base, index * 2 + part)
            return carry

        lax.fori_loop(0, 8, step, 0)


def same_kernel(own_ref, tiles_ref, cols_ref, total_ref, field_ref, aux_ref, rows, away):
    fill_rows(own_ref, rows, 0, 0)
    for own, cell in enumerate(OWN):
        for number in range(4):
            column = jnp.broadcast_to(rows[cell, number, 0:1, :], (128, 128)).T
            start = (own * 4 + number) * 16
            cols_ref[start : start + 16] = column.reshape(16, 8, 128)
        for system in range(2):
            row = system * 4 + own
            mask = -own_ref[cell, 5:6]
            field_ref[row : row + 1] = own_ref[cell, 4 + system : 5 + system]
            aux_ref[row : row + 1] = mask
            aux_ref[8 + row : 9 + row] = own_ref[cell, 7:8] * mask
    fill_away(SAME, own_ref, own_ref, rows, away)
    build_tiles(SAME, rows, cols_ref, away, tiles_ref, None, total_ref)


def side_kernel(own_ref, lower_ref, upper_ref, cols_ref, before_ref, field_ref, aux_ref, tiles_ref, next_ref, rows, away, total, image):
    fill_rows(lower_ref, rows, 0, -1)
    fill_rows(upper_ref, rows, 16, 1)
    fill_away(SIDE, own_ref, lower_ref, rows, away)
    build_tiles(SIDE, rows, cols_ref, away, tiles_ref, before_ref, total)
    reduce_rows(total, image)
    next_ref[...] = next_basis(0, image[...], field_ref[...], None, aux_ref[0:8], aux_ref[8:16])


SHAPE = functools.partial(jax.ShapeDtypeStruct, dtype=jnp.float32)


def cost(flops):
    return pl.CostEstimate(flops=flops, bytes_accessed=4 * 1024 * 1024, transcendentals=0)


def run_same(own):
    return pl.pallas_call(
        same_kernel,
        out_shape=(
            SHAPE((36 * 16, 8, 128)),
            SHAPE((256, 8, 128)),
            SHAPE((128, 8, 128)),
            SHAPE((8, 128)),
            SHAPE((16, 128)),
        ),
        in_specs=[VMEM],
        out_specs=(VMEM,) * 5,
        scratch_shapes=[
            pltpu.VMEM((16, 6, 8, 128), jnp.float32),
            pltpu.VMEM((36, 8, 128), jnp.float32),
        ],
        compiler_params=PARAMS,
        cost_estimate=cost(40 * 36 * 16384),
        name="tiles_same",
    )(own)


def run_side(*inputs):
    return pl.pallas_call(
        side_kernel,
        out_shape=(SHAPE((72 * 16, 8, 128)), SHAPE((8, 128))),
        in_specs=[VMEM] * 7,
        out_specs=(VMEM,) * 2,
        scratch_shapes=[
            pltpu.VMEM((32, 6, 8, 128), jnp.float32),
            pltpu.VMEM((72, 8, 128), jnp.float32),
            pltpu.VMEM((128, 8, 128), jnp.float32),
            pltpu.VMEM((8, 128), jnp.float32),
        ],
        compiler_params=PARAMS,
        cost_estimate=cost(40 * 72 * 16384),
        name="tiles_side",
    )(*inputs)


def gram_row(fields):
    entries = [fields[i] * fields[j] for i, j in PAIRS] + fields[:4]
    lane = lax.broadcasted_iota(jnp.int32, (1, 128), 1)
    row = jnp.zeros((1, 128), jnp.float32)
    for number, entry in enumerate(entries):
        for system in range(2):
            part = jnp.sum(entry[system * 4 : system * 4 + 4], axis=0, keepdims=True)
            part = jnp.sum(part, axis=1, keepdims=True)
            row = row + jnp.where(lane == 2 * number + system, part, 0.0)
    return row


def fill_fields(halo_ref, rows, first):
    for system in range(2):
        for cell in range(16):
            row = system * 16 + cell
            rows[(first + cell) * 2 + system] = spread(halo_ref[row : row + 1])


def apply_tiles(offsets, tiles_ref, rows, before, total):
    size = len(offsets)

    for own in range(4):
        base = (own // 2) * 4 + own % 2
        for group in range(4):
            places = [[(system * 4 + own) * 16 + group * 4 + part for part in range(4)] for system in range(2)]
            if before is None:
                sums = [[None] * 4 for _ in range(2)]
            else:
                sums = [[before[place] for place in line] for line in places]
            for number, offset in enumerate(offsets):
                cell = base + neighbor(offset)
                right = [rows[cell * 2 + system] for system in range(2)]
                for part in range(4):
                    tile = tiles_ref[(own * size + number) * 16 + group * 4 + part]
                    for system in range(2):
                        term = tile * right[system]
                        held = sums[system][part]
                        sums[system][part] = term if held is None else held + term
            for system in range(2):
                for part in range(4):
                    total[places[system][part]] = sums[system][part]


def apply_same_kernel(tiles_ref, halo_ref, total_ref, rows):
    fill_fields(halo_ref, rows, 0)
    apply_tiles(SAME, tiles_ref, rows, None, total_ref)


def apply_side_kernel(step, last, tiles_ref, lower_ref, upper_ref, before_ref, aux_ref, *refs):
    count = step + 1
    fields, next_ref, rest = refs[:count], refs[count], refs[count + 1 :]
    if last:
        gram_ref, rest = rest[0], rest[1:]
    rows, total, image = rest
    fill_fields(lower_ref, rows, 0)
    fill_fields(upper_ref, rows, 16)
    apply_tiles(SIDE, tiles_ref, rows, before_ref, total)
    reduce_rows(total, image)
    values = [field[...] for field in fields]
    new = next_basis(step, image[...], values[-1], values[-2], aux_ref[0:8], aux_ref[8:16])
    next_ref[...] = new
    if last:
        gram_ref[...] = gram_row(values + [new])


def run_apply_same(tiles, halo):
    return pl.pallas_call(
        apply_same_kernel,
        out_shape=SHAPE((128, 8, 128)),
        in_specs=[VMEM] * 2,
        out_specs=VMEM,
        scratch_shapes=[pltpu.VMEM((32, 8, 128), jnp.float32)],
        compiler_params=PARAMS,
        cost_estimate=cost(4 * 36 * 16384),
        name="apply_same",
    )(tiles, halo)


def run_apply_side(step, last, tiles, lower, upper, before, aux, fields):
    outs = (SHAPE((8, 128)), SHAPE((1, 128))) if last else (SHAPE((8, 128)),)
    return pl.pallas_call(
        functools.partial(apply_side_kernel, step, last),
        out_shape=outs,
        in_specs=[VMEM] * (5 + len(fields)),
        out_specs=tuple(VMEM for _ in outs),
        scratch_shapes=[
            pltpu.VMEM((64, 8, 128), jnp.float32),
            pltpu.VMEM((128, 8, 128), jnp.float32),
            pltpu.VMEM((8, 128), jnp.float32),
        ],
        compiler_params=PARAMS,
        cost_estimate=cost(4 * 72 * 16384),
        name=f"apply_side{step}",
    )(tiles, lower, upper, before, aux, *fields)


def combine(coefs, fields):
    value = coefs[0] * fields[0]
    for coef, field in zip(coefs[1:], fields[1:]):
        value = value + coef * field
    return value


def finish_kernel(gram_ref, w0, w1, w2, w3, w4, charges_ref, residual_ref):
    fields = [ref[...] for ref in (w0, w1, w2, w3, w4)]
    summed = spread(jnp.sum(gram_ref[...], axis=0, keepdims=True))
    lane = lax.broadcasted_iota(jnp.int32, (8, 128), 1)
    system = lax.broadcasted_iota(jnp.int32, (8, 128), 0) // 4

    def entry(number):
        picked = jnp.where(lane == 2 * number + system, summed, 0.0)
        return jnp.broadcast_to(jnp.sum(picked, axis=1, keepdims=True), (8, 128))

    gram = {}
    for number, (i, j) in enumerate(PAIRS):
        gram[i, j] = gram[j, i] = entry(number)
    totals = [entry(len(PAIRS) + number) for number in range(4)]

    def dot(left, right):
        result = None
        for i, a in enumerate(left):
            part = None
            for j, b in enumerate(right):
                term = gram[i, j] * b
                part = term if part is None else part + term
            result = a * part if result is None else result + a * part
        return result

    def multiply(vector):
        size = len(vector)
        out = []
        for row in range(size + 1):
            value = None
            if row >= 1:
                value = SCALE[row - 1] * vector[row - 1]
            if row < size:
                term = SHIFT[row] * vector[row]
                value = term if value is None else value + term
            if row + 1 < size:
                value = value + SCALE[row + 1] * BACK[row + 1] * vector[row + 1]
            out.append(value)
        return out

    one = jnp.ones((8, 128), jnp.float32)
    residual = [one]
    direction = [one]
    answer = []
    norm_now = gram[0, 0]
    for step in range(4):
        image = multiply(direction)
        alpha = norm_now / dot(direction, image)
        answer = [
            alpha * d if k >= len(answer) else answer[k] + alpha * d for k, d in enumerate(direction)
        ]
        residual = [
            residual[k] - alpha * value if k < len(residual) else -alpha * value
            for k, value in enumerate(image)
        ]
        if step == 3:
            break
        norm_next = dot(residual, residual)
        ratio = norm_next / norm_now
        direction = [
            value + ratio * direction[k] if k < len(direction) else value
            for k, value in enumerate(residual)
        ]
        norm_now = norm_next
    value = combine(residual, fields)
    solution = combine(answer, fields[:4])
    total = combine(answer, totals)
    charges = solution[0:4] - total[0:4] / total[4:8] * solution[4:8]
    for y in range(2):
        charges_ref[0, y] = charges[2 * y : 2 * y + 2]
        for system in range(2):
            row = system * 4 + 2 * y
            residual_ref[system, 0, y] = value[row : row + 2]


def run_finish(gathered, fields):
    shape = functools.partial(jax.ShapeDtypeStruct, dtype=jnp.float32)
    return pl.pallas_call(
        finish_kernel,
        out_shape=(shape((1, 2, 2, 128)), shape((2, 1, 2, 2, 128))),
        in_specs=[VMEM] * 6,
        out_specs=(VMEM, VMEM),
        compiler_params=PARAMS,
        name="finish",
    )(gathered, *fields)


def shifted(value, axis, steps):
    count = lax.axis_size(axis)
    pairs = [(source, (source + steps) % count) for source in range(count)]
    return lax.ppermute(value, axis, pairs)


def spread_all(value, axes, count):
    sent = jnp.broadcast_to(value[None], (count,) + value.shape)
    return lax.all_to_all(sent, axes, 0, 0)


def wrapped(axis):
    here, count = lax.axis_index(axis), lax.axis_size(axis)
    below = jnp.where(here == 0, count - 1, here - 1)
    above = jnp.where(here == count - 1, 0, here + 1)
    return [value.astype(jnp.uint32) for value in (below, here, above)]


def around(every, places, cells):
    def part(place):
        start = [place] + [jnp.uint32(0)] * (every.ndim - 1)
        return lax.dynamic_slice(every, start, (1,) + every.shape[1:])[0]

    below, here, above = [part(place) for place in places]
    cells = cells - 1
    below = lax.slice_in_dim(below, 1, 2, axis=cells)
    above = lax.slice_in_dim(above, 0, 1, axis=cells)
    return jnp.concatenate([below, here, above], axis=cells)


def exchange(sent, dim, places):
    every = lax.all_to_all(sent, ("gy", "gz"), 0, 0)
    every = every.reshape((lax.axis_size("gy"), lax.axis_size("gz")) + sent.shape[1:])
    block = around(every, places[0:3], 2 + dim)
    block = around(block, places[3:6], 2 + dim)
    return block, shifted(block, "gx", 1), shifted(block, "gx", -1)


def shards(frac_positions, shielding, hardness, electroneg, counts, neighbor_list):
    count_x, count_y, count_z = [lax.axis_size(axis) for axis in ("gx", "gy", "gz")]
    places = frac_positions.transpose(0, 1, 3, 2, 4)
    count = count_y * count_z
    indices = lax.optimization_barrier(wrapped("gy") + wrapped("gz"))
    order = sum(indices[1:], indices[0]).astype(jnp.int32).reshape(1)
    packed = run_pack(count, order, places, shielding, hardness, electroneg, counts, neighbor_list)
    layers = exchange(packed.reshape(count, 2, 2, 8, 128), 0, indices)
    own, lower, upper = [layer.reshape(16, 8, 128) for layer in layers]
    tiles_same, cols, total, w0, aux = run_same(own)
    tiles_side, w1 = run_side(own, lower, upper, cols, total, w0, aux)
    fields = [w0, w1]
    for step in (1, 2, 3):
        sent = jnp.broadcast_to(fields[-1].reshape(1, 2, 2, 2, 128), (count, 2, 2, 2, 128))
        layers = exchange(sent, 1, indices)
        own, lower, upper = [layer.reshape(32, 128) for layer in layers]
        total = run_apply_same(tiles_same, own)
        outs = run_apply_side(step, step == 3, tiles_side, lower, upper, total, aux, fields)
        fields.append(outs[0])
    gram = outs[1]
    gram = jnp.sum(spread_all(gram, ("gy", "gz"), count_y * count_z), axis=0)
    gram = spread_all(gram, "gx", count_x)
    return run_finish(gram.reshape(count_x, 128), fields)


def solution(mesh):
    placed = (
        P("gx", "gy", "gz", None, None),
        P("gx", "gy", "gz", None),
        P("gx", "gy", "gz", None),
        P("gx", "gy", "gz", None),
        P("gx", "gy", "gz"),
        P("gx", "gy", "gz", None),
    )
    return jax.shard_map(
        shards,
        mesh=mesh,
        in_specs=placed,
        out_specs=(P("gx", "gy", "gz", None), P(None, "gx", "gy", "gz", None)),
        check_vma=False,
    )
```

```python
import functools

import jax
import jax.numpy as jnp
from jax import lax
from jax.experimental import pallas as pl
from jax.experimental.pallas import tpu as pltpu
from jax.sharding import PartitionSpec as P

CODES = {
    (0, 0, 1): 0,
    (0, 1, -1): 1,
    (0, 1, 0): 2,
    (0, 1, 1): 3,
    (1, -1, -1): 4,
    (1, -1, 0): 5,
    (1, -1, 1): 6,
    (1, 0, -1): 7,
    (1, 0, 0): 8,
    (1, 0, 1): 9,
    (1, 1, -1): 10,
    (1, 1, 0): 11,
    (1, 1, 1): 12,
}
SHELL = [(x, y, z) for x in (-1, 0, 1) for y in (-1, 0, 1) for z in (-1, 0, 1)]

SHIFT = (220.0, 110.0, 145.0, 140.0)
SCALE = (60.0, 70.0, 70.0, 70.0)
BACK = (0.0, 0.7, 1.0, 1.0)
PAIRS = [(i, j) for i in range(4) for j in range(i, 5)]
VMEM = pl.BlockSpec(memory_space=pltpu.VMEM)
SMEM = pl.BlockSpec(memory_space=pltpu.SMEM)
PARAMS = pltpu.CompilerParams(vmem_limit_bytes=24 * 1024 * 1024)


OWN = [(1 + y) * 4 + 1 + z for y in range(2) for z in range(2)]
SAME = [offset for offset in SHELL if offset[0] == 0]
SIDE = [offset for offset in SHELL if offset[0] != 0]


def spread(row):
    return jnp.broadcast_to(row, (8, 128))


def reduce_rows(total_ref, image_ref):
    for field in range(8):
        block = total_ref[field * 16 : (field + 1) * 16].reshape(128, 128)
        image_ref[field : field + 1, :] = jnp.sum(block.T, axis=0, keepdims=True)


def next_basis(step, image, field, before, mask, hard):
    value = image * mask + hard * field
    value = (value - SHIFT[step] * field) * (1.0 / SCALE[step])
    if BACK[step]:
        value = value - BACK[step] * before
    return value


def pack_kernel(order_ref, *refs):
    sources, packed_ref, inputs, semaphores = refs[:6], refs[6], refs[7:13], refs[13]
    copies = [
        pltpu.make_async_copy(source, target, semaphores.at[number])
        for number, (source, target) in enumerate(zip(sources, inputs))
    ]
    for copy in copies:
        copy.start()
    for copy in copies:
        copy.wait()
    place_ref, shield_ref, hard_ref, electro_ref, count_ref, list_ref = inputs
    lane = lax.broadcasted_iota(jnp.int32, (1, 128), 1)
    for y in range(2):
        for z in range(2):
            cell = 2 * y + z
            count = jnp.broadcast_to(count_ref[0, y : y + 1, z : z + 1], (1, 128))
            mask = jnp.where(lane < count, 1.0, 0.0)
            flags = jnp.zeros((1, 128), jnp.float32)
            for number in range(13):
                code = jnp.broadcast_to(list_ref[0, y, z : z + 1, number : number + 1], (1, 128))
                flags = jnp.where(lane == code, 1.0, flags)
            rows = []
            for number in range(3):
                rows.append(place_ref[0, y, number, z : z + 1])
            shield = shield_ref[0, y, z : z + 1]
            rows.append(jnp.exp(-1.5 * jnp.log(shield)) * (1000.0**-0.5))
            rows.append(-electro_ref[0, y, z : z + 1] * mask)
            rows.append(-mask)
            rows.append(flags)
            rows.append(hard_ref[0, y, z : z + 1])
            block = jnp.concatenate(rows, axis=0)
            packed_ref[cell] = block


def run_pack(order, *inputs):
    return pl.pallas_call(
        pack_kernel,
        out_shape=jax.ShapeDtypeStruct((4, 8, 128), jnp.float32),
        in_specs=[SMEM] + [pl.BlockSpec(memory_space=pltpu.HBM)] * 6,
        out_specs=VMEM,
        scratch_shapes=[pltpu.VMEM(value.shape, value.dtype) for value in inputs]
        + [pltpu.SemaphoreType.DMA((6,))],
        compiler_params=pltpu.CompilerParams(vmem_limit_bytes=63 * 1024 * 1024),
        name="pack",
    )(order, *inputs)


def fill_rows(packed_ref, rows, first, layer):
    for y in range(4):
        for z in range(4):
            cell = y * 4 + z
            block = packed_ref[cell]
            for number, shift in enumerate((float(layer), y - 1.0, z - 1.0)):
                rows[first + cell, number] = spread(block[number : number + 1] + shift)
            for number in range(3, 6):
                rows[first + cell, number] = spread(block[number : number + 1])


def neighbor(offset):
    layer = 1 if offset[0] == 1 else 0
    return layer * 16 + (1 + offset[1]) * 4 + 1 + offset[2]


def fill_away(offsets, own_ref, lower_ref, rows, away):
    for own, cell in enumerate(OWN):
        y, z = own // 2, own % 2
        for number, offset in enumerate(offsets):
            place = neighbor(offset) + y * 4 + z
            row = rows[place, 0] + (1.0 + rows[place, 5]) * 100.0
            if offset in CODES:
                flag = own_ref[cell, 6:7, CODES[offset] : CODES[offset] + 1]
            elif offset == (0, 0, 0):
                flag = None
            else:
                code = CODES[tuple(-value for value in offset)]
                flag = lower_ref[cell + offset[1] * 4 + offset[2], 6:7, code : code + 1]
            if flag is not None:
                row = row + jnp.broadcast_to((1.0 - flag) * 100.0, (8, 128))
            away[own * len(offsets) + number] = row


def build_tiles(offsets, rows, cols, away, tiles_ref, before, total):
    sub = lax.broadcasted_iota(jnp.int32, (8, 128), 0)
    lane = lax.broadcasted_iota(jnp.int32, (8, 128), 1)
    size = len(offsets)

    def body(own, base, chunk):
        xi, yi, zi, si = [cols[(own * 4 + number) * 16 + chunk] for number in range(4)]
        if before is None:
            sums = [jnp.zeros((8, 128), jnp.float32) for _ in range(2)]
        else:
            sums = [before[(system * 4 + own) * 16 + chunk] for system in range(2)]
        for number, offset in enumerate(offsets):
            cell = base + neighbor(offset)
            dx = away[own * size + number] - xi
            dy = rows[cell, 1] - yi
            dz = rows[cell, 2] - zi
            square = jnp.maximum(dx * dx + dy * dy + dz * dz, 1e-30)
            ratio = square * lax.rsqrt(square)
            fourth = square * square
            taper = 1.44 + fourth * (-50.4 + ratio * (120.96 + ratio * (-100.8 + 28.8 * ratio)))
            cube = square * ratio + rows[cell, 3] * si
            value = taper * jnp.exp2(jnp.log(cube) * (-1.0 / (3.0 * 0.6931471805599453)))
            keep = square < 1.0
            if offset == (0, 0, 0):
                keep = keep & (sub + chunk * 8 != lane)
            value = jnp.where(keep, value, 0.0)
            tiles_ref[(own * size + number) * 16 + chunk] = value
            sums[0] = sums[0] + value * rows[cell, 4]
            sums[1] = sums[1] - value
        for system in range(2):
            total[(system * 4 + own) * 16 + chunk] = sums[system]

    for own in range(4):
        base = (own // 2) * 4 + own % 2

        def step(index, carry, own=own, base=base):
            for part in range(2):
                body(own, base, index * 2 + part)
            return carry

        lax.fori_loop(0, 8, step, 0)


def same_kernel(own_ref, tiles_ref, cols_ref, total_ref, field_ref, aux_ref, rows, away):
    fill_rows(own_ref, rows, 0, 0)
    for own, cell in enumerate(OWN):
        for number in range(4):
            column = jnp.broadcast_to(rows[cell, number, 0:1, :], (128, 128)).T
            start = (own * 4 + number) * 16
            cols_ref[start : start + 16] = column.reshape(16, 8, 128)
        for system in range(2):
            row = system * 4 + own
            mask = -own_ref[cell, 5:6]
            field_ref[row : row + 1] = own_ref[cell, 4 + system : 5 + system]
            aux_ref[row : row + 1] = mask
            aux_ref[8 + row : 9 + row] = own_ref[cell, 7:8] * mask
    fill_away(SAME, own_ref, own_ref, rows, away)
    build_tiles(SAME, rows, cols_ref, away, tiles_ref, None, total_ref)


def side_kernel(own_ref, lower_ref, upper_ref, cols_ref, before_ref, field_ref, aux_ref, tiles_ref, next_ref, rows, away, total, image):
    fill_rows(lower_ref, rows, 0, -1)
    fill_rows(upper_ref, rows, 16, 1)
    fill_away(SIDE, own_ref, lower_ref, rows, away)
    build_tiles(SIDE, rows, cols_ref, away, tiles_ref, before_ref, total)
    reduce_rows(total, image)
    next_ref[...] = next_basis(0, image[...], field_ref[...], None, aux_ref[0:8], aux_ref[8:16])


SHAPE = functools.partial(jax.ShapeDtypeStruct, dtype=jnp.float32)


def cost(flops):
    return pl.CostEstimate(flops=flops, bytes_accessed=4 * 1024 * 1024, transcendentals=0)


def run_same(own):
    return pl.pallas_call(
        same_kernel,
        out_shape=(
            SHAPE((36 * 16, 8, 128)),
            SHAPE((256, 8, 128)),
            SHAPE((128, 8, 128)),
            SHAPE((8, 128)),
            SHAPE((16, 128)),
        ),
        in_specs=[VMEM],
        out_specs=(VMEM,) * 5,
        scratch_shapes=[
            pltpu.VMEM((16, 6, 8, 128), jnp.float32),
            pltpu.VMEM((36, 8, 128), jnp.float32),
        ],
        compiler_params=PARAMS,
        cost_estimate=cost(40 * 36 * 16384),
        name="tiles_same",
    )(own)


def run_side(*inputs):
    return pl.pallas_call(
        side_kernel,
        out_shape=(SHAPE((72 * 16, 8, 128)), SHAPE((8, 128))),
        in_specs=[VMEM] * 7,
        out_specs=(VMEM,) * 2,
        scratch_shapes=[
            pltpu.VMEM((32, 6, 8, 128), jnp.float32),
            pltpu.VMEM((72, 8, 128), jnp.float32),
            pltpu.VMEM((128, 8, 128), jnp.float32),
            pltpu.VMEM((8, 128), jnp.float32),
        ],
        compiler_params=PARAMS,
        cost_estimate=cost(40 * 72 * 16384),
        name="tiles_side",
    )(*inputs)


def gram_row(fields):
    entries = [fields[i] * fields[j] for i, j in PAIRS] + fields[:4]
    lane = lax.broadcasted_iota(jnp.int32, (1, 128), 1)
    row = jnp.zeros((1, 128), jnp.float32)
    for number, entry in enumerate(entries):
        for system in range(2):
            part = jnp.sum(entry[system * 4 : system * 4 + 4], axis=0, keepdims=True)
            part = jnp.sum(part, axis=1, keepdims=True)
            row = row + jnp.where(lane == 2 * number + system, part, 0.0)
    return row


def fill_fields(halo_ref, rows, first):
    for system in range(2):
        for cell in range(16):
            row = system * 16 + cell
            rows[(first + cell) * 2 + system] = spread(halo_ref[row : row + 1])


def apply_tiles(offsets, tiles_ref, rows, before, total):
    size = len(offsets)

    for own in range(4):
        base = (own // 2) * 4 + own % 2
        for group in range(4):
            places = [[(system * 4 + own) * 16 + group * 4 + part for part in range(4)] for system in range(2)]
            if before is None:
                sums = [[None] * 4 for _ in range(2)]
            else:
                sums = [[before[place] for place in line] for line in places]
            for number, offset in enumerate(offsets):
                cell = base + neighbor(offset)
                right = [rows[cell * 2 + system] for system in range(2)]
                for part in range(4):
                    tile = tiles_ref[(own * size + number) * 16 + group * 4 + part]
                    for system in range(2):
                        term = tile * right[system]
                        held = sums[system][part]
                        sums[system][part] = term if held is None else held + term
            for system in range(2):
                for part in range(4):
                    total[places[system][part]] = sums[system][part]


def apply_same_kernel(tiles_ref, halo_ref, total_ref, rows):
    fill_fields(halo_ref, rows, 0)
    apply_tiles(SAME, tiles_ref, rows, None, total_ref)


def apply_side_kernel(step, last, tiles_ref, lower_ref, upper_ref, before_ref, aux_ref, *refs):
    count = step + 1
    fields, next_ref, rest = refs[:count], refs[count], refs[count + 1 :]
    if last:
        gram_ref, rest = rest[0], rest[1:]
    rows, total, image = rest
    fill_fields(lower_ref, rows, 0)
    fill_fields(upper_ref, rows, 16)
    apply_tiles(SIDE, tiles_ref, rows, before_ref, total)
    reduce_rows(total, image)
    values = [field[...] for field in fields]
    new = next_basis(step, image[...], values[-1], values[-2], aux_ref[0:8], aux_ref[8:16])
    next_ref[...] = new
    if last:
        gram_ref[...] = gram_row(values + [new])


def run_apply_same(tiles, halo):
    return pl.pallas_call(
        apply_same_kernel,
        out_shape=SHAPE((128, 8, 128)),
        in_specs=[VMEM] * 2,
        out_specs=VMEM,
        scratch_shapes=[pltpu.VMEM((32, 8, 128), jnp.float32)],
        compiler_params=PARAMS,
        cost_estimate=cost(4 * 36 * 16384),
        name="apply_same",
    )(tiles, halo)


def run_apply_side(step, last, tiles, lower, upper, before, aux, fields):
    outs = (SHAPE((8, 128)), SHAPE((1, 128))) if last else (SHAPE((8, 128)),)
    return pl.pallas_call(
        functools.partial(apply_side_kernel, step, last),
        out_shape=outs,
        in_specs=[VMEM] * (5 + len(fields)),
        out_specs=tuple(VMEM for _ in outs),
        scratch_shapes=[
            pltpu.VMEM((64, 8, 128), jnp.float32),
            pltpu.VMEM((128, 8, 128), jnp.float32),
            pltpu.VMEM((8, 128), jnp.float32),
        ],
        compiler_params=PARAMS,
        cost_estimate=cost(4 * 72 * 16384),
        name=f"apply_side{step}",
    )(tiles, lower, upper, before, aux, *fields)


def combine(coefs, fields):
    value = coefs[0] * fields[0]
    for coef, field in zip(coefs[1:], fields[1:]):
        value = value + coef * field
    return value


def finish_kernel(gram_ref, w0, w1, w2, w3, w4, charges_ref, residual_ref):
    fields = [ref[...] for ref in (w0, w1, w2, w3, w4)]
    summed = spread(jnp.sum(gram_ref[...], axis=0, keepdims=True))
    lane = lax.broadcasted_iota(jnp.int32, (8, 128), 1)
    system = lax.broadcasted_iota(jnp.int32, (8, 128), 0) // 4

    def entry(number):
        picked = jnp.where(lane == 2 * number + system, summed, 0.0)
        return jnp.broadcast_to(jnp.sum(picked, axis=1, keepdims=True), (8, 128))

    gram = {}
    for number, (i, j) in enumerate(PAIRS):
        gram[i, j] = gram[j, i] = entry(number)
    totals = [entry(len(PAIRS) + number) for number in range(4)]

    def dot(left, right):
        result = None
        for i, a in enumerate(left):
            part = None
            for j, b in enumerate(right):
                term = gram[i, j] * b
                part = term if part is None else part + term
            result = a * part if result is None else result + a * part
        return result

    def multiply(vector):
        size = len(vector)
        out = []
        for row in range(size + 1):
            value = None
            if row >= 1:
                value = SCALE[row - 1] * vector[row - 1]
            if row < size:
                term = SHIFT[row] * vector[row]
                value = term if value is None else value + term
            if row + 1 < size:
                value = value + SCALE[row + 1] * BACK[row + 1] * vector[row + 1]
            out.append(value)
        return out

    one = jnp.ones((8, 128), jnp.float32)
    residual = [one]
    direction = [one]
    answer = []
    norm_now = gram[0, 0]
    for step in range(4):
        image = multiply(direction)
        alpha = norm_now / dot(direction, image)
        answer = [
            alpha * d if k >= len(answer) else answer[k] + alpha * d for k, d in enumerate(direction)
        ]
        residual = [
            residual[k] - alpha * value if k < len(residual) else -alpha * value
            for k, value in enumerate(image)
        ]
        if step == 3:
            break
        norm_next = dot(residual, residual)
        ratio = norm_next / norm_now
        direction = [
            value + ratio * direction[k] if k < len(direction) else value
            for k, value in enumerate(residual)
        ]
        norm_now = norm_next
    value = combine(residual, fields)
    solution = combine(answer, fields[:4])
    total = combine(answer, totals)
    charges = solution[0:4] - total[0:4] / total[4:8] * solution[4:8]
    for y in range(2):
        charges_ref[0, y] = charges[2 * y : 2 * y + 2]
        for system in range(2):
            row = system * 4 + 2 * y
            residual_ref[system, 0, y] = value[row : row + 2]


def run_finish(gathered, fields):
    shape = functools.partial(jax.ShapeDtypeStruct, dtype=jnp.float32)
    return pl.pallas_call(
        finish_kernel,
        out_shape=(shape((1, 2, 2, 128)), shape((2, 1, 2, 2, 128))),
        in_specs=[VMEM] * 6,
        out_specs=(VMEM, VMEM),
        compiler_params=PARAMS,
        name="finish",
    )(gathered, *fields)


def shifted(value, axis, steps):
    count = lax.axis_size(axis)
    pairs = [(source, (source + steps) % count) for source in range(count)]
    return lax.ppermute(value, axis, pairs)


def spread_all(value, axes, count):
    sent = jnp.broadcast_to(value[None], (count,) + value.shape)
    return lax.all_to_all(sent, axes, 0, 0)


def wrapped(axis):
    here, count = lax.axis_index(axis), lax.axis_size(axis)
    below = jnp.where(here == 0, count - 1, here - 1)
    above = jnp.where(here == count - 1, 0, here + 1)
    return [value.astype(jnp.uint32) for value in (below, here, above)]


def around(every, places, cells):
    def part(place):
        start = [place] + [jnp.uint32(0)] * (every.ndim - 1)
        return lax.dynamic_slice(every, start, (1,) + every.shape[1:])[0]

    below, here, above = [part(place) for place in places]
    cells = cells - 1
    below = lax.slice_in_dim(below, 1, 2, axis=cells)
    above = lax.slice_in_dim(above, 0, 1, axis=cells)
    return jnp.concatenate([below, here, above], axis=cells)


def exchange(sent, dim, places):
    every = lax.all_to_all(sent, ("gy", "gz"), 0, 0)
    every = every.reshape((lax.axis_size("gy"), lax.axis_size("gz")) + sent.shape[1:])
    block = around(every, places[0:3], 2 + dim)
    block = around(block, places[3:6], 2 + dim)
    return block, shifted(block, "gx", 1), shifted(block, "gx", -1)


def exchange_cells(value, places):
    below = shifted(value[1:2], "gy", 1)
    above = shifted(value[0:1], "gy", -1)
    value = jnp.concatenate([below, value, above], axis=0)
    block = around(spread_all(value, "gz", lax.axis_size("gz")), places[3:6], 2)
    return block, shifted(block, "gx", 1), shifted(block, "gx", -1)


def shards(frac_positions, shielding, hardness, electroneg, counts, neighbor_list):
    count_x, count_y, count_z = [lax.axis_size(axis) for axis in ("gx", "gy", "gz")]
    places = frac_positions.transpose(0, 1, 3, 2, 4)
    count = count_y * count_z
    indices = lax.optimization_barrier(wrapped("gy") + wrapped("gz"))
    order = sum(indices[1:], indices[0]).astype(jnp.int32).reshape(1)
    packed = run_pack(order, places, shielding, hardness, electroneg, counts, neighbor_list)
    layers = exchange_cells(packed.reshape(2, 2, 8, 128), indices)
    own, lower, upper = [layer.reshape(16, 8, 128) for layer in layers]
    tiles_same, cols, total, w0, aux = run_same(own)
    tiles_side, w1 = run_side(own, lower, upper, cols, total, w0, aux)
    fields = [w0, w1]
    for step in (1, 2, 3):
        sent = jnp.broadcast_to(fields[-1].reshape(1, 2, 2, 2, 128), (count, 2, 2, 2, 128))
        layers = exchange(sent, 1, indices)
        own, lower, upper = [layer.reshape(32, 128) for layer in layers]
        total = run_apply_same(tiles_same, own)
        outs = run_apply_side(step, step == 3, tiles_side, lower, upper, total, aux, fields)
        fields.append(outs[0])
    gram = outs[1]
    gram = jnp.sum(spread_all(gram, ("gy", "gz"), count_y * count_z), axis=0)
    gram = spread_all(gram, "gx", count_x)
    return run_finish(gram.reshape(count_x, 128), fields)


def solution(mesh):
    placed = (
        P("gx", "gy", "gz", None, None),
        P("gx", "gy", "gz", None),
        P("gx", "gy", "gz", None),
        P("gx", "gy", "gz", None),
        P("gx", "gy", "gz"),
        P("gx", "gy", "gz", None),
    )
    return jax.shard_map(
        shards,
        mesh=mesh,
        in_specs=placed,
        out_specs=(P("gx", "gy", "gz", None), P(None, "gx", "gy", "gz", None)),
        check_vma=False,
    )
```

```python
import functools

import jax
import jax.numpy as jnp
from jax import lax
from jax.experimental import pallas as pl
from jax.experimental.pallas import tpu as pltpu
from jax.sharding import PartitionSpec as P

CODES = {
    (0, 0, 1): 0,
    (0, 1, -1): 1,
    (0, 1, 0): 2,
    (0, 1, 1): 3,
    (1, -1, -1): 4,
    (1, -1, 0): 5,
    (1, -1, 1): 6,
    (1, 0, -1): 7,
    (1, 0, 0): 8,
    (1, 0, 1): 9,
    (1, 1, -1): 10,
    (1, 1, 0): 11,
    (1, 1, 1): 12,
}
SHELL = [(x, y, z) for x in (-1, 0, 1) for y in (-1, 0, 1) for z in (-1, 0, 1)]

SHIFT = (220.0, 110.0, 145.0, 140.0)
SCALE = (60.0, 70.0, 70.0, 70.0)
BACK = (0.0, 0.7, 1.0, 1.0)
PAIRS = [(i, j) for i in range(4) for j in range(i, 5)]
VMEM = pl.BlockSpec(memory_space=pltpu.VMEM)
SMEM = pl.BlockSpec(memory_space=pltpu.SMEM)
PARAMS = pltpu.CompilerParams(vmem_limit_bytes=24 * 1024 * 1024)


OWN = [(1 + y) * 4 + 1 + z for y in range(2) for z in range(2)]
SAME = [offset for offset in SHELL if offset[0] == 0]
SIDE = [offset for offset in SHELL if offset[0] != 0]


def spread(row):
    return jnp.broadcast_to(row, (8, 128))


def reduce_rows(total_ref, image_ref):
    for field in range(8):
        block = total_ref[field * 16 : (field + 1) * 16].reshape(128, 128)
        image_ref[field : field + 1, :] = jnp.sum(block.T, axis=0, keepdims=True)


def next_basis(step, image, field, before, mask, hard):
    value = jnp.where(mask > 0.0, image, 0.0) + hard * field
    value = (value - SHIFT[step] * field) * (1.0 / SCALE[step])
    if BACK[step]:
        value = value - BACK[step] * before
    return value


def pack_kernel(order_ref, *refs):
    sources, packed_ref, inputs, semaphores = refs[:6], refs[6], refs[7:13], refs[13]
    copies = [
        pltpu.make_async_copy(source, target, semaphores.at[number])
        for number, (source, target) in enumerate(zip(sources, inputs))
    ]
    for copy in copies:
        copy.start()
    for copy in copies:
        copy.wait()
    place_ref, shield_ref, hard_ref, electro_ref, count_ref, list_ref = inputs
    lane = lax.broadcasted_iota(jnp.int32, (1, 128), 1)
    for y in range(2):
        for z in range(2):
            cell = 2 * y + z
            count = jnp.broadcast_to(count_ref[0, y : y + 1, z : z + 1], (1, 128))
            mask = jnp.where(lane < count, 1.0, 0.0)
            flags = jnp.zeros((1, 128), jnp.float32)
            for number in range(13):
                code = jnp.broadcast_to(list_ref[0, y, z : z + 1, number : number + 1], (1, 128))
                flags = jnp.where(lane == code, 1.0, flags)
            rows = []
            for number in range(3):
                rows.append(place_ref[0, y, number, z : z + 1])
            shield = shield_ref[0, y, z : z + 1]
            rows.append(jnp.exp(-1.5 * jnp.log(shield)) * (1000.0**-0.5))
            rows.append(-electro_ref[0, y, z : z + 1] * mask)
            rows.append(-mask)
            rows.append(flags)
            rows.append(hard_ref[0, y, z : z + 1])
            block = jnp.concatenate(rows, axis=0)
            packed_ref[cell] = block


def run_pack(order, *inputs):
    return pl.pallas_call(
        pack_kernel,
        out_shape=pltpu.VMEM((4, 8, 128), jnp.float32),
        in_specs=[SMEM] + [pl.BlockSpec(memory_space=pltpu.HBM)] * 6,
        out_specs=VMEM,
        scratch_shapes=[pltpu.VMEM(value.shape, value.dtype) for value in inputs]
        + [pltpu.SemaphoreType.DMA((6,))],
        compiler_params=pltpu.CompilerParams(vmem_limit_bytes=60 * 1024 * 1024),
        name="pack",
    )(order, *inputs)


def fill_rows(packed_ref, rows, first, layer):
    for y in range(4):
        for z in range(4):
            cell = y * 4 + z
            block = packed_ref[cell]
            for number, shift in enumerate((float(layer), y - 1.0, z - 1.0)):
                rows[first + cell, number] = spread(block[number : number + 1] + shift)
            for number in range(3, 6):
                rows[first + cell, number] = spread(block[number : number + 1])


def neighbor(offset):
    layer = 1 if offset[0] == 1 else 0
    return layer * 16 + (1 + offset[1]) * 4 + 1 + offset[2]


def fill_away(offsets, own_ref, lower_ref, rows, away):
    for own, cell in enumerate(OWN):
        y, z = own // 2, own % 2
        for number, offset in enumerate(offsets):
            place = neighbor(offset) + y * 4 + z
            row = rows[place, 0] + (1.0 + rows[place, 5]) * 100.0
            if offset in CODES:
                flag = own_ref[cell, 6:7, CODES[offset] : CODES[offset] + 1]
            elif offset == (0, 0, 0):
                flag = None
            else:
                code = CODES[tuple(-value for value in offset)]
                flag = lower_ref[cell + offset[1] * 4 + offset[2], 6:7, code : code + 1]
            if flag is not None:
                row = row + jnp.broadcast_to((1.0 - flag) * 100.0, (8, 128))
            away[own * len(offsets) + number] = row


def build_tiles(offsets, own_ref, rows, cols, away, tiles_ref, before, total):
    sub = lax.broadcasted_iota(jnp.int32, (8, 128), 0)
    lane = lax.broadcasted_iota(jnp.int32, (8, 128), 1)
    size = len(offsets)

    def body(own, base, chunk):
        xi, yi, zi, si = [cols[(own * 4 + number) * 16 + chunk] for number in range(4)]
        if before is None:
            sums = [jnp.zeros((8, 128), jnp.float32) for _ in range(2)]
        else:
            sums = [before[(system * 4 + own) * 16 + chunk] for system in range(2)]
        for number, offset in enumerate(offsets):
            cell = base + neighbor(offset)
            dx = away[own * size + number] - xi
            dy = rows[cell, 1] - yi
            dz = rows[cell, 2] - zi
            square = jnp.maximum(dx * dx + dy * dy + dz * dz, 1e-30)
            ratio = square * lax.rsqrt(square)
            fourth = square * square
            taper = 1.44 + fourth * (-50.4 + ratio * (120.96 + ratio * (-100.8 + 28.8 * ratio)))
            cube = square * ratio + rows[cell, 3] * si
            value = taper * jnp.exp2(jnp.log(cube) * (-1.0 / (3.0 * 0.6931471805599453)))
            keep = square < 1.0
            if offset == (0, 0, 0):
                keep = keep & (sub + chunk * 8 != lane)
            value = jnp.where(keep, value, 0.0)
            tiles_ref[(own * size + number) * 16 + chunk] = value
            sums[0] = sums[0] + value * rows[cell, 4]
            sums[1] = sums[1] - value
        for system in range(2):
            total[(system * 4 + own) * 16 + chunk] = sums[system]

    for own in range(4):
        base = (own // 2) * 4 + own % 2

        def step(index, carry, own=own, base=base):
            for part in range(2):
                body(own, base, index * 2 + part)
            return carry

        count = jnp.sum(-own_ref[OWN[own], 5:6]).astype(jnp.int32)
        lax.fori_loop(0, lax.shift_right_logical(count + 15, 4), step, 0)


def same_kernel(own_ref, tiles_ref, cols_ref, total_ref, field_ref, aux_ref, rows, away):
    fill_rows(own_ref, rows, 0, 0)
    for own, cell in enumerate(OWN):
        for number in range(4):
            column = jnp.broadcast_to(rows[cell, number, 0:1, :], (128, 128)).T
            start = (own * 4 + number) * 16
            cols_ref[start : start + 16] = column.reshape(16, 8, 128)
        for system in range(2):
            row = system * 4 + own
            mask = -own_ref[cell, 5:6]
            field_ref[row : row + 1] = own_ref[cell, 4 + system : 5 + system]
            aux_ref[row : row + 1] = mask
            aux_ref[8 + row : 9 + row] = own_ref[cell, 7:8] * mask
    fill_away(SAME, own_ref, own_ref, rows, away)
    build_tiles(SAME, own_ref, rows, cols_ref, away, tiles_ref, None, total_ref)


def side_kernel(own_ref, lower_ref, upper_ref, cols_ref, before_ref, field_ref, aux_ref, tiles_ref, next_ref, rows, away, total, image):
    fill_rows(lower_ref, rows, 0, -1)
    fill_rows(upper_ref, rows, 16, 1)
    fill_away(SIDE, own_ref, lower_ref, rows, away)
    build_tiles(SIDE, own_ref, rows, cols_ref, away, tiles_ref, before_ref, total)
    reduce_rows(total, image)
    next_ref[...] = next_basis(0, image[...], field_ref[...], None, aux_ref[0:8], aux_ref[8:16])


SHAPE = functools.partial(jax.ShapeDtypeStruct, dtype=jnp.float32)


def cost(flops):
    return pl.CostEstimate(flops=flops, bytes_accessed=4 * 1024 * 1024, transcendentals=0)


def run_same(own):
    return pl.pallas_call(
        same_kernel,
        out_shape=(
            SHAPE((36 * 16, 8, 128)),
            SHAPE((256, 8, 128)),
            SHAPE((128, 8, 128)),
            SHAPE((8, 128)),
            SHAPE((16, 128)),
        ),
        in_specs=[VMEM],
        out_specs=(VMEM,) * 5,
        scratch_shapes=[
            pltpu.VMEM((16, 6, 8, 128), jnp.float32),
            pltpu.VMEM((36, 8, 128), jnp.float32),
        ],
        compiler_params=PARAMS,
        cost_estimate=cost(40 * 36 * 16384),
        name="tiles_same",
    )(own)


def run_side(*inputs):
    return pl.pallas_call(
        side_kernel,
        out_shape=(SHAPE((72 * 16, 8, 128)), SHAPE((8, 128))),
        in_specs=[VMEM] * 7,
        out_specs=(VMEM,) * 2,
        scratch_shapes=[
            pltpu.VMEM((32, 6, 8, 128), jnp.float32),
            pltpu.VMEM((72, 8, 128), jnp.float32),
            pltpu.VMEM((128, 8, 128), jnp.float32),
            pltpu.VMEM((8, 128), jnp.float32),
        ],
        compiler_params=PARAMS,
        cost_estimate=cost(40 * 72 * 16384),
        name="tiles_side",
    )(*inputs)


def gram_row(fields):
    entries = [fields[i] * fields[j] for i, j in PAIRS] + fields[:4]
    lane = lax.broadcasted_iota(jnp.int32, (1, 128), 1)
    row = jnp.zeros((1, 128), jnp.float32)
    for number, entry in enumerate(entries):
        for system in range(2):
            part = jnp.sum(entry[system * 4 : system * 4 + 4], axis=0, keepdims=True)
            part = jnp.sum(part, axis=1, keepdims=True)
            row = row + jnp.where(lane == 2 * number + system, part, 0.0)
    return row


def fill_fields(halo_ref, rows, first):
    for system in range(2):
        for cell in range(16):
            row = system * 16 + cell
            rows[(first + cell) * 2 + system] = spread(halo_ref[row : row + 1])


def apply_tiles(offsets, tiles_ref, rows, before, total):
    size = len(offsets)

    for own in range(4):
        base = (own // 2) * 4 + own % 2
        for group in range(4):
            places = [[(system * 4 + own) * 16 + group * 4 + part for part in range(4)] for system in range(2)]
            if before is None:
                sums = [[None] * 4 for _ in range(2)]
            else:
                sums = [[before[place] for place in line] for line in places]
            for number, offset in enumerate(offsets):
                cell = base + neighbor(offset)
                right = [rows[cell * 2 + system] for system in range(2)]
                for part in range(4):
                    tile = tiles_ref[(own * size + number) * 16 + group * 4 + part]
                    for system in range(2):
                        term = tile * right[system]
                        held = sums[system][part]
                        sums[system][part] = term if held is None else held + term
            for system in range(2):
                for part in range(4):
                    total[places[system][part]] = sums[system][part]


def apply_same_kernel(tiles_ref, halo_ref, total_ref, rows):
    fill_fields(halo_ref, rows, 0)
    apply_tiles(SAME, tiles_ref, rows, None, total_ref)


def apply_side_kernel(step, last, tiles_ref, lower_ref, upper_ref, before_ref, aux_ref, *refs):
    count = step + 1
    fields, next_ref, rest = refs[:count], refs[count], refs[count + 1 :]
    if last:
        gram_ref, rest = rest[0], rest[1:]
    rows, total, image = rest
    fill_fields(lower_ref, rows, 0)
    fill_fields(upper_ref, rows, 16)
    apply_tiles(SIDE, tiles_ref, rows, before_ref, total)
    reduce_rows(total, image)
    values = [field[...] for field in fields]
    new = next_basis(step, image[...], values[-1], values[-2], aux_ref[0:8], aux_ref[8:16])
    next_ref[...] = new
    if last:
        gram_ref[...] = gram_row(values + [new])


def run_apply_same(tiles, halo):
    return pl.pallas_call(
        apply_same_kernel,
        out_shape=SHAPE((128, 8, 128)),
        in_specs=[VMEM] * 2,
        out_specs=VMEM,
        scratch_shapes=[pltpu.VMEM((32, 8, 128), jnp.float32)],
        compiler_params=PARAMS,
        cost_estimate=cost(4 * 36 * 16384),
        name="apply_same",
    )(tiles, halo)


def run_apply_side(step, last, tiles, lower, upper, before, aux, fields):
    outs = (SHAPE((8, 128)), SHAPE((1, 128))) if last else (SHAPE((8, 128)),)
    return pl.pallas_call(
        functools.partial(apply_side_kernel, step, last),
        out_shape=outs,
        in_specs=[VMEM] * (5 + len(fields)),
        out_specs=tuple(VMEM for _ in outs),
        scratch_shapes=[
            pltpu.VMEM((64, 8, 128), jnp.float32),
            pltpu.VMEM((128, 8, 128), jnp.float32),
            pltpu.VMEM((8, 128), jnp.float32),
        ],
        compiler_params=PARAMS,
        cost_estimate=cost(4 * 72 * 16384),
        name=f"apply_side{step}",
    )(tiles, lower, upper, before, aux, *fields)


def combine(coefs, fields):
    value = coefs[0] * fields[0]
    for coef, field in zip(coefs[1:], fields[1:]):
        value = value + coef * field
    return value


def finish_kernel(gram_ref, w0, w1, w2, w3, w4, charges_ref, residual_ref):
    fields = [ref[...] for ref in (w0, w1, w2, w3, w4)]
    summed = spread(jnp.sum(gram_ref[...], axis=0, keepdims=True))
    lane = lax.broadcasted_iota(jnp.int32, (8, 128), 1)
    system = lax.broadcasted_iota(jnp.int32, (8, 128), 0) // 4

    def entry(number):
        picked = jnp.where(lane == 2 * number + system, summed, 0.0)
        return jnp.broadcast_to(jnp.sum(picked, axis=1, keepdims=True), (8, 128))

    gram = {}
    for number, (i, j) in enumerate(PAIRS):
        gram[i, j] = gram[j, i] = entry(number)
    totals = [entry(len(PAIRS) + number) for number in range(4)]

    def dot(left, right):
        result = None
        for i, a in enumerate(left):
            part = None
            for j, b in enumerate(right):
                term = gram[i, j] * b
                part = term if part is None else part + term
            result = a * part if result is None else result + a * part
        return result

    def multiply(vector):
        size = len(vector)
        out = []
        for row in range(size + 1):
            value = None
            if row >= 1:
                value = SCALE[row - 1] * vector[row - 1]
            if row < size:
                term = SHIFT[row] * vector[row]
                value = term if value is None else value + term
            if row + 1 < size:
                value = value + SCALE[row + 1] * BACK[row + 1] * vector[row + 1]
            out.append(value)
        return out

    one = jnp.ones((8, 128), jnp.float32)
    residual = [one]
    direction = [one]
    answer = []
    norm_now = gram[0, 0]
    for step in range(4):
        image = multiply(direction)
        alpha = norm_now / dot(direction, image)
        answer = [
            alpha * d if k >= len(answer) else answer[k] + alpha * d for k, d in enumerate(direction)
        ]
        residual = [
            residual[k] - alpha * value if k < len(residual) else -alpha * value
            for k, value in enumerate(image)
        ]
        if step == 3:
            break
        norm_next = dot(residual, residual)
        ratio = norm_next / norm_now
        direction = [
            value + ratio * direction[k] if k < len(direction) else value
            for k, value in enumerate(residual)
        ]
        norm_now = norm_next
    value = combine(residual, fields)
    solution = combine(answer, fields[:4])
    total = combine(answer, totals)
    charges = solution[0:4] - total[0:4] / total[4:8] * solution[4:8]
    for y in range(2):
        charges_ref[0, y] = charges[2 * y : 2 * y + 2]
        for system in range(2):
            row = system * 4 + 2 * y
            residual_ref[system, 0, y] = value[row : row + 2]


def run_finish(gathered, fields):
    shape = functools.partial(jax.ShapeDtypeStruct, dtype=jnp.float32)
    return pl.pallas_call(
        finish_kernel,
        out_shape=(shape((1, 2, 2, 128)), shape((2, 1, 2, 2, 128))),
        in_specs=[VMEM] * 6,
        out_specs=(VMEM, VMEM),
        compiler_params=PARAMS,
        name="finish",
    )(gathered, *fields)


def shifted(value, axis, steps):
    count = lax.axis_size(axis)
    pairs = [(source, (source + steps) % count) for source in range(count)]
    return lax.ppermute(value, axis, pairs)


def spread_all(value, axes, count):
    sent = jnp.broadcast_to(value[None], (count,) + value.shape)
    return lax.all_to_all(sent, axes, 0, 0)


def wrapped(axis):
    here, count = lax.axis_index(axis), lax.axis_size(axis)
    below = jnp.where(here == 0, count - 1, here - 1)
    above = jnp.where(here == count - 1, 0, here + 1)
    return [value.astype(jnp.uint32) for value in (below, here, above)]


def around(every, places, cells):
    def part(place):
        start = [place] + [jnp.uint32(0)] * (every.ndim - 1)
        return lax.dynamic_slice(every, start, (1,) + every.shape[1:])[0]

    below, here, above = [part(place) for place in places]
    cells = cells - 1
    below = lax.slice_in_dim(below, 1, 2, axis=cells)
    above = lax.slice_in_dim(above, 0, 1, axis=cells)
    return jnp.concatenate([below, here, above], axis=cells)


def exchange(sent, dim, places):
    every = lax.all_to_all(sent, ("gy", "gz"), 0, 0)
    every = every.reshape((lax.axis_size("gy"), lax.axis_size("gz")) + sent.shape[1:])
    block = around(every, places[0:3], 2 + dim)
    block = around(block, places[3:6], 2 + dim)
    return block, shifted(block, "gx", 1), shifted(block, "gx", -1)


def exchange_cells(value, places):
    below = shifted(value[1:2], "gy", 1)
    above = shifted(value[0:1], "gy", -1)
    value = jnp.concatenate([below, value, above], axis=0)
    block = around(spread_all(value, "gz", lax.axis_size("gz")), places[3:6], 2)
    return block, shifted(block, "gx", 1), shifted(block, "gx", -1)


def shards(frac_positions, shielding, hardness, electroneg, counts, neighbor_list):
    count_x, count_y, count_z = [lax.axis_size(axis) for axis in ("gx", "gy", "gz")]
    places = frac_positions.transpose(0, 1, 3, 2, 4)
    count = count_y * count_z
    indices = lax.optimization_barrier(wrapped("gy") + wrapped("gz"))
    order = sum(indices[1:], indices[0]).astype(jnp.int32).reshape(1)
    packed = run_pack(order, places, shielding, hardness, electroneg, counts, neighbor_list)
    layers = exchange_cells(packed.reshape(2, 2, 8, 128), indices)
    own, lower, upper = [layer.reshape(16, 8, 128) for layer in layers]
    tiles_same, cols, total, w0, aux = run_same(own)
    tiles_side, w1 = run_side(own, lower, upper, cols, total, w0, aux)
    fields = [w0, w1]
    for step in (1, 2, 3):
        sent = jnp.broadcast_to(fields[-1].reshape(1, 2, 2, 2, 128), (count, 2, 2, 2, 128))
        layers = exchange(sent, 1, indices)
        own, lower, upper = [layer.reshape(32, 128) for layer in layers]
        total = run_apply_same(tiles_same, own)
        outs = run_apply_side(step, step == 3, tiles_side, lower, upper, total, aux, fields)
        fields.append(outs[0])
    gram = outs[1]
    gram = jnp.sum(spread_all(gram, ("gy", "gz"), count_y * count_z), axis=0)
    gram = spread_all(gram, "gx", count_x)
    return run_finish(gram.reshape(count_x, 128), fields)


def solution(mesh):
    placed = (
        P("gx", "gy", "gz", None, None),
        P("gx", "gy", "gz", None),
        P("gx", "gy", "gz", None),
        P("gx", "gy", "gz", None),
        P("gx", "gy", "gz"),
        P("gx", "gy", "gz", None),
    )
    return jax.shard_map(
        shards,
        mesh=mesh,
        in_specs=placed,
        out_specs=(P("gx", "gy", "gz", None), P(None, "gx", "gy", "gz", None)),
        check_vma=False,
    )
```

```python
import functools

import jax
import jax.numpy as jnp
from jax import lax
from jax.experimental import pallas as pl
from jax.experimental.pallas import tpu as pltpu
from jax.sharding import PartitionSpec as P

CODES = {
    (0, 0, 1): 0,
    (0, 1, -1): 1,
    (0, 1, 0): 2,
    (0, 1, 1): 3,
    (1, -1, -1): 4,
    (1, -1, 0): 5,
    (1, -1, 1): 6,
    (1, 0, -1): 7,
    (1, 0, 0): 8,
    (1, 0, 1): 9,
    (1, 1, -1): 10,
    (1, 1, 0): 11,
    (1, 1, 1): 12,
}
SHELL = [(x, y, z) for x in (-1, 0, 1) for y in (-1, 0, 1) for z in (-1, 0, 1)]

SHIFT = (220.0, 110.0, 145.0, 140.0)
SCALE = (60.0, 70.0, 70.0, 70.0)
BACK = (0.0, 0.7, 1.0, 1.0)
PAIRS = [(i, j) for i in range(4) for j in range(i, 4)]
VMEM = pl.BlockSpec(memory_space=pltpu.VMEM)
SMEM = pl.BlockSpec(memory_space=pltpu.SMEM)
PARAMS = pltpu.CompilerParams(vmem_limit_bytes=24 * 1024 * 1024)


OWN = [(1 + y) * 4 + 1 + z for y in range(2) for z in range(2)]
SAME = [offset for offset in SHELL if offset[0] == 0]
SIDE = [offset for offset in SHELL if offset[0] != 0]
LOWER, UPPER = SIDE[:9], SIDE[9:]


def spread(row):
    return jnp.broadcast_to(row, (8, 128))


def reduce_rows(total_ref, image_ref):
    for field in range(8):
        block = total_ref[field * 16 : (field + 1) * 16].reshape(128, 128)
        image_ref[field : field + 1, :] = jnp.sum(block.T, axis=0, keepdims=True)


def next_basis(step, image, field, before, mask, hard):
    value = jnp.where(mask > 0.0, image, 0.0) + hard * field
    value = (value - SHIFT[step] * field) * (1.0 / SCALE[step])
    if BACK[step]:
        value = value - BACK[step] * before
    return value


def pack_kernel(order_ref, *refs):
    sources, packed_ref, inputs, semaphores = refs[:6], refs[6], refs[7:13], refs[13]
    copies = [
        pltpu.make_async_copy(source, target, semaphores.at[number])
        for number, (source, target) in enumerate(zip(sources, inputs))
    ]
    for copy in copies:
        copy.start()
    for copy in copies:
        copy.wait()
    place_ref, shield_ref, hard_ref, electro_ref, count_ref, list_ref = inputs
    lane = lax.broadcasted_iota(jnp.int32, (1, 128), 1)
    for y in range(2):
        for z in range(2):
            cell = 2 * y + z
            count = jnp.broadcast_to(count_ref[0, y : y + 1, z : z + 1], (1, 128))
            mask = jnp.where(lane < count, 1.0, 0.0)
            flags = jnp.zeros((1, 128), jnp.float32)
            for number in range(13):
                code = jnp.broadcast_to(list_ref[0, y, z : z + 1, number : number + 1], (1, 128))
                flags = jnp.where(lane == code, 1.0, flags)
            rows = []
            for number in range(3):
                rows.append(place_ref[0, y, number, z : z + 1])
            shield = shield_ref[0, y, z : z + 1]
            rows.append(jnp.exp(-1.5 * jnp.log(shield)) * (1000.0**-0.5))
            rows.append(-electro_ref[0, y, z : z + 1] * mask)
            rows.append(-mask)
            rows.append(flags)
            rows.append(hard_ref[0, y, z : z + 1])
            block = jnp.concatenate(rows, axis=0)
            packed_ref[cell] = block


def run_pack(order, *inputs):
    return pl.pallas_call(
        pack_kernel,
        out_shape=pltpu.VMEM((4, 8, 128), jnp.float32),
        in_specs=[SMEM] + [pl.BlockSpec(memory_space=pltpu.HBM)] * 6,
        out_specs=VMEM,
        scratch_shapes=[pltpu.VMEM(value.shape, value.dtype) for value in inputs]
        + [pltpu.SemaphoreType.DMA((6,))],
        compiler_params=pltpu.CompilerParams(vmem_limit_bytes=60 * 1024 * 1024),
        name="pack",
    )(order, *inputs)


def fill_rows(packed_ref, rows, first, layer):
    for y in range(4):
        for z in range(4):
            cell = y * 4 + z
            block = packed_ref[cell]
            for number, shift in enumerate((float(layer), y - 1.0, z - 1.0)):
                rows[first + cell, number] = spread(block[number : number + 1] + shift)
            for number in range(3, 6):
                rows[first + cell, number] = spread(block[number : number + 1])


def neighbor(offset):
    layer = 1 if offset[0] == 1 else 0
    return layer * 16 + (1 + offset[1]) * 4 + 1 + offset[2]


def fill_away(offsets, own_ref, lower_ref, rows, away):
    for own, cell in enumerate(OWN):
        y, z = own // 2, own % 2
        for number, offset in enumerate(offsets):
            place = neighbor(offset) + y * 4 + z
            row = rows[place, 0] + (1.0 + rows[place, 5]) * 100.0
            if offset in CODES:
                flag = own_ref[cell, 6:7, CODES[offset] : CODES[offset] + 1]
            elif offset == (0, 0, 0):
                flag = None
            else:
                code = CODES[tuple(-value for value in offset)]
                flag = lower_ref[cell + offset[1] * 4 + offset[2], 6:7, code : code + 1]
            if flag is not None:
                row = row + jnp.broadcast_to((1.0 - flag) * 100.0, (8, 128))
            away[own * len(offsets) + number] = row


def build_tiles(offsets, own_ref, rows, cols, away, tiles_ref, before, total):
    sub = lax.broadcasted_iota(jnp.int32, (8, 128), 0)
    lane = lax.broadcasted_iota(jnp.int32, (8, 128), 1)
    size = len(offsets)

    def body(own, base, chunk):
        xi, yi, zi, si = [cols[(own * 4 + number) * 16 + chunk] for number in range(4)]
        if before is None:
            sums = [jnp.zeros((8, 128), jnp.float32) for _ in range(2)]
        else:
            sums = [before[(system * 4 + own) * 16 + chunk] for system in range(2)]
        for number, offset in enumerate(offsets):
            cell = base + neighbor(offset)
            dx = away[own * size + number] - xi
            dy = rows[cell, 1] - yi
            dz = rows[cell, 2] - zi
            square = jnp.maximum(dx * dx + dy * dy + dz * dz, 1e-30)
            ratio = square * lax.rsqrt(square)
            fourth = square * square
            taper = 1.44 + fourth * (-50.4 + ratio * (120.96 + ratio * (-100.8 + 28.8 * ratio)))
            cube = square * ratio + rows[cell, 3] * si
            value = taper * jnp.exp2(jnp.log(cube) * (-1.0 / (3.0 * 0.6931471805599453)))
            keep = square < 1.0
            if offset == (0, 0, 0):
                keep = keep & (sub + chunk * 8 != lane)
            value = jnp.where(keep, value, 0.0)
            tiles_ref[(own * size + number) * 16 + chunk] = value
            sums[0] = sums[0] + value * rows[cell, 4]
            sums[1] = sums[1] - value
        for system in range(2):
            total[(system * 4 + own) * 16 + chunk] = sums[system]

    for own in range(4):
        base = (own // 2) * 4 + own % 2

        def step(index, carry, own=own, base=base):
            for part in range(2):
                body(own, base, index * 2 + part)
            return carry

        count = jnp.sum(-own_ref[OWN[own], 5:6]).astype(jnp.int32)
        lax.fori_loop(0, lax.shift_right_logical(count + 15, 4), step, 0)


def same_kernel(own_ref, tiles_ref, cols_ref, total_ref, field_ref, aux_ref, rows, away):
    fill_rows(own_ref, rows, 0, 0)
    for own, cell in enumerate(OWN):
        for number in range(4):
            column = jnp.broadcast_to(rows[cell, number, 0:1, :], (128, 128)).T
            start = (own * 4 + number) * 16
            cols_ref[start : start + 16] = column.reshape(16, 8, 128)
        for system in range(2):
            row = system * 4 + own
            mask = -own_ref[cell, 5:6]
            field_ref[row : row + 1] = own_ref[cell, 4 + system : 5 + system]
            aux_ref[row : row + 1] = mask
            aux_ref[8 + row : 9 + row] = own_ref[cell, 7:8] * mask
    fill_away(SAME, own_ref, own_ref, rows, away)
    build_tiles(SAME, own_ref, rows, cols_ref, away, tiles_ref, None, total_ref)


def side_kernel(own_ref, lower_ref, upper_ref, cols_ref, before_ref, field_ref, aux_ref, tiles_ref, next_ref, rows, away, total, image):
    fill_rows(lower_ref, rows, 0, -1)
    fill_rows(upper_ref, rows, 16, 1)
    fill_away(SIDE, own_ref, lower_ref, rows, away)
    build_tiles(SIDE, own_ref, rows, cols_ref, away, tiles_ref, before_ref, total)
    reduce_rows(total, image)
    next_ref[...] = next_basis(0, image[...], field_ref[...], None, aux_ref[0:8], aux_ref[8:16])


SHAPE = functools.partial(jax.ShapeDtypeStruct, dtype=jnp.float32)


def cost(flops):
    return pl.CostEstimate(flops=flops, bytes_accessed=4 * 1024 * 1024, transcendentals=0)


def run_same(own):
    return pl.pallas_call(
        same_kernel,
        out_shape=(
            SHAPE((36 * 16, 8, 128)),
            SHAPE((256, 8, 128)),
            SHAPE((128, 8, 128)),
            SHAPE((8, 128)),
            SHAPE((16, 128)),
        ),
        in_specs=[VMEM],
        out_specs=(VMEM,) * 5,
        scratch_shapes=[
            pltpu.VMEM((16, 6, 8, 128), jnp.float32),
            pltpu.VMEM((36, 8, 128), jnp.float32),
        ],
        compiler_params=PARAMS,
        cost_estimate=cost(40 * 36 * 16384),
        name="tiles_same",
    )(own)


def run_side(*inputs):
    return pl.pallas_call(
        side_kernel,
        out_shape=(SHAPE((72 * 16, 8, 128)), SHAPE((8, 128))),
        in_specs=[VMEM] * 7,
        out_specs=(VMEM,) * 2,
        scratch_shapes=[
            pltpu.VMEM((32, 6, 8, 128), jnp.float32),
            pltpu.VMEM((72, 8, 128), jnp.float32),
            pltpu.VMEM((128, 8, 128), jnp.float32),
            pltpu.VMEM((8, 128), jnp.float32),
        ],
        compiler_params=PARAMS,
        cost_estimate=cost(40 * 72 * 16384),
        name="tiles_side",
    )(*inputs)


def gram_row(fields, image):
    entries = [fields[i] * fields[j] for i, j in PAIRS] + [fields[3] * image] + fields
    lane = lax.broadcasted_iota(jnp.int32, (1, 128), 1)
    row = jnp.zeros((1, 128), jnp.float32)
    for number, entry in enumerate(entries):
        for system in range(2):
            part = jnp.sum(entry[system * 4 : system * 4 + 4], axis=0, keepdims=True)
            part = jnp.sum(part, axis=1, keepdims=True)
            row = row + jnp.where(lane == 2 * number + system, part, 0.0)
    return row


def fill_fields(halo_ref, rows, first):
    for system in range(2):
        for cell in range(16):
            row = system * 16 + cell
            rows[(first + cell) * 2 + system] = spread(halo_ref[row : row + 1])


def apply_tiles(offsets, size, first, tiles_ref, rows, before, total):

    for own in range(4):
        base = (own // 2) * 4 + own % 2
        for group in range(4):
            places = [[(system * 4 + own) * 16 + group * 4 + part for part in range(4)] for system in range(2)]
            if before is None:
                sums = [[None] * 4 for _ in range(2)]
            else:
                sums = [[before[place] for place in line] for line in places]
            for number, offset in enumerate(offsets):
                cell = base + neighbor(offset)
                right = [rows[cell * 2 + system] for system in range(2)]
                for part in range(4):
                    tile = tiles_ref[(own * size + first + number) * 16 + group * 4 + part]
                    for system in range(2):
                        term = tile * right[system]
                        held = sums[system][part]
                        sums[system][part] = term if held is None else held + term
            for system in range(2):
                for part in range(4):
                    total[places[system][part]] = sums[system][part]


def apply_same_kernel(tiles_ref, halo_ref, total_ref, rows):
    fill_fields(halo_ref, rows, 0)
    apply_tiles(SAME, 9, 0, tiles_ref, rows, None, total_ref)


def apply_side_kernel(step, tiles_ref, lower_ref, upper_ref, before_ref, aux_ref, *refs):
    fields, (next_ref, rows, total, image) = refs[: step + 1], refs[step + 1 :]
    fill_fields(lower_ref, rows, 0)
    fill_fields(upper_ref, rows, 16)
    apply_tiles(SIDE, 18, 0, tiles_ref, rows, before_ref, total)
    reduce_rows(total, image)
    before, field = fields[step - 1][...], fields[step][...]
    next_ref[...] = next_basis(step, image[...], field, before, aux_ref[0:8], aux_ref[8:16])


def apply_upper_kernel(tiles_ref, upper_ref, before_ref, aux_ref, *refs):
    fields, (total_ref, gram_ref, rows, total, image) = [ref[...] for ref in refs[:4]], refs[4:]
    fill_fields(upper_ref, rows, 16)
    apply_tiles(UPPER, 18, 9, tiles_ref, rows, None, total)
    part = total[...]
    both = before_ref[...] + part
    total_ref[...] = both
    total[...] = both + part
    reduce_rows(total, image)
    value = jnp.where(aux_ref[0:8] > 0.0, image[...], 0.0) + aux_ref[8:16] * fields[3]
    gram_ref[...] = gram_row(fields, value)


def run_apply_same(tiles, halo):
    return pl.pallas_call(
        apply_same_kernel,
        out_shape=SHAPE((128, 8, 128)),
        in_specs=[VMEM] * 2,
        out_specs=VMEM,
        scratch_shapes=[pltpu.VMEM((32, 8, 128), jnp.float32)],
        compiler_params=PARAMS,
        cost_estimate=cost(4 * 36 * 16384),
        name="apply_same",
    )(tiles, halo)


SCRATCH = [
    pltpu.VMEM((64, 8, 128), jnp.float32),
    pltpu.VMEM((128, 8, 128), jnp.float32),
    pltpu.VMEM((8, 128), jnp.float32),
]


def run_apply_side(step, tiles, lower, upper, before, aux, fields):
    return pl.pallas_call(
        functools.partial(apply_side_kernel, step),
        out_shape=SHAPE((8, 128)),
        in_specs=[VMEM] * (5 + len(fields)),
        out_specs=VMEM,
        scratch_shapes=SCRATCH,
        compiler_params=PARAMS,
        cost_estimate=cost(4 * 72 * 16384),
        name=f"apply_side{step}",
    )(tiles, lower, upper, before, aux, *fields)


def run_apply_upper(tiles, upper, before, aux, fields):
    return pl.pallas_call(
        apply_upper_kernel,
        out_shape=(SHAPE((128, 8, 128)), SHAPE((1, 128))),
        in_specs=[VMEM] * (4 + len(fields)),
        out_specs=(VMEM, VMEM),
        scratch_shapes=SCRATCH,
        compiler_params=PARAMS,
        cost_estimate=cost(4 * 36 * 16384),
        name="apply_upper",
    )(tiles, upper, before, aux, *fields)


def combine(coefs, fields):
    value = coefs[0] * fields[0]
    for coef, field in zip(coefs[1:], fields[1:]):
        value = value + coef * field
    return value


def finish_kernel(gram_ref, tiles_ref, lower_ref, before_ref, aux_ref, *refs):
    fields, (charges_ref, residual_ref, rows, sums, last) = [ref[...] for ref in refs[:4]], refs[4:]
    fill_fields(lower_ref, rows, 0)
    apply_tiles(LOWER, 18, 0, tiles_ref, rows, before_ref, sums)
    reduce_rows(sums, last)
    fields.append(next_basis(3, last[...], fields[3], fields[2], aux_ref[0:8], aux_ref[8:16]))
    summed = spread(jnp.sum(gram_ref[...], axis=0, keepdims=True))
    lane = lax.broadcasted_iota(jnp.int32, (8, 128), 1)
    system = lax.broadcasted_iota(jnp.int32, (8, 128), 0) // 4

    def entry(number):
        picked = jnp.where(lane == 2 * number + system, summed, 0.0)
        return jnp.broadcast_to(jnp.sum(picked, axis=1, keepdims=True), (8, 128))

    gram = {}
    for number, (i, j) in enumerate(PAIRS):
        gram[i, j] = gram[j, i] = entry(number)
    totals = [entry(len(PAIRS) + 1 + number) for number in range(4)]
    for i in range(4):
        if i == 3:
            value = entry(len(PAIRS))
        else:
            value = SCALE[i] * gram[i + 1, 3] + SHIFT[i] * gram[i, 3]
            if BACK[i]:
                value = value + SCALE[i] * BACK[i] * gram[i - 1, 3]
        value = (value - SHIFT[3] * gram[i, 3]) * (1.0 / SCALE[3]) - BACK[3] * gram[i, 2]
        gram[i, 4] = gram[4, i] = value

    def dot(left, right):
        result = None
        for i, a in enumerate(left):
            part = None
            for j, b in enumerate(right):
                term = gram[i, j] * b
                part = term if part is None else part + term
            result = a * part if result is None else result + a * part
        return result

    def multiply(vector):
        size = len(vector)
        out = []
        for row in range(size + 1):
            value = None
            if row >= 1:
                value = SCALE[row - 1] * vector[row - 1]
            if row < size:
                term = SHIFT[row] * vector[row]
                value = term if value is None else value + term
            if row + 1 < size:
                value = value + SCALE[row + 1] * BACK[row + 1] * vector[row + 1]
            out.append(value)
        return out

    one = jnp.ones((8, 128), jnp.float32)
    residual = [one]
    direction = [one]
    answer = []
    norm_now = gram[0, 0]
    for step in range(4):
        image = multiply(direction)
        alpha = norm_now / dot(direction, image)
        answer = [
            alpha * d if k >= len(answer) else answer[k] + alpha * d for k, d in enumerate(direction)
        ]
        residual = [
            residual[k] - alpha * value if k < len(residual) else -alpha * value
            for k, value in enumerate(image)
        ]
        if step == 3:
            break
        norm_next = dot(residual, residual)
        ratio = norm_next / norm_now
        direction = [
            value + ratio * direction[k] if k < len(direction) else value
            for k, value in enumerate(residual)
        ]
        norm_now = norm_next
    value = combine(residual, fields)
    solution = combine(answer, fields[:4])
    total = combine(answer, totals)
    charges = solution[0:4] - total[0:4] / total[4:8] * solution[4:8]
    for y in range(2):
        charges_ref[0, y] = charges[2 * y : 2 * y + 2]
        for system in range(2):
            row = system * 4 + 2 * y
            residual_ref[system, 0, y] = value[row : row + 2]


def run_finish(gram, tiles, lower, before, aux, fields):
    return pl.pallas_call(
        finish_kernel,
        out_shape=(SHAPE((1, 2, 2, 128)), SHAPE((2, 1, 2, 2, 128))),
        in_specs=[VMEM] * 9,
        out_specs=(VMEM, VMEM),
        scratch_shapes=SCRATCH,
        compiler_params=PARAMS,
        name="finish",
    )(gram, tiles, lower, before, aux, *fields)


def shifted(value, axis, steps):
    count = lax.axis_size(axis)
    pairs = [(source, (source + steps) % count) for source in range(count)]
    return lax.ppermute(value, axis, pairs)


def spread_all(value, axes, count):
    sent = jnp.broadcast_to(value[None], (count,) + value.shape)
    return lax.all_to_all(sent, axes, 0, 0)


def wrapped(axis):
    here, count = lax.axis_index(axis), lax.axis_size(axis)
    below = jnp.where(here == 0, count - 1, here - 1)
    above = jnp.where(here == count - 1, 0, here + 1)
    return [value.astype(jnp.uint32) for value in (below, here, above)]


def around(every, places, cells):
    def part(place):
        start = [place] + [jnp.uint32(0)] * (every.ndim - 1)
        return lax.dynamic_slice(every, start, (1,) + every.shape[1:])[0]

    below, here, above = [part(place) for place in places]
    cells = cells - 1
    below = lax.slice_in_dim(below, 1, 2, axis=cells)
    above = lax.slice_in_dim(above, 0, 1, axis=cells)
    return jnp.concatenate([below, here, above], axis=cells)


def exchange(sent, dim, places):
    every = lax.all_to_all(sent, ("gy", "gz"), 0, 0)
    every = every.reshape((lax.axis_size("gy"), lax.axis_size("gz")) + sent.shape[1:])
    block = around(every, places[0:3], 2 + dim)
    block = around(block, places[3:6], 2 + dim)
    return block, shifted(block, "gx", 1), shifted(block, "gx", -1)


def exchange_cells(value, places):
    below = shifted(value[1:2], "gy", 1)
    above = shifted(value[0:1], "gy", -1)
    value = jnp.concatenate([below, value, above], axis=0)
    block = around(spread_all(value, "gz", lax.axis_size("gz")), places[3:6], 2)
    return block, shifted(block, "gx", 1), shifted(block, "gx", -1)


def shards(frac_positions, shielding, hardness, electroneg, counts, neighbor_list):
    count_x, count_y, count_z = [lax.axis_size(axis) for axis in ("gx", "gy", "gz")]
    places = frac_positions.transpose(0, 1, 3, 2, 4)
    count = count_y * count_z
    indices = lax.optimization_barrier(wrapped("gy") + wrapped("gz"))
    order = sum(indices[1:], indices[0]).astype(jnp.int32).reshape(1)
    packed = run_pack(order, places, shielding, hardness, electroneg, counts, neighbor_list)
    layers = exchange_cells(packed.reshape(2, 2, 8, 128), indices)
    own, lower, upper = [layer.reshape(16, 8, 128) for layer in layers]
    tiles_same, cols, total, w0, aux = run_same(own)
    tiles_side, w1 = run_side(own, lower, upper, cols, total, w0, aux)
    fields = [w0, w1]
    for step in (1, 2, 3):
        sent = jnp.broadcast_to(fields[-1].reshape(1, 2, 2, 2, 128), (count, 2, 2, 2, 128))
        layers = exchange(sent, 1, indices)
        own, lower, upper = [layer.reshape(32, 128) for layer in layers]
        total = run_apply_same(tiles_same, own)
        if step < 3:
            fields.append(run_apply_side(step, tiles_side, lower, upper, total, aux, fields))
    total, gram = run_apply_upper(tiles_side, upper, total, aux, fields)
    gram = jnp.sum(spread_all(gram, ("gy", "gz"), count), axis=0)
    gram = spread_all(gram, "gx", count_x).reshape(count_x, 128)
    return run_finish(gram, tiles_side, lower, total, aux, fields)


def solution(mesh):
    placed = (
        P("gx", "gy", "gz", None, None),
        P("gx", "gy", "gz", None),
        P("gx", "gy", "gz", None),
        P("gx", "gy", "gz", None),
        P("gx", "gy", "gz"),
        P("gx", "gy", "gz", None),
    )
    return jax.shard_map(
        shards,
        mesh=mesh,
        in_specs=placed,
        out_specs=(P("gx", "gy", "gz", None), P(None, "gx", "gy", "gz", None)),
        check_vma=False,
    )
```

```python
import functools

import jax
import jax.numpy as jnp
from jax import lax
from jax.experimental import pallas as pl
from jax.experimental.pallas import tpu as pltpu
from jax.sharding import PartitionSpec as P

CODES = {
    (0, 0, 1): 0,
    (0, 1, -1): 1,
    (0, 1, 0): 2,
    (0, 1, 1): 3,
    (1, -1, -1): 4,
    (1, -1, 0): 5,
    (1, -1, 1): 6,
    (1, 0, -1): 7,
    (1, 0, 0): 8,
    (1, 0, 1): 9,
    (1, 1, -1): 10,
    (1, 1, 0): 11,
    (1, 1, 1): 12,
}
SHELL = [(x, y, z) for x in (-1, 0, 1) for y in (-1, 0, 1) for z in (-1, 0, 1)]

SHIFT = (220.0, 110.0, 145.0, 140.0)
SCALE = (60.0, 70.0, 70.0, 70.0)
BACK = (0.0, 0.7, 1.0, 1.0)
PAIRS = [(i, j) for i in range(4) for j in range(i, 4)]
VMEM = pl.BlockSpec(memory_space=pltpu.VMEM)
SMEM = pl.BlockSpec(memory_space=pltpu.SMEM)
PARAMS = pltpu.CompilerParams(vmem_limit_bytes=24 * 1024 * 1024)


OWN = [(1 + y) * 4 + 1 + z for y in range(2) for z in range(2)]
SAME = [offset for offset in SHELL if offset[0] == 0]
SIDE = [offset for offset in SHELL if offset[0] != 0]
LOWER, UPPER = SIDE[:9], SIDE[9:]


def spread(row):
    return jnp.broadcast_to(row, (8, 128))


def reduce_rows(total_ref, image_ref):
    for field in range(8):
        block = total_ref[field * 16 : (field + 1) * 16].reshape(128, 128)
        image_ref[field : field + 1, :] = jnp.sum(block.T, axis=0, keepdims=True)


def next_basis(step, image, field, before, mask, hard):
    value = jnp.where(mask > 0.0, image, 0.0) + hard * field
    value = (value - SHIFT[step] * field) * (1.0 / SCALE[step])
    if BACK[step]:
        value = value - BACK[step] * before
    return value


def pack_kernel(order_ref, *refs):
    sources, packed_ref, inputs, semaphores = refs[:6], refs[6], refs[7:13], refs[13]
    copies = [
        pltpu.make_async_copy(source, target, semaphores.at[number])
        for number, (source, target) in enumerate(zip(sources, inputs))
    ]
    for copy in copies:
        copy.start()
    for copy in copies:
        copy.wait()
    place_ref, shield_ref, hard_ref, electro_ref, count_ref, list_ref = inputs
    lane = lax.broadcasted_iota(jnp.int32, (1, 128), 1)
    for y in range(2):
        for z in range(2):
            cell = 2 * y + z
            count = jnp.broadcast_to(count_ref[0, y : y + 1, z : z + 1], (1, 128))
            mask = jnp.where(lane < count, 1.0, 0.0)
            flags = jnp.zeros((1, 128), jnp.float32)
            for number in range(13):
                code = jnp.broadcast_to(list_ref[0, y, z : z + 1, number : number + 1], (1, 128))
                flags = jnp.where(lane == code, 1.0, flags)
            rows = []
            for number in range(3):
                rows.append(place_ref[0, y, number, z : z + 1])
            shield = shield_ref[0, y, z : z + 1]
            rows.append(jnp.exp(-1.5 * jnp.log(shield)) * (1000.0**-0.5))
            rows.append(-electro_ref[0, y, z : z + 1] * mask)
            rows.append(-mask)
            rows.append(flags)
            rows.append(hard_ref[0, y, z : z + 1])
            block = jnp.concatenate(rows, axis=0)
            packed_ref[cell] = block


def run_pack(order, *inputs):
    return pl.pallas_call(
        pack_kernel,
        out_shape=pltpu.VMEM((4, 8, 128), jnp.float32),
        in_specs=[SMEM] + [pl.BlockSpec(memory_space=pltpu.HBM)] * 6,
        out_specs=VMEM,
        scratch_shapes=[pltpu.VMEM(value.shape, value.dtype) for value in inputs]
        + [pltpu.SemaphoreType.DMA((6,))],
        compiler_params=pltpu.CompilerParams(vmem_limit_bytes=60 * 1024 * 1024),
        name="pack",
    )(order, *inputs)


def fill_rows(packed_ref, rows, first, layer):
    for y in range(4):
        for z in range(4):
            cell = y * 4 + z
            block = packed_ref[cell]
            for number, shift in enumerate((float(layer), y - 1.0, z - 1.0)):
                rows[first + cell, number] = spread(block[number : number + 1] + shift)
            for number in range(3, 6):
                rows[first + cell, number] = spread(block[number : number + 1])


def neighbor(offset):
    layer = 1 if offset[0] == 1 else 0
    return layer * 16 + (1 + offset[1]) * 4 + 1 + offset[2]


def fill_away(offsets, own_ref, lower_ref, rows, away):
    for own, cell in enumerate(OWN):
        y, z = own // 2, own % 2
        for number, offset in enumerate(offsets):
            place = neighbor(offset) + y * 4 + z
            row = rows[place, 0] + (1.0 + rows[place, 5]) * 100.0
            if offset in CODES:
                flag = own_ref[cell, 6:7, CODES[offset] : CODES[offset] + 1]
            elif offset == (0, 0, 0):
                flag = None
            else:
                code = CODES[tuple(-value for value in offset)]
                flag = lower_ref[cell + offset[1] * 4 + offset[2], 6:7, code : code + 1]
            if flag is not None:
                row = row + jnp.broadcast_to((1.0 - flag) * 100.0, (8, 128))
            away[own * len(offsets) + number] = row


def build_tiles(offsets, own_ref, rows, cols, away, tiles_ref, before, total):
    sub = lax.broadcasted_iota(jnp.int32, (8, 128), 0)
    lane = lax.broadcasted_iota(jnp.int32, (8, 128), 1)
    size = len(offsets)

    def body(own, base, chunk):
        xi, yi, zi, si = [cols[(own * 4 + number) * 16 + chunk] for number in range(4)]
        if before is None:
            sums = [jnp.zeros((8, 128), jnp.float32) for _ in range(2)]
        else:
            sums = [before[(system * 4 + own) * 16 + chunk] for system in range(2)]
        for number, offset in enumerate(offsets):
            cell = base + neighbor(offset)
            dx = away[own * size + number] - xi
            dy = rows[cell, 1] - yi
            dz = rows[cell, 2] - zi
            square = jnp.maximum(dx * dx + dy * dy + dz * dz, 1e-30)
            ratio = square * lax.rsqrt(square)
            fourth = square * square
            taper = 1.44 + fourth * (-50.4 + ratio * (120.96 + ratio * (-100.8 + 28.8 * ratio)))
            cube = square * ratio + rows[cell, 3] * si
            value = taper * jnp.exp2(jnp.log(cube) * (-1.0 / (3.0 * 0.6931471805599453)))
            keep = square < 1.0
            if offset == (0, 0, 0):
                keep = keep & (sub + chunk * 8 != lane)
            value = jnp.where(keep, value, 0.0)
            tiles_ref[(own * size + number) * 16 + chunk] = value
            sums[0] = sums[0] + value * rows[cell, 4]
            sums[1] = sums[1] - value
        for system in range(2):
            total[(system * 4 + own) * 16 + chunk] = sums[system]

    for own in range(4):
        base = (own // 2) * 4 + own % 2

        def step(index, carry, own=own, base=base):
            for part in range(2):
                body(own, base, index * 2 + part)
            return carry

        count = jnp.sum(-own_ref[OWN[own], 5:6]).astype(jnp.int32)
        lax.fori_loop(0, lax.shift_right_logical(count + 15, 4), step, 0)


def same_kernel(own_ref, tiles_ref, cols_ref, total_ref, field_ref, aux_ref, rows, away):
    fill_rows(own_ref, rows, 0, 0)
    for own, cell in enumerate(OWN):
        for number in range(4):
            column = jnp.broadcast_to(rows[cell, number, 0:1, :], (128, 128)).T
            start = (own * 4 + number) * 16
            cols_ref[start : start + 16] = column.reshape(16, 8, 128)
        for system in range(2):
            row = system * 4 + own
            mask = -own_ref[cell, 5:6]
            field_ref[row : row + 1] = own_ref[cell, 4 + system : 5 + system]
            aux_ref[row : row + 1] = mask
            aux_ref[8 + row : 9 + row] = own_ref[cell, 7:8] * mask
    fill_away(SAME, own_ref, own_ref, rows, away)
    build_tiles(SAME, own_ref, rows, cols_ref, away, tiles_ref, None, total_ref)


def side_kernel(own_ref, lower_ref, upper_ref, cols_ref, before_ref, field_ref, aux_ref, tiles_ref, next_ref, rows, away, total, image):
    fill_rows(lower_ref, rows, 0, -1)
    fill_rows(upper_ref, rows, 16, 1)
    fill_away(SIDE, own_ref, lower_ref, rows, away)
    build_tiles(SIDE, own_ref, rows, cols_ref, away, tiles_ref, before_ref, total)
    reduce_rows(total, image)
    next_ref[...] = next_basis(0, image[...], field_ref[...], None, aux_ref[0:8], aux_ref[8:16])


SHAPE = functools.partial(jax.ShapeDtypeStruct, dtype=jnp.float32)


def cost(flops):
    return pl.CostEstimate(flops=flops, bytes_accessed=4 * 1024 * 1024, transcendentals=0)


def run_same(own):
    return pl.pallas_call(
        same_kernel,
        out_shape=(
            SHAPE((36 * 16, 8, 128)),
            SHAPE((256, 8, 128)),
            SHAPE((128, 8, 128)),
            SHAPE((8, 128)),
            SHAPE((16, 128)),
        ),
        in_specs=[VMEM],
        out_specs=(VMEM,) * 5,
        scratch_shapes=[
            pltpu.VMEM((16, 6, 8, 128), jnp.float32),
            pltpu.VMEM((36, 8, 128), jnp.float32),
        ],
        compiler_params=PARAMS,
        cost_estimate=cost(40 * 36 * 16384),
        name="tiles_same",
    )(own)


def run_side(*inputs):
    return pl.pallas_call(
        side_kernel,
        out_shape=(SHAPE((72 * 16, 8, 128)), SHAPE((8, 128))),
        in_specs=[VMEM] * 7,
        out_specs=(VMEM,) * 2,
        scratch_shapes=[
            pltpu.VMEM((32, 6, 8, 128), jnp.float32),
            pltpu.VMEM((72, 8, 128), jnp.float32),
            pltpu.VMEM((128, 8, 128), jnp.float32),
            pltpu.VMEM((8, 128), jnp.float32),
        ],
        compiler_params=PARAMS,
        cost_estimate=cost(40 * 72 * 16384),
        name="tiles_side",
    )(*inputs)


def gram_row(fields, image):
    entries = [fields[i] * fields[j] for i, j in PAIRS] + [fields[3] * image] + fields
    lane = lax.broadcasted_iota(jnp.int32, (1, 128), 1)
    row = jnp.zeros((1, 128), jnp.float32)
    for number, entry in enumerate(entries):
        for system in range(2):
            part = jnp.sum(entry[system * 4 : system * 4 + 4], axis=0, keepdims=True)
            part = jnp.sum(part, axis=1, keepdims=True)
            row = row + jnp.where(lane == 2 * number + system, part, 0.0)
    return row


def fill_fields(halo_ref, rows, first):
    for system in range(2):
        for cell in range(16):
            row = system * 16 + cell
            rows[(first + cell) * 2 + system] = spread(halo_ref[row : row + 1])


def apply_tiles(offsets, size, first, tiles_ref, rows, before, total):

    for own in range(4):
        base = (own // 2) * 4 + own % 2
        for group in range(4):
            places = [[(system * 4 + own) * 16 + group * 4 + part for part in range(4)] for system in range(2)]
            if before is None:
                sums = [[None] * 4 for _ in range(2)]
            else:
                sums = [[before[place] for place in line] for line in places]
            for number, offset in enumerate(offsets):
                cell = base + neighbor(offset)
                right = [rows[cell * 2 + system] for system in range(2)]
                for part in range(4):
                    tile = tiles_ref[(own * size + first + number) * 16 + group * 4 + part]
                    for system in range(2):
                        term = tile * right[system]
                        held = sums[system][part]
                        sums[system][part] = term if held is None else held + term
            for system in range(2):
                for part in range(4):
                    total[places[system][part]] = sums[system][part]


def apply_same_kernel(tiles_ref, halo_ref, total_ref, rows):
    fill_fields(halo_ref, rows, 0)
    apply_tiles(SAME, 9, 0, tiles_ref, rows, None, total_ref)


def apply_side_kernel(step, tiles_ref, lower_ref, upper_ref, before_ref, aux_ref, *refs):
    fields, (next_ref, rows, total, image) = refs[: step + 1], refs[step + 1 :]
    fill_fields(lower_ref, rows, 0)
    fill_fields(upper_ref, rows, 16)
    apply_tiles(SIDE, 18, 0, tiles_ref, rows, before_ref, total)
    reduce_rows(total, image)
    before, field = fields[step - 1][...], fields[step][...]
    next_ref[...] = next_basis(step, image[...], field, before, aux_ref[0:8], aux_ref[8:16])


def apply_upper_kernel(tiles_ref, upper_ref, before_ref, aux_ref, *refs):
    fields, (total_ref, gram_ref, rows, total, image) = [ref[...] for ref in refs[:4]], refs[4:]
    fill_fields(upper_ref, rows, 16)
    apply_tiles(UPPER, 18, 9, tiles_ref, rows, None, total)
    part = total[...]
    both = before_ref[...] + part
    total_ref[...] = both
    total[...] = both + part
    reduce_rows(total, image)
    value = jnp.where(aux_ref[0:8] > 0.0, image[...], 0.0) + aux_ref[8:16] * fields[3]
    gram_ref[...] = gram_row(fields, value)


def run_apply_same(tiles, halo):
    return pl.pallas_call(
        apply_same_kernel,
        out_shape=SHAPE((128, 8, 128)),
        in_specs=[VMEM] * 2,
        out_specs=VMEM,
        scratch_shapes=[pltpu.VMEM((32, 8, 128), jnp.float32)],
        compiler_params=PARAMS,
        cost_estimate=cost(4 * 36 * 16384),
        name="apply_same",
    )(tiles, halo)


def apply_lower_kernel(tiles_ref, lower_ref, before_ref, aux_ref, w2_ref, w3_ref, next_ref, rows, total, image):
    fill_fields(lower_ref, rows, 0)
    apply_tiles(LOWER, 18, 0, tiles_ref, rows, before_ref, total)
    reduce_rows(total, image)
    next_ref[...] = next_basis(3, image[...], w3_ref[...], w2_ref[...], aux_ref[0:8], aux_ref[8:16])


SCRATCH = [
    pltpu.VMEM((64, 8, 128), jnp.float32),
    pltpu.VMEM((128, 8, 128), jnp.float32),
    pltpu.VMEM((8, 128), jnp.float32),
]


def run_apply_side(step, tiles, lower, upper, before, aux, fields):
    return pl.pallas_call(
        functools.partial(apply_side_kernel, step),
        out_shape=SHAPE((8, 128)),
        in_specs=[VMEM] * (5 + len(fields)),
        out_specs=VMEM,
        scratch_shapes=SCRATCH,
        compiler_params=PARAMS,
        cost_estimate=cost(4 * 72 * 16384),
        name=f"apply_side{step}",
    )(tiles, lower, upper, before, aux, *fields)


def run_apply_upper(tiles, upper, before, aux, fields):
    return pl.pallas_call(
        apply_upper_kernel,
        out_shape=(SHAPE((128, 8, 128)), SHAPE((1, 128))),
        in_specs=[VMEM] * (4 + len(fields)),
        out_specs=(VMEM, VMEM),
        scratch_shapes=SCRATCH,
        compiler_params=PARAMS,
        cost_estimate=cost(4 * 36 * 16384),
        name="apply_upper",
    )(tiles, upper, before, aux, *fields)


def run_apply_lower(*inputs):
    return pl.pallas_call(
        apply_lower_kernel,
        out_shape=SHAPE((8, 128)),
        in_specs=[VMEM] * 6,
        out_specs=VMEM,
        scratch_shapes=SCRATCH,
        compiler_params=PARAMS,
        cost_estimate=cost(4 * 36 * 16384),
        name="apply_lower",
    )(*inputs)


def combine(coefs, fields):
    value = coefs[0] * fields[0]
    for coef, field in zip(coefs[1:], fields[1:]):
        value = value + coef * field
    return value


def finish_kernel(gram_ref, *refs):
    fields, (charges_ref, residual_ref) = [ref[...] for ref in refs[:5]], refs[5:]
    summed = spread(jnp.sum(gram_ref[...], axis=0, keepdims=True))
    lane = lax.broadcasted_iota(jnp.int32, (8, 128), 1)
    system = lax.broadcasted_iota(jnp.int32, (8, 128), 0) // 4

    def entry(number):
        picked = jnp.where(lane == 2 * number + system, summed, 0.0)
        return jnp.broadcast_to(jnp.sum(picked, axis=1, keepdims=True), (8, 128))

    gram = {}
    for number, (i, j) in enumerate(PAIRS):
        gram[i, j] = gram[j, i] = entry(number)
    totals = [entry(len(PAIRS) + 1 + number) for number in range(4)]
    for i in range(4):
        if i == 3:
            value = entry(len(PAIRS))
        else:
            value = SCALE[i] * gram[i + 1, 3] + SHIFT[i] * gram[i, 3]
            if BACK[i]:
                value = value + SCALE[i] * BACK[i] * gram[i - 1, 3]
        value = (value - SHIFT[3] * gram[i, 3]) * (1.0 / SCALE[3]) - BACK[3] * gram[i, 2]
        gram[i, 4] = gram[4, i] = value

    def dot(left, right):
        result = None
        for i, a in enumerate(left):
            part = None
            for j, b in enumerate(right):
                term = gram[i, j] * b
                part = term if part is None else part + term
            result = a * part if result is None else result + a * part
        return result

    def multiply(vector):
        size = len(vector)
        out = []
        for row in range(size + 1):
            value = None
            if row >= 1:
                value = SCALE[row - 1] * vector[row - 1]
            if row < size:
                term = SHIFT[row] * vector[row]
                value = term if value is None else value + term
            if row + 1 < size:
                value = value + SCALE[row + 1] * BACK[row + 1] * vector[row + 1]
            out.append(value)
        return out

    one = jnp.ones((8, 128), jnp.float32)
    residual = [one]
    direction = [one]
    answer = []
    norm_now = gram[0, 0]
    for step in range(4):
        image = multiply(direction)
        alpha = norm_now / dot(direction, image)
        answer = [
            alpha * d if k >= len(answer) else answer[k] + alpha * d for k, d in enumerate(direction)
        ]
        residual = [
            residual[k] - alpha * value if k < len(residual) else -alpha * value
            for k, value in enumerate(image)
        ]
        if step == 3:
            break
        norm_next = dot(residual, residual)
        ratio = norm_next / norm_now
        direction = [
            value + ratio * direction[k] if k < len(direction) else value
            for k, value in enumerate(residual)
        ]
        norm_now = norm_next
    value = combine(residual, fields)
    solution = combine(answer, fields[:4])
    total = combine(answer, totals)
    charges = solution[0:4] - total[0:4] / total[4:8] * solution[4:8]
    for y in range(2):
        charges_ref[0, y] = charges[2 * y : 2 * y + 2]
        for system in range(2):
            row = system * 4 + 2 * y
            residual_ref[system, 0, y] = value[row : row + 2]


def run_finish(gram, fields):
    return pl.pallas_call(
        finish_kernel,
        out_shape=(SHAPE((1, 2, 2, 128)), SHAPE((2, 1, 2, 2, 128))),
        in_specs=[VMEM] * 6,
        out_specs=(VMEM, VMEM),
        compiler_params=PARAMS,
        name="finish",
    )(gram, *fields)


def shifted(value, axis, steps):
    count = lax.axis_size(axis)
    pairs = [(source, (source + steps) % count) for source in range(count)]
    return lax.ppermute(value, axis, pairs)


def spread_all(value, axes, count):
    sent = jnp.broadcast_to(value[None], (count,) + value.shape)
    return lax.all_to_all(sent, axes, 0, 0)


def wrapped(axis):
    here, count = lax.axis_index(axis), lax.axis_size(axis)
    below = jnp.where(here == 0, count - 1, here - 1)
    above = jnp.where(here == count - 1, 0, here + 1)
    return [value.astype(jnp.uint32) for value in (below, here, above)]


def around(every, places, cells):
    def part(place):
        start = [place] + [jnp.uint32(0)] * (every.ndim - 1)
        return lax.dynamic_slice(every, start, (1,) + every.shape[1:])[0]

    below, here, above = [part(place) for place in places]
    cells = cells - 1
    below = lax.slice_in_dim(below, 1, 2, axis=cells)
    above = lax.slice_in_dim(above, 0, 1, axis=cells)
    return jnp.concatenate([below, here, above], axis=cells)


def exchange(sent, dim, places):
    every = lax.all_to_all(sent, ("gy", "gz"), 0, 0)
    every = every.reshape((lax.axis_size("gy"), lax.axis_size("gz")) + sent.shape[1:])
    block = around(every, places[0:3], 2 + dim)
    block = around(block, places[3:6], 2 + dim)
    return block, shifted(block, "gx", 1), shifted(block, "gx", -1)


def exchange_cells(value, places):
    below = shifted(value[1:2], "gy", 1)
    above = shifted(value[0:1], "gy", -1)
    value = jnp.concatenate([below, value, above], axis=0)
    block = around(spread_all(value, "gz", lax.axis_size("gz")), places[3:6], 2)
    return block, shifted(block, "gx", 1), shifted(block, "gx", -1)


def shards(frac_positions, shielding, hardness, electroneg, counts, neighbor_list):
    count_x, count_y, count_z = [lax.axis_size(axis) for axis in ("gx", "gy", "gz")]
    places = frac_positions.transpose(0, 1, 3, 2, 4)
    count = count_y * count_z
    indices = lax.optimization_barrier(wrapped("gy") + wrapped("gz"))
    order = sum(indices[1:], indices[0]).astype(jnp.int32).reshape(1)
    packed = run_pack(order, places, shielding, hardness, electroneg, counts, neighbor_list)
    layers = exchange_cells(packed.reshape(2, 2, 8, 128), indices)
    own, lower, upper = [layer.reshape(16, 8, 128) for layer in layers]
    tiles_same, cols, total, w0, aux = run_same(own)
    tiles_side, w1 = run_side(own, lower, upper, cols, total, w0, aux)
    fields = [w0, w1]
    for step in (1, 2, 3):
        sent = jnp.broadcast_to(fields[-1].reshape(1, 2, 2, 2, 128), (count, 2, 2, 2, 128))
        layers = exchange(sent, 1, indices)
        own, lower, upper = [layer.reshape(32, 128) for layer in layers]
        total = run_apply_same(tiles_same, own)
        if step < 3:
            fields.append(run_apply_side(step, tiles_side, lower, upper, total, aux, fields))
    total, gram = run_apply_upper(tiles_side, upper, total, aux, fields)
    gram = jnp.sum(spread_all(gram, ("gy", "gz"), count), axis=0)
    gram = spread_all(gram, "gx", count_x).reshape(count_x, 128)
    fields.append(run_apply_lower(tiles_side, lower, total, aux, fields[2], fields[3]))
    return run_finish(gram, fields)


def solution(mesh):
    placed = (
        P("gx", "gy", "gz", None, None),
        P("gx", "gy", "gz", None),
        P("gx", "gy", "gz", None),
        P("gx", "gy", "gz", None),
        P("gx", "gy", "gz"),
        P("gx", "gy", "gz", None),
    )
    return jax.shard_map(
        shards,
        mesh=mesh,
        in_specs=placed,
        out_specs=(P("gx", "gy", "gz", None), P(None, "gx", "gy", "gz", None)),
        check_vma=False,
    )
```

```python
import functools

import jax
import jax.numpy as jnp
from jax import lax
from jax.experimental import pallas as pl
from jax.experimental.pallas import tpu as pltpu
from jax.sharding import PartitionSpec as P

CODES = {
    (0, 0, 1): 0,
    (0, 1, -1): 1,
    (0, 1, 0): 2,
    (0, 1, 1): 3,
    (1, -1, -1): 4,
    (1, -1, 0): 5,
    (1, -1, 1): 6,
    (1, 0, -1): 7,
    (1, 0, 0): 8,
    (1, 0, 1): 9,
    (1, 1, -1): 10,
    (1, 1, 0): 11,
    (1, 1, 1): 12,
}
SHELL = [(x, y, z) for x in (-1, 0, 1) for y in (-1, 0, 1) for z in (-1, 0, 1)]

SHIFT = (220.0, 110.0, 145.0, 140.0)
SCALE = (60.0, 70.0, 70.0, 70.0)
BACK = (0.0, 0.7, 1.0, 1.0)
PAIRS = [(i, j) for i in range(4) for j in range(i, 4)]
VMEM = pl.BlockSpec(memory_space=pltpu.VMEM)
SMEM = pl.BlockSpec(memory_space=pltpu.SMEM)
PARAMS = pltpu.CompilerParams(vmem_limit_bytes=24 * 1024 * 1024)


OWN = [(1 + y) * 4 + 1 + z for y in range(2) for z in range(2)]
SAME = [offset for offset in SHELL if offset[0] == 0]
SIDE = [offset for offset in SHELL if offset[0] != 0]
LOWER, UPPER = SIDE[:9], SIDE[9:]


def spread(row):
    return jnp.broadcast_to(row, (8, 128))


def reduce_rows(total_ref, image_ref):
    for field in range(8):
        block = total_ref[field * 16 : (field + 1) * 16].reshape(128, 128)
        image_ref[field : field + 1, :] = jnp.sum(block.T, axis=0, keepdims=True)


def next_basis(step, image, field, before, mask, hard):
    value = jnp.where(mask > 0.0, image, 0.0) + hard * field
    value = (value - SHIFT[step] * field) * (1.0 / SCALE[step])
    if BACK[step]:
        value = value - BACK[step] * before
    return value


def pack_kernel(order_ref, *refs):
    sources, packed_ref, inputs, semaphores = refs[:6], refs[6], refs[7:13], refs[13]
    copies = [
        pltpu.make_async_copy(source, target, semaphores.at[number])
        for number, (source, target) in enumerate(zip(sources, inputs))
    ]
    for copy in copies:
        copy.start()
    for copy in copies:
        copy.wait()
    place_ref, shield_ref, hard_ref, electro_ref, count_ref, list_ref = inputs
    lane = lax.broadcasted_iota(jnp.int32, (1, 128), 1)
    for y in range(2):
        for z in range(2):
            cell = 2 * y + z
            count = jnp.broadcast_to(count_ref[0, y : y + 1, z : z + 1], (1, 128))
            mask = jnp.where(lane < count, 1.0, 0.0)
            flags = jnp.zeros((1, 128), jnp.float32)
            for number in range(13):
                code = jnp.broadcast_to(list_ref[0, y, z : z + 1, number : number + 1], (1, 128))
                flags = jnp.where(lane == code, 1.0, flags)
            rows = []
            for number in range(3):
                rows.append(place_ref[0, y, number, z : z + 1])
            shield = shield_ref[0, y, z : z + 1]
            rows.append(jnp.exp(-1.5 * jnp.log(shield)) * (1000.0**-0.5))
            rows.append(-electro_ref[0, y, z : z + 1] * mask)
            rows.append(-mask)
            rows.append(flags)
            rows.append(hard_ref[0, y, z : z + 1])
            block = jnp.concatenate(rows, axis=0)
            packed_ref[cell] = block


def run_pack(order, *inputs):
    return pl.pallas_call(
        pack_kernel,
        out_shape=pltpu.VMEM((4, 8, 128), jnp.float32),
        in_specs=[SMEM] + [pl.BlockSpec(memory_space=pltpu.HBM)] * 6,
        out_specs=VMEM,
        scratch_shapes=[pltpu.VMEM(value.shape, value.dtype) for value in inputs]
        + [pltpu.SemaphoreType.DMA((6,))],
        compiler_params=pltpu.CompilerParams(vmem_limit_bytes=60 * 1024 * 1024),
        name="pack",
    )(order, *inputs)


def fill_rows(packed_ref, rows, first, layer):
    for y in range(4):
        for z in range(4):
            cell = y * 4 + z
            block = packed_ref[cell]
            for number, shift in enumerate((float(layer), y - 1.0, z - 1.0)):
                rows[first + cell, number] = spread(block[number : number + 1] + shift)
            for number in range(3, 6):
                rows[first + cell, number] = spread(block[number : number + 1])


def neighbor(offset):
    layer = 1 if offset[0] == 1 else 0
    return layer * 16 + (1 + offset[1]) * 4 + 1 + offset[2]


def fill_away(offsets, own_ref, lower_ref, rows, away):
    for own, cell in enumerate(OWN):
        y, z = own // 2, own % 2
        for number, offset in enumerate(offsets):
            place = neighbor(offset) + y * 4 + z
            row = rows[place, 0] + (1.0 + rows[place, 5]) * 100.0
            if offset in CODES:
                flag = own_ref[cell, 6:7, CODES[offset] : CODES[offset] + 1]
            elif offset == (0, 0, 0):
                flag = None
            else:
                code = CODES[tuple(-value for value in offset)]
                flag = lower_ref[cell + offset[1] * 4 + offset[2], 6:7, code : code + 1]
            if flag is not None:
                row = row + jnp.broadcast_to((1.0 - flag) * 100.0, (8, 128))
            away[own * len(offsets) + number] = row


def build_tiles(offsets, own_ref, rows, cols, away, tiles_ref, before, total):
    sub = lax.broadcasted_iota(jnp.int32, (8, 128), 0)
    lane = lax.broadcasted_iota(jnp.int32, (8, 128), 1)
    size = len(offsets)

    def body(own, base, chunk):
        xi, yi, zi, si = [cols[(own * 4 + number) * 16 + chunk] for number in range(4)]
        if before is None:
            sums = [jnp.zeros((8, 128), jnp.float32) for _ in range(2)]
        else:
            sums = [before[(system * 4 + own) * 16 + chunk] for system in range(2)]
        for number, offset in enumerate(offsets):
            cell = base + neighbor(offset)
            dx = away[own * size + number] - xi
            dy = rows[cell, 1] - yi
            dz = rows[cell, 2] - zi
            square = jnp.maximum(dx * dx + dy * dy + dz * dz, 1e-30)
            ratio = square * lax.rsqrt(square)
            fourth = square * square
            taper = 1.44 + fourth * (-50.4 + ratio * (120.96 + ratio * (-100.8 + 28.8 * ratio)))
            cube = square * ratio + rows[cell, 3] * si
            value = taper * jnp.exp2(jnp.log(cube) * (-1.0 / (3.0 * 0.6931471805599453)))
            keep = square < 1.0
            if offset == (0, 0, 0):
                keep = keep & (sub + chunk * 8 != lane)
            value = jnp.where(keep, value, 0.0)
            tiles_ref[(own * size + number) * 16 + chunk] = value
            sums[0] = sums[0] + value * rows[cell, 4]
            sums[1] = sums[1] - value
        for system in range(2):
            total[(system * 4 + own) * 16 + chunk] = sums[system]

    for own in range(4):
        base = (own // 2) * 4 + own % 2

        def step(index, carry, own=own, base=base):
            for part in range(2):
                body(own, base, index * 2 + part)
            return carry

        count = jnp.sum(-own_ref[OWN[own], 5:6]).astype(jnp.int32)
        lax.fori_loop(0, lax.shift_right_logical(count + 15, 4), step, 0)


def same_kernel(own_ref, tiles_ref, cols_ref, total_ref, field_ref, aux_ref, rows, away):
    fill_rows(own_ref, rows, 0, 0)
    for own, cell in enumerate(OWN):
        for number in range(4):
            column = jnp.broadcast_to(rows[cell, number, 0:1, :], (128, 128)).T
            start = (own * 4 + number) * 16
            cols_ref[start : start + 16] = column.reshape(16, 8, 128)
        for system in range(2):
            row = system * 4 + own
            mask = -own_ref[cell, 5:6]
            field_ref[row : row + 1] = own_ref[cell, 4 + system : 5 + system]
            aux_ref[row : row + 1] = mask
            aux_ref[8 + row : 9 + row] = own_ref[cell, 7:8] * mask
    fill_away(SAME, own_ref, own_ref, rows, away)
    build_tiles(SAME, own_ref, rows, cols_ref, away, tiles_ref, None, total_ref)


def upper_kernel(own_ref, upper_ref, cols_ref, before_ref, tiles_ref, total_ref, rows, away):
    fill_rows(upper_ref, rows, 16, 1)
    fill_away(UPPER, own_ref, own_ref, rows, away)
    build_tiles(UPPER, own_ref, rows, cols_ref, away, tiles_ref, before_ref, total_ref)


def lower_kernel(own_ref, lower_ref, cols_ref, before_ref, field_ref, aux_ref, tiles_ref, next_ref, rows, away, total, image):
    fill_rows(lower_ref, rows, 0, -1)
    fill_away(LOWER, own_ref, lower_ref, rows, away)
    build_tiles(LOWER, own_ref, rows, cols_ref, away, tiles_ref, before_ref, total)
    reduce_rows(total, image)
    next_ref[...] = next_basis(0, image[...], field_ref[...], None, aux_ref[0:8], aux_ref[8:16])


SHAPE = functools.partial(jax.ShapeDtypeStruct, dtype=jnp.float32)


def cost(flops):
    return pl.CostEstimate(flops=flops, bytes_accessed=4 * 1024 * 1024, transcendentals=0)


def run_same(own):
    return pl.pallas_call(
        same_kernel,
        out_shape=(
            SHAPE((36 * 16, 8, 128)),
            SHAPE((256, 8, 128)),
            SHAPE((128, 8, 128)),
            SHAPE((8, 128)),
            SHAPE((16, 128)),
        ),
        in_specs=[VMEM],
        out_specs=(VMEM,) * 5,
        scratch_shapes=[
            pltpu.VMEM((16, 6, 8, 128), jnp.float32),
            pltpu.VMEM((36, 8, 128), jnp.float32),
        ],
        compiler_params=PARAMS,
        cost_estimate=cost(40 * 36 * 16384),
        name="tiles_same",
    )(own)


PLACES = [pltpu.VMEM((32, 6, 8, 128), jnp.float32), pltpu.VMEM((36, 8, 128), jnp.float32)]


def run_upper(*inputs):
    return pl.pallas_call(
        upper_kernel,
        out_shape=(SHAPE((36 * 16, 8, 128)), SHAPE((128, 8, 128))),
        in_specs=[VMEM] * 4,
        out_specs=(VMEM,) * 2,
        scratch_shapes=PLACES,
        compiler_params=PARAMS,
        cost_estimate=cost(40 * 36 * 16384),
        name="tiles_upper",
    )(*inputs)


def run_lower(*inputs):
    return pl.pallas_call(
        lower_kernel,
        out_shape=(SHAPE((36 * 16, 8, 128)), SHAPE((8, 128))),
        in_specs=[VMEM] * 6,
        out_specs=(VMEM,) * 2,
        scratch_shapes=PLACES + [pltpu.VMEM((128, 8, 128), jnp.float32), pltpu.VMEM((8, 128), jnp.float32)],
        compiler_params=PARAMS,
        cost_estimate=cost(40 * 36 * 16384),
        name="tiles_lower",
    )(*inputs)


def gram_row(fields, image):
    entries = [fields[i] * fields[j] for i, j in PAIRS] + [fields[3] * image] + fields
    lane = lax.broadcasted_iota(jnp.int32, (1, 128), 1)
    row = jnp.zeros((1, 128), jnp.float32)
    for number, entry in enumerate(entries):
        for system in range(2):
            part = jnp.sum(entry[system * 4 : system * 4 + 4], axis=0, keepdims=True)
            part = jnp.sum(part, axis=1, keepdims=True)
            row = row + jnp.where(lane == 2 * number + system, part, 0.0)
    return row


def fill_fields(halo_ref, rows, first):
    for system in range(2):
        for cell in range(16):
            row = system * 16 + cell
            rows[(first + cell) * 2 + system] = spread(halo_ref[row : row + 1])


def apply_tiles(offsets, size, first, tiles_ref, rows, before, total):

    for own in range(4):
        base = (own // 2) * 4 + own % 2
        for group in range(4):
            places = [[(system * 4 + own) * 16 + group * 4 + part for part in range(4)] for system in range(2)]
            if before is None:
                sums = [[None] * 4 for _ in range(2)]
            else:
                sums = [[before[place] for place in line] for line in places]
            for number, offset in enumerate(offsets):
                cell = base + neighbor(offset)
                right = [rows[cell * 2 + system] for system in range(2)]
                for part in range(4):
                    tile = tiles_ref[(own * size + first + number) * 16 + group * 4 + part]
                    for system in range(2):
                        term = tile * right[system]
                        held = sums[system][part]
                        sums[system][part] = term if held is None else held + term
            for system in range(2):
                for part in range(4):
                    total[places[system][part]] = sums[system][part]


def apply_same_kernel(tiles_ref, halo_ref, total_ref, rows):
    fill_fields(halo_ref, rows, 0)
    apply_tiles(SAME, 9, 0, tiles_ref, rows, None, total_ref)


def apply_half_kernel(tiles_ref, upper_ref, before_ref, total_ref, rows):
    fill_fields(upper_ref, rows, 16)
    apply_tiles(UPPER, 9, 0, tiles_ref, rows, before_ref, total_ref)


def apply_upper_kernel(tiles_ref, upper_ref, before_ref, aux_ref, *refs):
    fields, (total_ref, gram_ref, rows, total, image) = [ref[...] for ref in refs[:4]], refs[4:]
    fill_fields(upper_ref, rows, 16)
    apply_tiles(UPPER, 9, 0, tiles_ref, rows, None, total)
    part = total[...]
    both = before_ref[...] + part
    total_ref[...] = both
    total[...] = both + part
    reduce_rows(total, image)
    value = jnp.where(aux_ref[0:8] > 0.0, image[...], 0.0) + aux_ref[8:16] * fields[3]
    gram_ref[...] = gram_row(fields, value)


def run_apply_same(tiles, halo):
    return pl.pallas_call(
        apply_same_kernel,
        out_shape=SHAPE((128, 8, 128)),
        in_specs=[VMEM] * 2,
        out_specs=VMEM,
        scratch_shapes=[pltpu.VMEM((32, 8, 128), jnp.float32)],
        compiler_params=PARAMS,
        cost_estimate=cost(4 * 36 * 16384),
        name="apply_same",
    )(tiles, halo)


def apply_lower_kernel(step, tiles_ref, lower_ref, before_ref, aux_ref, past_ref, field_ref, next_ref, rows, total, image):
    fill_fields(lower_ref, rows, 0)
    apply_tiles(LOWER, 9, 0, tiles_ref, rows, before_ref, total)
    reduce_rows(total, image)
    next_ref[...] = next_basis(step, image[...], field_ref[...], past_ref[...], aux_ref[0:8], aux_ref[8:16])


SCRATCH = [
    pltpu.VMEM((64, 8, 128), jnp.float32),
    pltpu.VMEM((128, 8, 128), jnp.float32),
    pltpu.VMEM((8, 128), jnp.float32),
]


def run_apply_half(tiles, upper, before):
    return pl.pallas_call(
        apply_half_kernel,
        out_shape=SHAPE((128, 8, 128)),
        in_specs=[VMEM] * 3,
        out_specs=VMEM,
        scratch_shapes=SCRATCH[:1],
        compiler_params=PARAMS,
        cost_estimate=cost(4 * 36 * 16384),
        name="apply_half",
    )(tiles, upper, before)


def run_apply_upper(tiles, upper, before, aux, fields):
    return pl.pallas_call(
        apply_upper_kernel,
        out_shape=(SHAPE((128, 8, 128)), SHAPE((1, 128))),
        in_specs=[VMEM] * (4 + len(fields)),
        out_specs=(VMEM, VMEM),
        scratch_shapes=SCRATCH,
        compiler_params=PARAMS,
        cost_estimate=cost(4 * 36 * 16384),
        name="apply_upper",
    )(tiles, upper, before, aux, *fields)


def run_apply_lower(step, *inputs):
    return pl.pallas_call(
        functools.partial(apply_lower_kernel, step),
        out_shape=SHAPE((8, 128)),
        in_specs=[VMEM] * 6,
        out_specs=VMEM,
        scratch_shapes=SCRATCH,
        compiler_params=PARAMS,
        cost_estimate=cost(4 * 36 * 16384),
        name=f"apply_lower{step}",
    )(*inputs)


def combine(coefs, fields):
    value = coefs[0] * fields[0]
    for coef, field in zip(coefs[1:], fields[1:]):
        value = value + coef * field
    return value


def finish_kernel(gram_ref, *refs):
    fields, (charges_ref, residual_ref) = [ref[...] for ref in refs[:5]], refs[5:]
    summed = spread(jnp.sum(gram_ref[...], axis=0, keepdims=True))
    lane = lax.broadcasted_iota(jnp.int32, (8, 128), 1)
    system = lax.broadcasted_iota(jnp.int32, (8, 128), 0) // 4

    def entry(number):
        picked = jnp.where(lane == 2 * number + system, summed, 0.0)
        return jnp.broadcast_to(jnp.sum(picked, axis=1, keepdims=True), (8, 128))

    gram = {}
    for number, (i, j) in enumerate(PAIRS):
        gram[i, j] = gram[j, i] = entry(number)
    totals = [entry(len(PAIRS) + 1 + number) for number in range(4)]
    for i in range(4):
        if i == 3:
            value = entry(len(PAIRS))
        else:
            value = SCALE[i] * gram[i + 1, 3] + SHIFT[i] * gram[i, 3]
            if BACK[i]:
                value = value + SCALE[i] * BACK[i] * gram[i - 1, 3]
        value = (value - SHIFT[3] * gram[i, 3]) * (1.0 / SCALE[3]) - BACK[3] * gram[i, 2]
        gram[i, 4] = gram[4, i] = value

    def dot(left, right):
        result = None
        for i, a in enumerate(left):
            part = None
            for j, b in enumerate(right):
                term = gram[i, j] * b
                part = term if part is None else part + term
            result = a * part if result is None else result + a * part
        return result

    def multiply(vector):
        size = len(vector)
        out = []
        for row in range(size + 1):
            value = None
            if row >= 1:
                value = SCALE[row - 1] * vector[row - 1]
            if row < size:
                term = SHIFT[row] * vector[row]
                value = term if value is None else value + term
            if row + 1 < size:
                value = value + SCALE[row + 1] * BACK[row + 1] * vector[row + 1]
            out.append(value)
        return out

    one = jnp.ones((8, 128), jnp.float32)
    residual = [one]
    direction = [one]
    answer = []
    norm_now = gram[0, 0]
    for step in range(4):
        image = multiply(direction)
        alpha = norm_now / dot(direction, image)
        answer = [
            alpha * d if k >= len(answer) else answer[k] + alpha * d for k, d in enumerate(direction)
        ]
        residual = [
            residual[k] - alpha * value if k < len(residual) else -alpha * value
            for k, value in enumerate(image)
        ]
        if step == 3:
            break
        norm_next = dot(residual, residual)
        ratio = norm_next / norm_now
        direction = [
            value + ratio * direction[k] if k < len(direction) else value
            for k, value in enumerate(residual)
        ]
        norm_now = norm_next
    value = combine(residual, fields)
    solution = combine(answer, fields[:4])
    total = combine(answer, totals)
    charges = solution[0:4] - total[0:4] / total[4:8] * solution[4:8]
    for y in range(2):
        charges_ref[0, y] = charges[2 * y : 2 * y + 2]
        for system in range(2):
            row = system * 4 + 2 * y
            residual_ref[system, 0, y] = value[row : row + 2]


def run_finish(gram, fields):
    return pl.pallas_call(
        finish_kernel,
        out_shape=(SHAPE((1, 2, 2, 128)), SHAPE((2, 1, 2, 2, 128))),
        in_specs=[VMEM] * 6,
        out_specs=(VMEM, VMEM),
        compiler_params=PARAMS,
        name="finish",
    )(gram, *fields)


def shifted(value, axis, steps):
    count = lax.axis_size(axis)
    pairs = [(source, (source + steps) % count) for source in range(count)]
    return lax.ppermute(value, axis, pairs)


def spread_all(value, axes, count):
    sent = jnp.broadcast_to(value[None], (count,) + value.shape)
    return lax.all_to_all(sent, axes, 0, 0)


def wrapped(axis):
    here, count = lax.axis_index(axis), lax.axis_size(axis)
    below = jnp.where(here == 0, count - 1, here - 1)
    above = jnp.where(here == count - 1, 0, here + 1)
    return [value.astype(jnp.uint32) for value in (below, here, above)]


def around(every, places, cells):
    def part(place):
        start = [place] + [jnp.uint32(0)] * (every.ndim - 1)
        return lax.dynamic_slice(every, start, (1,) + every.shape[1:])[0]

    below, here, above = [part(place) for place in places]
    cells = cells - 1
    below = lax.slice_in_dim(below, 1, 2, axis=cells)
    above = lax.slice_in_dim(above, 0, 1, axis=cells)
    return jnp.concatenate([below, here, above], axis=cells)


def exchange(sent, dim, places):
    every = lax.all_to_all(sent, ("gy", "gz"), 0, 0)
    every = every.reshape((lax.axis_size("gy"), lax.axis_size("gz")) + sent.shape[1:])
    block = around(every, places[0:3], 2 + dim)
    block = around(block, places[3:6], 2 + dim)
    return block, shifted(block, "gx", 1), shifted(block, "gx", -1)


def exchange_cells(value, places):
    below = shifted(value[1:2], "gy", 1)
    above = shifted(value[0:1], "gy", -1)
    value = jnp.concatenate([below, value, above], axis=0)
    block = around(spread_all(value, "gz", lax.axis_size("gz")), places[3:6], 2)
    return block, shifted(block, "gx", 1), shifted(block, "gx", -1)


def shards(frac_positions, shielding, hardness, electroneg, counts, neighbor_list):
    count_x, count_y, count_z = [lax.axis_size(axis) for axis in ("gx", "gy", "gz")]
    places = frac_positions.transpose(0, 1, 3, 2, 4)
    count = count_y * count_z
    indices = lax.optimization_barrier(wrapped("gy") + wrapped("gz"))
    order = sum(indices[1:], indices[0]).astype(jnp.int32).reshape(1)
    packed = run_pack(order, places, shielding, hardness, electroneg, counts, neighbor_list)
    layers = exchange_cells(packed.reshape(2, 2, 8, 128), indices)
    own, lower, upper = [layer.reshape(16, 8, 128) for layer in layers]
    tiles_same, cols, total, w0, aux = run_same(own)
    tiles_upper, total = run_upper(own, upper, cols, total)
    tiles_lower, w1 = run_lower(own, lower, cols, total, w0, aux)
    fields = [w0, w1]
    for step in (1, 2, 3):
        sent = jnp.broadcast_to(fields[-1].reshape(1, 2, 2, 2, 128), (count, 2, 2, 2, 128))
        layers = exchange(sent, 1, indices)
        own, lower, upper = [layer.reshape(32, 128) for layer in layers]
        total = run_apply_same(tiles_same, own)
        if step < 3:
            total = run_apply_half(tiles_upper, upper, total)
            fields.append(run_apply_lower(step, tiles_lower, lower, total, aux, fields[-2], fields[-1]))
    total, gram = run_apply_upper(tiles_upper, upper, total, aux, fields)
    gram = jnp.sum(spread_all(gram, ("gy", "gz"), count), axis=0)
    gram = spread_all(gram, "gx", count_x).reshape(count_x, 128)
    fields.append(run_apply_lower(3, tiles_lower, lower, total, aux, fields[2], fields[3]))
    return run_finish(gram, fields)


def solution(mesh):
    placed = (
        P("gx", "gy", "gz", None, None),
        P("gx", "gy", "gz", None),
        P("gx", "gy", "gz", None),
        P("gx", "gy", "gz", None),
        P("gx", "gy", "gz"),
        P("gx", "gy", "gz", None),
    )
    return jax.shard_map(
        shards,
        mesh=mesh,
        in_specs=placed,
        out_specs=(P("gx", "gy", "gz", None), P(None, "gx", "gy", "gz", None)),
        check_vma=False,
    )
```
